32 devices in a mesh: dp: 8 (over y, x, core), tensor: 4 (over z).
Axes of the slice: x: 2, y: 2, z: 4, core: 2. Of those that a mesh axis runs over, the one named last changes fastest.
Arguments:
- tokens: bfloat16 [8192, 1024], P(('dp', 'tensor')), may hold values from -6 to 6
- document_lengths: int32 [512], replicated, may hold values from 1 to 512, 8192 in all
- query_proj_weight: bfloat16 [1024, 1024], P(None, 'tensor'), may hold values from -0.1875 to 0.1875
- query_proj_bias: bfloat16 [1024], P('tensor'), may hold values from -3 to 3
- key_proj_weight: bfloat16 [1024, 1024], P(None, 'tensor'), may hold values from -0.1875 to 0.1875
- value_proj_weight: bfloat16 [1024, 1024], P(None, 'tensor'), may hold values from -0.1875 to 0.1875
- value_proj_bias: bfloat16 [1024], P('tensor'), may hold values from -3 to 3
- query_adapter_down: bfloat16 [1024, 8], replicated, may hold values from -0.1875 to 0.1875
- value_adapter_down: bfloat16 [1024, 8], replicated, may hold values from -0.1875 to 0.1875
- query_adapter_up: bfloat16 [8, 1024], P(None, 'tensor'), may hold values from -1 to 1
- value_adapter_up: bfloat16 [8, 1024], P(None, 'tensor'), may hold values from -1 to 1
- attention_out_weight: bfloat16 [1024, 1024], P('tensor'), may hold values from -0.75 to 0.75
- attention_out_bias: bfloat16 [1024], replicated, may hold values from -3 to 3
- attention_norm_gain: bfloat16 [1024], replicated, may hold values from 0.25 to 1.75
- attention_norm_bias: bfloat16 [1024], replicated, may hold values from -3 to 3
- up_proj_weight: bfloat16 [1024, 4096], P(None, 'tensor'), may hold values from -0.1875 to 0.1875
- up_proj_bias: bfloat16 [4096], P('tensor'), may hold values from -3 to 3
- down_proj_weight: bfloat16 [4096, 1024], P('tensor'), may hold values from -0.125 to 0.125
- down_proj_bias: bfloat16 [1024], replicated, may hold values from -3 to 3
- feedforward_norm_gain: bfloat16 [1024], replicated, may hold values from 0.25 to 1.75
- feedforward_norm_bias: bfloat16 [1024], replicated, may hold values from -3 to 3
- cotangent: bfloat16 [8192, 1024], P(('dp', 'tensor')), may hold values from -6 to 6
Outputs:
- output: bfloat16 [8192, 1024], P(('dp', 'tensor'))
- grad_tokens: bfloat16 [8192, 1024], P(('dp', 'tensor'))
- grad_lora_b_query: float32 [8, 1024], P(None, 'tensor')
- grad_lora_b_value: float32 [8, 1024], P(None, 'tensor')
The draws below stay inside these ranges and needn't reach their ends.
Inputs may be any that keep to these rules, and one draw needn't show every extreme that they name: `document_lengths`: the documents lie one after another over the 8192 positions of the stream and fill it; at least one document has exactly 512 tokens, none has more.
All inputs are finite; a program needn't handle non-finite values.
Results may differ from the reference program's by a relative error of at most 0.017.
The reference program's roundings to bfloat16 on the way count: a program that leaves them out, or rounds other values in their place, can miss the bound.
Values may be sent and summed in bfloat16 or wider, within the bound.
A program may use at most 128 MiB of HBM per device.

```python
import math
import jax
import jax.numpy as jnp
import numpy as np
from jax import lax

MODEL_WIDTH = 1024
H = 16
HD = 64
FF = 4096
ADAPTER_RANK = 8
MAXLEN = 512
QBLK = 512
TOKENS = 8192
NDOCS = 512


def block_scale(key, extent, split, smallest, high):
    def one(position, parts):
        heights = jax.random.uniform(jax.random.fold_in(jax.random.fold_in(key, 6), position), (parts,), jnp.float32, smallest / len(split), high / len(split))
        return jnp.repeat(jnp.exp(heights), extent[position] // parts).reshape((-1,) + (1,) * (len(extent) - position - 1))

    loudness = one(*split[0])
    for cut in split[1:]:
        loudness = loudness * one(*cut)
    return loudness


def split_up(count, total, most, slope):
    loads = [(1 << 20) // math.isqrt(grade ** slope) + 1 for grade in range(2, count + 1)]
    spare, holding = total - most - (count - 1), [1] * (count - 1)
    while spare > 0:
        free = [i for i in range(count - 1) if holding[i] < most]
        whole, remaining = sum([loads[i] for i in free]), spare
        for i in free:
            extra = min(most - holding[i], max(1, remaining * loads[i] // whole), spare)
            holding[i] = holding[i] + extra
            spare = spare - extra
    return np.array([most] + holding)


def ragged_sizes(key, count, total, most, slope):
    if count == 2:
        one = jax.random.randint(key, (), max(1, total - most), min(most, total - 1) + 1)
        return jnp.stack([one, total - one])
    sizes = jnp.asarray(split_up(count, total, most, slope), jnp.int32)
    pairs = (count - 1) // 2
    donor, taker = sizes[1:1 + 2 * pairs:2], sizes[2:2 + 2 * pairs:2]
    slack = jnp.minimum(donor - 1, most - taker)
    shifted = jax.random.randint(jax.random.fold_in(key, 1), (pairs,), 0, 1 << 20) % (slack + 1)
    sizes = sizes.at[1:1 + 2 * pairs:2].set(donor - shifted).at[2:2 + 2 * pairs:2].set(taker + shifted)
    return sizes[jax.random.permutation(jax.random.fold_in(key, 2), count)]


def centred(rng, shape, deviation, bound, cuts=(), kind=jnp.bfloat16):
    drawn = deviation * jax.random.normal(rng, shape, jnp.float32)
    if cuts:
        drawn = drawn * block_scale(rng, shape, cuts, -0.22, 0.18)
    return jnp.clip(drawn, -bound, bound).astype(kind)


def setup_inputs(seed: int = 0) -> dict:
    arg_keys = jax.random.split(jax.random.key(seed), 23)
    tokens = centred(arg_keys[0], (TOKENS, MODEL_WIDTH), 1.0, 6.0, ((0, 32),))
    document_lengths = ragged_sizes(arg_keys[1], NDOCS, TOKENS, MAXLEN, 2).astype(jnp.int32)
    query_proj_weight = centred(arg_keys[2], (MODEL_WIDTH, MODEL_WIDTH), MODEL_WIDTH ** -0.5, 0.1875, ((1, 4),))
    query_proj_bias = centred(arg_keys[3], (MODEL_WIDTH,), 0.5, 3.0, ((0, 4),))
    key_proj_weight = centred(arg_keys[4], (MODEL_WIDTH, MODEL_WIDTH), MODEL_WIDTH ** -0.5, 0.1875, ((1, 4),))
    value_proj_weight = centred(arg_keys[5], (MODEL_WIDTH, MODEL_WIDTH), MODEL_WIDTH ** -0.5, 0.1875, ((1, 4),))
    value_proj_bias = centred(arg_keys[6], (MODEL_WIDTH,), 0.5, 3.0, ((0, 4),))
    query_adapter_down = centred(arg_keys[7], (MODEL_WIDTH, ADAPTER_RANK), MODEL_WIDTH ** -0.5, 0.1875)
    value_adapter_down = centred(arg_keys[8], (MODEL_WIDTH, ADAPTER_RANK), MODEL_WIDTH ** -0.5, 0.1875)
    query_adapter_up = centred(arg_keys[9], (ADAPTER_RANK, MODEL_WIDTH), (4 * ADAPTER_RANK) ** -0.5, 1.0, ((1, 4),))
    value_adapter_up = centred(arg_keys[10], (ADAPTER_RANK, MODEL_WIDTH), (4 * ADAPTER_RANK) ** -0.5, 1.0, ((1, 4),))
    attention_out_weight = centred(arg_keys[11], (MODEL_WIDTH, MODEL_WIDTH), (MODEL_WIDTH // 16) ** -0.5, 0.75, ((0, 4),))
    attention_out_bias = centred(arg_keys[12], (MODEL_WIDTH,), 0.5, 3.0)
    attention_norm_gain = jnp.clip(1.0 + 0.15 * jax.random.normal(arg_keys[13], (MODEL_WIDTH,), jnp.float32), 0.25, 1.75).astype(jnp.bfloat16)
    attention_norm_bias = centred(arg_keys[14], (MODEL_WIDTH,), 0.5, 3.0)
    up_proj_weight = centred(arg_keys[15], (MODEL_WIDTH, FF), MODEL_WIDTH ** -0.5, 0.1875, ((1, 4),))
    up_proj_bias = centred(arg_keys[16], (FF,), 0.5, 3.0, ((0, 4),))
    down_proj_weight = centred(arg_keys[17], (FF, MODEL_WIDTH), (FF // 2) ** -0.5, 0.125, ((0, 4),))
    down_proj_bias = centred(arg_keys[18], (MODEL_WIDTH,), 0.5, 3.0)
    feedforward_norm_gain = jnp.clip(1.0 + 0.15 * jax.random.normal(arg_keys[19], (MODEL_WIDTH,), jnp.float32), 0.25, 1.75).astype(jnp.bfloat16)
    feedforward_norm_bias = centred(arg_keys[20], (MODEL_WIDTH,), 0.5, 3.0)
    cotangent = centred(arg_keys[21], (TOKENS, MODEL_WIDTH), 1.0, 6.0, ((0, 32),))
    return {"tokens": tokens, "document_lengths": document_lengths, "query_proj_weight": query_proj_weight, "query_proj_bias": query_proj_bias, "key_proj_weight": key_proj_weight, "value_proj_weight": value_proj_weight, "value_proj_bias": value_proj_bias, "query_adapter_down": query_adapter_down, "value_adapter_down": value_adapter_down, "query_adapter_up": query_adapter_up, "value_adapter_up": value_adapter_up, "attention_out_weight": attention_out_weight, "attention_out_bias": attention_out_bias, "attention_norm_gain": attention_norm_gain, "attention_norm_bias": attention_norm_bias, "up_proj_weight": up_proj_weight, "up_proj_bias": up_proj_bias, "down_proj_weight": down_proj_weight, "down_proj_bias": down_proj_bias, "feedforward_norm_gain": feedforward_norm_gain, "feedforward_norm_bias": feedforward_norm_bias, "cotangent": cotangent}


@jax.custom_vjp
def rank_space(v):
    return lax.optimization_barrier(v.astype(jnp.bfloat16)).astype(jnp.float32)

@jax.custom_vjp
def rank_space_grad(v):
    return v

def low_keep(v):
    return (rank_space(v), None)

def low_pass(kept, grad):
    return (grad,)

def back_keep(v):
    return (v, None)

def back_low(kept, grad):
    return (rank_space(grad),)
rank_space.defvjp(low_keep, low_pass)
rank_space_grad.defvjp(back_keep, back_low)
adapter_scale = 2.0
norm_eps = 1e-05
masked_score = -1e+30
highest = lax.Precision.HIGHEST

def matrix_product(left, right):
    return jnp.dot(left, right, precision=highest, preferred_element_type=jnp.float32)

def layer_norm(input_rows, norm_gain, norm_shift):
    centre = input_rows - lax.optimization_barrier(jnp.mean(input_rows, axis=-1, keepdims=True))
    variance = lax.optimization_barrier(jnp.mean(centre * centre, axis=-1, keepdims=True))
    return centre * lax.rsqrt(variance + norm_eps) * norm_gain + norm_shift

def doc_index(document_lengths, positions):
    ends = jnp.cumsum(document_lengths, dtype=jnp.int32)
    passed = lax.optimization_barrier(jnp.sum((ends[None, :] <= positions[:, None]).astype(jnp.int32), axis=1, dtype=jnp.int32))
    inside = (positions >= 0) & (passed < document_lengths.shape[0])
    return jnp.where(inside, passed, -1).astype(jnp.int32)

@jax.checkpoint
def attend(begin_row, query_rows, keys_pad, values_pad, query_ids, key_ids):
    window = QBLK + 2 * MAXLEN
    q_blk = lax.dynamic_slice_in_dim(query_rows, begin_row, QBLK, 0)
    k_win = lax.dynamic_slice_in_dim(keys_pad, begin_row, window, 0)
    v_win = lax.dynamic_slice_in_dim(values_pad, begin_row, window, 0)
    ids_q = lax.dynamic_slice_in_dim(query_ids, begin_row, QBLK, 0)
    ids_k = lax.dynamic_slice_in_dim(key_ids, begin_row, window, 0)
    scores = jnp.einsum('qhd,khd->hqk', q_blk, k_win, precision=highest) * (1.0 / math.sqrt(HD))
    scores = rank_space_grad(scores)
    allowed = ids_q[:, None] == ids_k[None, :]
    scores = jnp.where(allowed[None], scores, masked_score)
    row_max = lax.optimization_barrier(jnp.max(scores, axis=-1, keepdims=True))
    exp_scores = jnp.exp(scores - row_max)
    weights = rank_space(exp_scores / lax.optimization_barrier(jnp.sum(exp_scores, axis=-1, keepdims=True)))
    return jnp.einsum('hqk,khd->qhd', weights, v_win, precision=highest)

def attention(query_rows, keys, value_rows, document_lengths):
    count_all = query_rows.shape[0]
    q_heads = query_rows.reshape(count_all, H, HD)
    k_pad = jnp.pad(keys, ((MAXLEN, MAXLEN), (0, 0))).reshape(count_all + 2 * MAXLEN, H, HD)
    v_pad = jnp.pad(value_rows, ((MAXLEN, MAXLEN), (0, 0))).reshape(count_all + 2 * MAXLEN, H, HD)
    positions = jnp.arange(count_all + 2 * MAXLEN, dtype=jnp.int32) - MAXLEN
    key_ids = doc_index(document_lengths, positions)
    query_ids = key_ids[MAXLEN:MAXLEN + count_all]

    def one_block(block_at):
        return attend(block_at * QBLK, q_heads, k_pad, v_pad, query_ids, key_ids)
    outputs = lax.map(one_block, jnp.arange(count_all // QBLK, dtype=jnp.int32))
    return outputs.reshape(count_all, H * HD)

def reference(tokens, document_lengths, query_proj_weight, query_proj_bias, key_proj_weight, value_proj_weight, value_proj_bias, query_adapter_down, value_adapter_down, query_adapter_up, value_adapter_up, attention_out_weight, attention_out_bias, attention_norm_gain, attention_norm_bias, up_proj_weight, up_proj_bias, down_proj_weight, down_proj_bias, feedforward_norm_gain, feedforward_norm_bias, cotangent):

    def convert_float(array):
        return array.astype(jnp.float32)
    query_matrix, query_up_map, wk, value_matrix, value_up_map = (convert_float(query_proj_weight), convert_float(query_proj_bias), convert_float(key_proj_weight), convert_float(value_proj_weight), convert_float(value_proj_bias))
    query_down_map, value_down_map = (convert_float(query_adapter_down), convert_float(value_adapter_down))
    wo, bo = (convert_float(attention_out_weight), convert_float(attention_out_bias))
    g_one, c_one = (convert_float(attention_norm_gain), convert_float(attention_norm_bias))
    wu, bu, wd, bd = (convert_float(up_proj_weight), convert_float(up_proj_bias), convert_float(down_proj_weight), convert_float(down_proj_bias))
    g_two, c_two = (convert_float(feedforward_norm_gain), convert_float(feedforward_norm_bias))

    def forward_pass(input_rows, query_lifted, value_lifted):
        query_rank_rows = rank_space(rank_space_grad(matrix_product(input_rows, query_down_map)))
        value_rank_rows = rank_space(rank_space_grad(matrix_product(input_rows, value_down_map)))
        query_rows = rank_space(rank_space_grad(matrix_product(input_rows, query_matrix) + query_up_map + adapter_scale * matrix_product(query_rank_rows, query_lifted)))
        keys = rank_space(rank_space_grad(matrix_product(input_rows, wk)))
        value_rows = rank_space(rank_space_grad(matrix_product(input_rows, value_matrix) + value_up_map + adapter_scale * matrix_product(value_rank_rows, value_lifted)))
        attended = rank_space(rank_space_grad(attention(query_rows, keys, value_rows, document_lengths)))
        attn_branch = rank_space_grad(matrix_product(attended, wo) + bo)
        middle = layer_norm(input_rows + attn_branch, g_one, c_one)
        before = rank_space_grad(matrix_product(rank_space(middle), wu) + bu)
        hidden = rank_space(jax.nn.gelu(before, approximate=False))
        ffn_branch = rank_space_grad(matrix_product(hidden, wd) + bd)
        return layer_norm(middle + ffn_branch, g_two, c_two)
    final_output, backward_pass = jax.vjp(forward_pass, convert_float(tokens), convert_float(query_adapter_up), convert_float(value_adapter_up))
    grad_in, grad_bq, grad_bv = backward_pass(convert_float(cotangent))
    return (final_output.astype(jnp.bfloat16), grad_in.astype(jnp.bfloat16), grad_bq, grad_bv)
```

```python
import math

import jax
import jax.numpy as jnp
from jax import lax
from jax.experimental import pallas as pl
from jax.experimental.pallas import tpu as pltpu
from jax.sharding import PartitionSpec as P

MESH = pl.DeviceIdType.MESH
HD = 64
MAXLEN = 512
GROUP = 8
LANES = 128
NORM_EPS = 1e-05
MASKED = -1e30
LAG = 1
PLAN = (
    "+q0", "S0", "P20", "+q1", "Eq01", "Eq02", "S1", "Eq03", "T10", "S2", "Eq11", "+u0", "Eq12", "S3", "T11",
    "Eq13", "T12", "Eu01", "T13", "+u1", "P21", "Eu02", "P22", "T20", "Eu03", "P23", "T21", "Eu11", "Pn", "T22",
    "+o", "Eu12", "T23", "Eu13", "T30", "Eo1", "F", "P0", "T31", "+d0", "Eo2", "P4", "T32", "A0", "Eo3", "+d1",
    "A2", "T33", "A4", "Ed01", "A6", "Ed02", "Ed03", "L", "Pl", "Ed11", "B", "Ed12", "M", "U0", "U1", "Ed13", "U2",
    "U3", "D0", "D1", "D2", "D3",
)
F32 = jnp.float32
BF16 = jnp.bfloat16


def dot(left, right):
    return lax.dot_general(left, right, (((1,), (0,)), ((), ())), preferred_element_type=F32)


def dot_nt(left, right):
    return lax.dot_general(left, right, (((1,), (1,)), ((), ())), preferred_element_type=F32)


def tile(n):
    return pl.ds(pl.multiple_of(n * 256, 256), 256)


def layer_kernel(
    n_dp,
    x_in, cot_in, wq_in, wk_in, wv_in, wo_in, wup_in, wdn_in,
    len_in, qd_in, vd_in, qu_in, vu_in, qb_in, vb_in, ub_in, *rest
):
    vec_refs, rest = rest[:6], rest[6:]
    (
        out_ref, dx_ref, lora_ref,
        wqkv, wo, wup, wdn, small, lora_q, lora_v, vec_in, down_in,
        xwin, uwin, qwin, kwin, vwin, dowin, stwin, mask,
        att, attf, stat, midb, norm1, stat1, hid, gelp, acc, gffn, gbuf, dq, dk_acc, dv_acc, dkv,
        lsend, lrecv1, lrecv2,
        lsem, ssem, rsem,
    ) = rest
    rows = x_in.shape[0]
    width = x_in.shape[1]
    pairs = width // LANES
    dp, t = lax.axis_index("dp"), lax.axis_index("tensor")
    member = lax.rem(dp, GROUP)
    core = lax.rem(member, 2)
    yx = member // 2
    yx_x = yx + 1 - 2 * lax.rem(yx, 2)
    yx_y = yx + 2 - 4 * (yx // 2)
    yx_d = 3 - yx
    x_dev = (dp + 2 * (yx_x - yx), t)
    y_dev = (dp + 2 * (yx_y - yx), t)
    c_dev = (dp + 1 - 2 * core, t)

    def shard(a):
        first = jnp.where(t == 0, 1, t - 1)
        second = jnp.where(t == 0, 2, jnp.where(t == 3, 1, t + 1))
        third = jnp.where(t < 2, 3, 0)
        return jnp.where(a == 1, first, jnp.where(a == 2, second, third))

    barrier = pltpu.get_barrier_semaphore()
    for d in range(1, 4):
        pl.semaphore_signal(barrier, inc=1, device_id=(dp, lax.rem(t + d, 4)), device_id_type=MESH)
    for d in range(1, n_dp):
        pl.semaphore_signal(barrier, inc=1, device_id=(lax.rem(dp + d, n_dp), t), device_id_type=MESH)

    count = {"send": 0, "recv": 0, "local": 0}
    pending = []

    def alloc(kind, n):
        first = count[kind]
        count[kind] += n
        return first

    def when(pred, fn):
        if pred is None:
            fn()
        else:
            pl.when(pred)(fn)

    def remote(src, dst, recv, dev, pred=None):
        send = alloc("send", 1)
        copy = pltpu.make_async_remote_copy(
            src_ref=src, dst_ref=dst, send_sem=ssem.at[send], recv_sem=rsem.at[recv],
            device_id=dev, device_id_type=MESH,
        )
        when(pred, copy.start)
        pending.append((pred, copy))

    def arrived(dst, recv, pred=None):
        copy = pltpu.make_async_remote_copy(
            src_ref=dst, dst_ref=dst, send_sem=ssem.at[0], recv_sem=rsem.at[recv],
            device_id=(dp, t), device_id_type=MESH,
        )
        when(pred, copy.wait_recv)

    def local(src, dst):
        copy = pltpu.make_async_copy(src, dst, lsem.at[alloc("local", 1)])
        copy.start()
        return copy

    ld_qkv = [
        local(w, wqkv.at[t, :, :, :, pl.ds(256 * i, 256)]) for i, w in enumerate((wq_in, wk_in, wv_in))
    ]
    ld_x = [local(x_in, xwin.at[2])]
    ld_up = [local(wup_in, wup.at[t])]
    ld_o = [local(wo_in, wo.at[t])]
    ld_dn = [local(wdn_in, wdn.at[t])]
    ld_cot = [local(cot_in, gffn)]

    def done(copies):
        while copies:
            copies.pop().wait()

    class Chunk:
        def __init__(self, ref, first, size, loads):
            self.ref, self.first, self.size, self.loads = ref, first, size, loads
            self.zr = alloc("recv", 4)
            self.xr, self.yr, self.d1, self.d2, self.cr = (alloc("recv", 4) for _ in range(5))

        def region(self, s, place, lo=0, size=None):
            return self.ref.at[s, place, core, pl.ds(self.first + lo, size or self.size), :]

        def send(self):
            done(self.loads)
            own = self.region(t, yx)
            remote(own, own, self.zr + t, (dp, jnp.minimum(t + 1, 3)), t < 3)
            remote(own, own, self.zr + t, (dp, jnp.maximum(t - 1, 0)), t > 0)

        def stage0(self, a):
            s = shard(a)
            own = self.region(s, yx)
            arrived(own, self.zr + s)
            onward = jnp.where(s < t, t + 1, t - 1)
            remote(
                own, own, self.zr + s, (dp, jnp.clip(onward, 0, 3)),
                jnp.logical_and(onward >= 0, onward <= 3),
            )
            remote(own, own, self.xr + a, x_dev)
            remote(own, own, self.yr + a, y_dev)

        def stage1(self, a):
            s, half = shard(a), self.size // 2
            arrived(self.region(s, yx_x), self.xr + a)
            part = self.region(s, yx_x, 0, half)
            remote(part, part, self.d1 + a, y_dev)
            arrived(self.region(s, yx_y), self.yr + a)
            part = self.region(s, yx_y, half, half)
            remote(part, part, self.d2 + a, x_dev)

        def stage2(self, a):
            s, half = shard(a), self.size // 2
            arrived(self.region(s, yx_d, 0, half), self.d1 + a)
            arrived(self.region(s, yx_d, half, half), self.d2 + a)
            four = self.ref.at[s, :, core, pl.ds(self.first, self.size), :]
            remote(four, four, self.cr + a, c_dev)

        def stage3(self, a):
            s = shard(a)
            arrived(self.ref.at[s, :, 1 - core, pl.ds(self.first, self.size), :], self.cr + a)

    class Exchange:
        def __init__(self, ref, first, size):
            self.ref, self.first, self.size = ref, first, size
            self.base = alloc("recv", 6)

        def at(self, slot):
            return self.ref.at[slot, pl.ds(self.first, self.size), :]

        def go(self, src, dst, dev, pred):
            remote(self.at(src), self.at(dst), self.base + dst, dev, pred)

        def get(self, slot, pred):
            arrived(self.at(slot), self.base + slot, pred)

        def send(self, j):
            up, down = (dp, jnp.minimum(t + 1, 3)), (dp, jnp.maximum(t - 1, 0))
            if j == 1:
                self.go(2, 1, up, t < 3)
                self.go(2, 3, down, t > 0)
            if j == 2:
                self.go(1, 0, up, jnp.logical_and(t >= 1, t < 3))
                self.go(3, 4, down, jnp.logical_and(t > 0, t <= 2))
            if j == 3:
                self.go(0, 5, up, t == 2)
                self.go(4, 5, down, t == 1)

        def wait(self, j):
            if j == 1:
                self.get(1, t >= 1)
                self.get(3, t <= 2)
            if j == 2:
                self.get(0, t >= 2)
                self.get(4, t <= 1)
            if j == 3:
                self.get(5, jnp.logical_or(t == 0, t == 3))

        def send_far(self):
            after, before = (jnp.minimum(dp + 1, n_dp - 1), t), (jnp.maximum(dp - 1, 0), t)
            self.go(4, 0, after, jnp.logical_and(t <= 1, dp < n_dp - 1))
            self.go(0, 4, before, jnp.logical_and(t >= 2, dp > 0))

        def wait_far(self):
            self.get(0, jnp.logical_and(t <= 1, dp > 0))
            self.get(4, jnp.logical_and(t >= 2, dp < n_dp - 1))

        def send_near(self):
            after, before = (jnp.minimum(dp + 1, n_dp - 1), t), (jnp.maximum(dp - 1, 0), t)
            self.go(5, 1, after, jnp.logical_and(t == 0, dp < n_dp - 1))
            self.go(5, 3, before, jnp.logical_and(t == 3, dp > 0))

        def wait_near(self):
            self.get(1, jnp.logical_and(t == 0, dp > 0))
            self.get(3, jnp.logical_and(t == 3, dp < n_dp - 1))

    lane = lax.broadcasted_iota(jnp.int32, (1, LANES), 1)
    first_half = lane < HD

    def vec(i):
        return vec_in[i : i + 1, :]

    def halves(block):
        zero = jnp.zeros_like(block)
        return jnp.where(first_half, block, zero), jnp.where(first_half, zero, block)

    def clear(ref):
        @pl.when(jnp.logical_and(dp == 0, t <= 1))
        def _():
            ref[0] = jnp.zeros(ref.shape[1:], ref.dtype)

        @pl.when(jnp.logical_and(dp == 0, t == 0))
        def _():
            ref[1] = jnp.zeros(ref.shape[1:], ref.dtype)

        @pl.when(jnp.logical_and(dp == n_dp - 1, t >= 2))
        def _():
            ref[4] = jnp.zeros(ref.shape[1:], ref.dtype)

        @pl.when(jnp.logical_and(dp == n_dp - 1, t == 3))
        def _():
            ref[3] = jnp.zeros(ref.shape[1:], ref.dtype)

    def adapter(w):
        uwin[w] = dot_nt(xwin[w], down_in[...]).astype(BF16)

    def proj(w, pos, s):
        y = dot(xwin[w], wqkv[s].reshape(width, 3 * 256))
        u = uwin[w]
        place = (tile(pos), tile(s))
        q = y[:, :256] + dot(u, lora_q[s]) + small[s, 16:17, :]
        qwin[place] = (q * (1.0 / math.sqrt(HD))).astype(BF16)
        kwin[place] = y[:, 256:512].astype(BF16)
        v = y[:, 512:] + dot(u, lora_v[s]) + small[s, 17:18, :]
        vwin[place] = v.astype(BF16)

    def proj_all(w, pos):
        adapter(w)

        @pl.loop(0, 4, unroll=4)
        def _(s):
            proj(w, pos, s)

    def loop_pairs(lo, hi, body):
        @pl.loop(lo, hi, unroll=2)
        def _(p):
            body(p, pl.ds(pl.multiple_of(p * LANES, LANES), LANES))

    def column(index):
        return jnp.sum(jnp.where(lane == index, stat[...], 0.0), axis=1, keepdims=True)

    early = 4 * 256

    def attend(p, cols):
        q_heads = halves(qwin[tile(2), cols])
        k, v = kwin[0:early, cols], vwin[0:early, cols]
        outs, found = [], stat[...]
        for i in range(2):
            s = dot_nt(q_heads[i], k) + mask[:, 0:early]
            top = jnp.max(s, axis=1, keepdims=True)
            e = jnp.exp(s - top)
            total = jnp.sum(e, axis=1, keepdims=True)
            outs.append(dot(e.astype(BF16), v))
            found = jnp.where(lane == 2 * p + i, top, jnp.where(lane == 16 + 2 * p + i, total, found))
        attf[:, cols] = jnp.where(first_half, outs[0], outs[1])
        stat[...] = found

    def attend_last(p, cols):
        q_heads = halves(qwin[tile(2), cols])
        k, v = kwin[early:, cols], vwin[early:, cols]
        before, outs, found = attf[:, cols], [], stat[...]
        for i in range(2):
            old = column(2 * p + i)
            s = dot_nt(q_heads[i], k) + mask[:, early:]
            top = jnp.maximum(jnp.max(s, axis=1, keepdims=True), old)
            e = jnp.exp(s - top)
            alpha = jnp.exp(old - top)
            total = column(16 + 2 * p + i) * alpha + jnp.sum(e, axis=1, keepdims=True)
            outs.append((before * alpha + dot(e.astype(BF16), v)) * (1.0 / total))
            found = jnp.where(lane == 2 * p + i, top + jnp.log(total), found)
        o = jnp.where(first_half, outs[0], outs[1])
        attf[:, cols] = o
        att[:, cols] = o.astype(BF16)
        stat[...] = found

    def after_attention():
        @pl.loop(0, 4, unroll=4)
        def _(n):
            acc[:, tile(n)] = dot(att[...], wo[:, :, :, :, tile(n)].reshape(width, 256))

        z = xwin[2].astype(F32) + acc[...] + vec(0)
        centre = z - jnp.mean(z, axis=1, keepdims=True)
        r = lax.rsqrt(jnp.mean(centre * centre, axis=1, keepdims=True) + NORM_EPS)
        n1 = centre * r
        norm1[...] = n1
        stat1[...] = jnp.broadcast_to(r, stat1.shape)
        m = n1 * vec(1) + vec(2)
        midb[...] = m.astype(BF16)
        acc[...] = m + vec(3)

    def up(s):
        @pl.loop(0, 4, unroll=4)
        def _(n):
            b = dot(midb[...], wup[s, :, :, :, tile(n)].reshape(width, 256)) + small[s, pl.ds(18 + n, 1), :]
            cdf = 0.5 + 0.5 * lax.erf(b * (1.0 / math.sqrt(2.0)))
            hid[s, :, tile(n)] = (b * cdf).astype(BF16)
            gelp[s, :, tile(n)] = cdf + b * jnp.exp(-0.5 * b * b) * (1.0 / math.sqrt(2.0 * math.pi))

    def down(s):
        @pl.loop(0, 4, unroll=4)
        def _(n):
            acc[:, tile(n)] += dot(hid[s], wdn[s, :, :, :, tile(n)].reshape(width, 256))

    def second_norm():
        z = acc[...]
        centre = z - jnp.mean(z, axis=1, keepdims=True)
        r = lax.rsqrt(jnp.mean(centre * centre, axis=1, keepdims=True) + NORM_EPS)
        n2 = centre * r
        dk_acc[...] = n2 * vec(4) + vec(5)
        g = gffn[...].astype(F32) * vec(4)
        g = r * (g - jnp.mean(g, axis=1, keepdims=True) - n2 * jnp.mean(g * n2, axis=1, keepdims=True))
        acc[...] = g
        gffn[...] = g.astype(BF16)

    def ffn_back(s):
        @pl.loop(0, 4, unroll=4)
        def _(n):
            toward = dot_nt(gffn[...], wdn[s, n].reshape(256, width))
            gbuf[:, tile(n)] = (toward * gelp[s, :, tile(n)]).astype(BF16)

        @pl.loop(0, 4, unroll=4)
        def _(n):
            acc[:, tile(n)] += dot_nt(gbuf[...], wup[s, n].reshape(256, width))

    def first_norm_back():
        g = acc[...] * vec(1)
        n1 = norm1[...]
        g = g - jnp.mean(g, axis=1, keepdims=True) - n1 * jnp.mean(g * n1, axis=1, keepdims=True)
        g = stat1[:, 0:1] * g
        acc[...] = g
        gffn[...] = g.astype(BF16)

        @pl.loop(0, 4, unroll=4)
        def _(s):
            dowin[2, :, tile(s)] = dot_nt(gffn[...], wo[s].reshape(256, width)).astype(BF16)

        product = dowin[2].astype(F32) * attf[...]
        high = product.astype(BF16)
        low = (product - high.astype(F32)).astype(BF16)
        at_row = lax.broadcasted_iota(jnp.int32, (width, LANES), 0) // HD + 16
        at_lane = lax.broadcasted_iota(jnp.int32, (width, LANES), 1)
        pick = (at_row == at_lane).astype(F32).astype(BF16)
        delta = dot(high, pick) + dot(low, pick)
        both = jnp.where(lane < 16, stat[...], delta)
        stat[...] = both
        stwin[2] = both.T[0:32]

    def pass_queries(p, cols):
        q_heads, do_heads = halves(qwin[tile(2), cols]), halves(dowin[2, :, cols])
        k, v = kwin[:, cols], vwin[:, cols]
        parts = []
        for i in range(2):
            prob = jnp.exp(dot_nt(q_heads[i], k) + mask[...] - column(2 * p + i))
            ds = prob * (dot_nt(do_heads[i], v) - column(16 + 2 * p + i))
            parts.append(dot(ds.astype(BF16), k))
        dq[:, cols] = (jnp.where(first_half, parts[0], parts[1]) * (1.0 / math.sqrt(HD))).astype(BF16)

    def pass_keys(w, pos, lo, hi, first=False):
        def body(p, cols):
            k_heads, v_heads = halves(kwin[tile(2), cols]), halves(vwin[tile(2), cols])
            q, do = qwin[pos * 256 + lo : pos * 256 + hi, cols], dowin[w, lo:hi, cols]
            dk, dv = [], []
            for i in range(2):
                lse = stwin[w, pl.ds(2 * p + i, 1), :][:, lo:hi]
                delta = stwin[w, pl.ds(16 + 2 * p + i, 1), :][:, lo:hi]
                prob = jnp.exp(dot_nt(k_heads[i], q) + mask[:, pos * 256 + lo : pos * 256 + hi] - lse)
                ds = prob * (dot_nt(v_heads[i], do) - delta)
                dv.append(dot(prob.astype(BF16), do))
                dk.append(dot(ds.astype(BF16), q))
            dk, dv = jnp.where(first_half, dk[0], dk[1]), jnp.where(first_half, dv[0], dv[1])
            if first:
                dk_acc[:, cols] = dk
                dv_acc[:, cols] = dv
            else:
                dk_acc[:, cols] += dk
                dv_acc[:, cols] += dv

        loop_pairs(0, pairs, body)

    def lora_partial():
        u = uwin[2].astype(F32).T[0:16].astype(BF16)
        is_query = lax.broadcasted_iota(jnp.int32, (16, 1), 0) < 8
        for s in range(4):
            cols = slice(256 * s, 256 * s + 256)
            both = jnp.where(is_query, dot(u, dq[:, cols]), dot(u, dkv[1, :, cols]))
            lsend[s] = both

    def input_gradient():
        gu = jnp.zeros((rows, LANES), F32)
        for s in range(4):
            cols = slice(256 * s, 256 * s + 256)
            gu = gu + dot_nt(dq[:, cols], lora_q[s]) + dot_nt(dkv[1, :, cols], lora_v[s])
        gu = gu.astype(BF16)

        @pl.loop(0, 4, unroll=4)
        def _(n):
            total = acc[:, tile(n)] + dot(gu, down_in[:, tile(n)])
            for s in range(4):
                cols = slice(256 * s, 256 * s + 256)
                three = jnp.concatenate([dq[:, cols], dkv[0, :, cols], dkv[1, :, cols]], axis=1)
                total = total + dot_nt(three, wqkv[s, n].reshape(256, 3 * 256))
            norm1[:, tile(n)] = total

    def chunk(ref, first, size, loads):
        return Chunk(ref, first, size, loads)

    qkv0, qkv1 = chunk(wqkv, 0, 64, ld_qkv), chunk(wqkv, 64, 64, ld_qkv)
    up0, up1 = chunk(wup, 0, 64, ld_up), chunk(wup, 64, 64, ld_up)
    dn0, dn1 = chunk(wdn, 0, 64, ld_dn), chunk(wdn, 64, 64, ld_dn)
    o0 = chunk(wo, 0, 32, ld_o)
    half, quarter = rows // 2, rows // 4
    tok = [Exchange(xwin, i * quarter, quarter) for i in range(4)]
    small_base = alloc("recv", 4)
    wide = [Exchange(dowin, i * quarter, quarter) for i in range(4)]
    narrow = Exchange(stwin, 0, 32)
    lora1 = alloc("recv", 4)
    lora2 = alloc("recv", n_dp)

    clear(xwin)
    for i in range(8):
        cols = slice(LANES * i, LANES * i + LANES)
        for j, ref in enumerate(vec_refs):
            vec_in[j : j + 1, cols] = ref[i : i + 1, :].astype(F32)
    own_small = [2.0 * qu_in[...].astype(F32), 2.0 * vu_in[...].astype(F32)]
    small[t, 0:8, :] = own_small[0]
    small[t, 8:16, :] = own_small[1]
    for i in range(2):
        cols = slice(LANES * i, LANES * i + LANES)
        small[t, 16:17, cols] = qb_in[i : i + 1, :].astype(F32)
        small[t, 17:18, cols] = vb_in[i : i + 1, :].astype(F32)
        for j in range(4):
            small[t, 18 + j : 19 + j, cols] = ub_in[2 * j + i : 2 * j + i + 1, :].astype(F32)
    small[t, 22:24, :] = jnp.zeros((2, 256), F32)
    maps = [qd_in[...].astype(F32), vd_in[...].astype(F32), jnp.zeros((LANES - 16, width), F32)]
    down_in[...] = jnp.concatenate(maps, axis=0).astype(BF16)
    pl.semaphore_wait(barrier, 3 + n_dp - 1)
    done(ld_x)
    for d in range(1, 4):
        remote(small.at[t], small.at[t], small_base + t, (dp, lax.rem(t + d, 4)))

    near_first = jnp.where(t < 3, 3, 1)
    near_last = jnp.where(t < 3, 1, 3)
    blocks = {"0": (0, 0), "n": (near_first, 1), "2": (2, 2), "4": (4, 3), "l": (near_last, 4)}
    named = {"q0": qkv0, "q1": qkv1, "u0": up0, "u1": up1, "d0": dn0, "d1": dn1, "o": o0}
    events, waiting = [], []

    def run(entry):
        waiting.remove(entry)
        getattr(entry[1], "stage%d" % entry[3])(entry[2])

    def event(c, a):
        c.stage0(a)
        events.append((c, a))
        now = len(events)
        waiting.extend((now + k * LAG, c, a, k) for k in (1, 2, 3))
        for entry in sorted((e for e in waiting if e[0] <= now), key=lambda e: (e[0], e[3])):
            run(entry)

    def need(names, arrivals):
        cs = [named[n] for n in names]
        for entry in sorted((e for e in waiting if e[1] in cs and e[2] in arrivals), key=lambda e: (e[0], e[3])):
            run(entry)

    def setup():
        lengths = len_in[...]
        docs = lengths.shape[0] * LANES
        high, low = lengths // 256, lax.rem(lengths, 256)
        upto = (
            lax.broadcasted_iota(jnp.int32, (LANES, LANES), 0)
            <= lax.broadcasted_iota(jnp.int32, (LANES, LANES), 1)
        ).astype(F32).astype(BF16)

        def summed(part):
            return dot(part.astype(F32).astype(BF16), upto)

        ends = 256.0 * summed(high) + summed(low)
        window = mask.shape[1]
        first = (dp * 4 + t) * rows - MAXLEN
        spot = lax.broadcasted_iota(jnp.int32, (1, window), 1)
        nth = spot // rows
        nth = jnp.where(nth == 1, near_first, jnp.where(nth == 3, 4, jnp.where(nth == 4, near_last, nth)))
        position = first + nth * rows + lax.rem(spot, rows)
        place = position.astype(F32)
        passed = jnp.zeros((1, window), F32)
        before = jnp.zeros((1, 1), F32)
        for r in range(lengths.shape[0]):
            end = ends[r : r + 1, :] + before
            before = end[:, LANES - 1 :]
            column = jnp.broadcast_to(end, (LANES, LANES)).T[:, 0:1]
            passed = passed + jnp.sum((column <= place).astype(F32), axis=0, keepdims=True)
        inside = jnp.logical_and(position >= 0, passed < docs)
        ids = jnp.where(inside, passed, -1.0)
        own = jnp.broadcast_to(ids[:, 2 * rows : 3 * rows], (LANES, rows)).T[:, 0:1]
        mask[...] = jnp.where(own == ids, 0.0, MASKED)
        stat[...] = jnp.zeros(stat.shape, F32)

    def small_ready():
        for d in range(1, 4):
            peer = lax.rem(t + d, 4)
            arrived(small.at[peer], small_base + peer)
        none = jnp.zeros((8, 256), F32)
        lora_q[:, 16:, :] = jnp.zeros((4, LANES - 16, 256), BF16)
        lora_v[:, 16:, :] = jnp.zeros((4, LANES - 16, 256), BF16)
        for s in range(4):
            lora_q[s, 0:16, :] = jnp.concatenate([small[s, 0:8, :], none], axis=0).astype(BF16)
            lora_v[s, 0:16, :] = jnp.concatenate([none, small[s, 8:16, :]], axis=0).astype(BF16)

    everyone = (1, 2, 3)

    def part(a):
        return t if a == 0 else shard(a)

    for item in PLAN:
        kind, rest = item[0], item[1:]
        if kind == "+":
            named[rest].send()
        elif kind == "e":
            for a in everyone:
                event(named[rest], a)
        elif kind == "E":
            event(named[rest[:-1]], int(rest[-1]))
        elif kind == "S":
            tok[int(rest)].send(1)
        elif kind == "T":
            j, e = int(rest[0]), tok[int(rest[1])]
            e.wait(j)
            if j < 3:
                e.send(j + 1)
            if j == 2:
                e.send_far()
            if j == 3:
                e.send_near()
        elif kind == "F":
            for e in tok:
                e.wait_far()
        elif kind == "L":
            for e in tok:
                e.wait_near()
        elif kind == "N":
            need((rest[:-1],), (int(rest[-1]),) if rest[-1] != "*" else everyone)
        elif kind == "P":
            if rest[0] == "2":
                a = int(rest[1])
                if a == 0:
                    setup()
                    small_ready()
                    adapter(2)
                    done(ld_qkv)
                else:
                    need(("q0", "q1"), (a,))
                proj(2, 2, part(a))
            else:
                need(("q0", "q1"), everyone)
                proj_all(*blocks[rest[0]])
        elif kind == "A":
            loop_pairs(int(rest), int(rest) + 2, attend)
        elif kind == "B":
            loop_pairs(0, pairs, attend_last)
        elif kind == "M":
            need(("o",), everyone)
            done(ld_o)
            after_attention()
        elif kind == "U":
            a = int(rest)
            if a:
                need(("u0", "u1"), (a,))
            done(ld_up)
            up(part(a))
        elif kind == "D":
            a = int(rest)
            if a:
                need(("d0", "d1"), (a,))
            done(ld_dn)
            down(part(a))
    while waiting:
        run(min(waiting, key=lambda e: (e[0], e[3])))
    for copies in (ld_qkv, ld_o, ld_up, ld_dn):
        done(copies)

    done(ld_cot)
    second_norm()
    out_copy = local(dk_acc, out_ref)
    clear(dowin)
    clear(stwin)

    @pl.loop(0, 4, unroll=4)
    def _(s):
        ffn_back(s)

    first_norm_back()
    narrow.send(1)
    for e in wide:
        e.send(1)

    def turn(j, i):
        for e in [wide[i]] + ([narrow] if i == 0 else []):
            e.wait(j)
            if j < 3:
                e.send(j + 1)
            if j == 2:
                e.send_far()
            if j == 3:
                e.send_near()

    both = [narrow] + wide
    for i in range(4):
        loop_pairs(2 * i, 2 * i + 2, pass_queries)
        turn(1, i)
    out_copy.wait()
    pass_keys(2, 2, 0, rows, first=True)
    turn(2, 0)
    turn(2, 1)
    pass_keys(*blocks["n"], 0, rows)
    turn(2, 2)
    turn(2, 3)
    for e in both:
        e.wait_far()
    pass_keys(*blocks["0"], 0, rows)
    turn(3, 0)
    turn(3, 1)
    pass_keys(*blocks["4"], 0, rows)
    turn(3, 2)
    turn(3, 3)
    for e in both[:3]:
        e.wait_near()
    pass_keys(*blocks["l"], 0, half)
    for e in both[3:]:
        e.wait_near()
    pass_keys(*blocks["l"], half, rows)
    dkv[0] = dk_acc[...].astype(BF16)
    dkv[1] = dv_acc[...].astype(BF16)
    lora_partial()
    for d in range(1, 4):
        peer = lax.rem(t + d, 4)
        remote(lsend.at[peer], lrecv1.at[t], lora1 + t, (dp, peer))
    lrecv1[t] = lsend[t]
    input_gradient()
    dx_copy = local(norm1, dx_ref)
    for d in range(1, 4):
        peer = lax.rem(t + d, 4)
        arrived(lrecv1.at[peer], lora1 + peer)
    lrecv2[dp] = (lrecv1[0] + lrecv1[1]) + (lrecv1[2] + lrecv1[3])
    for d in range(1, n_dp):
        remote(lrecv2.at[dp], lrecv2.at[dp], lora2 + dp, (lax.rem(dp + d, n_dp), t))
    for d in range(1, n_dp):
        peer = lax.rem(dp + d, n_dp)
        arrived(lrecv2.at[peer], lora2 + peer)
    total = lrecv2[0]
    for i in range(1, n_dp):
        total = total + lrecv2[i]
    lora_ref[...] = total
    dx_copy.wait()
    for pred, copy in pending:
        when(pred, copy.wait_send)
    assert count["send"] <= ssem.shape[0] and count["recv"] <= rsem.shape[0]
    assert count["local"] <= lsem.shape[0]


def shards(
    tokens, document_lengths, query_proj_weight, query_proj_bias, key_proj_weight, value_proj_weight,
    value_proj_bias, query_adapter_down, value_adapter_down, query_adapter_up, value_adapter_up,
    attention_out_weight, attention_out_bias, attention_norm_gain, attention_norm_bias, up_proj_weight,
    up_proj_bias, down_proj_weight, down_proj_bias, feedforward_norm_gain, feedforward_norm_bias, cotangent,
):
    rows, width = tokens.shape
    n_dp = lax.axis_size("dp")
    window = rows + 2 * MAXLEN

    def fold(vector):
        return vector.reshape(vector.shape[0] // LANES, LANES)

    def cut(weight):
        return weight.reshape(4, 2, weight.shape[0] // GROUP, weight.shape[1])

    def vmem(shape, dtype):
        return pltpu.VMEM(shape, dtype)

    any_spec = pl.BlockSpec(memory_space=pl.ANY)
    vmem_spec = pl.BlockSpec(memory_space=pltpu.VMEM)
    full = (rows, width)
    rank = query_adapter_up.shape[0]
    call = pl.pallas_call(
        lambda *refs: layer_kernel(n_dp, *refs),
        out_shape=(
            jax.ShapeDtypeStruct(full, F32),
            jax.ShapeDtypeStruct(full, F32),
            jax.ShapeDtypeStruct((16, 256), F32),
        ),
        in_specs=[any_spec] * 8 + [vmem_spec] * 14,
        out_specs=(any_spec, any_spec, vmem_spec),
        scratch_shapes=[
            vmem((4, 4, 2, 128, 768), BF16),
            vmem((4, 4, 2, 32, 1024), BF16),
            vmem((4, 4, 2, 128, 1024), BF16),
            vmem((4, 4, 2, 128, 1024), BF16),
            vmem((4, 24, 256), F32),
            vmem((4, 128, 256), BF16),
            vmem((4, 128, 256), BF16),
            vmem((8, width), F32),
            vmem((LANES, width), BF16),
            vmem((6, rows, width), BF16),
            vmem((5, rows, LANES), BF16),
            vmem((window, width), BF16),
            vmem((window, width), BF16),
            vmem((window, width), BF16),
            vmem((6, rows, width), BF16),
            vmem((6, 32, rows), F32),
            vmem((rows, window), F32),
            vmem(full, BF16),
            vmem(full, F32),
            vmem((rows, LANES), F32),
            vmem(full, BF16),
            vmem(full, F32),
            vmem((rows, LANES), F32),
            vmem((4, rows, width), BF16),
            vmem((4, rows, width), F32),
            vmem(full, F32),
            vmem(full, BF16),
            vmem(full, BF16),
            vmem(full, BF16),
            vmem(full, F32),
            vmem(full, F32),
            vmem((2, rows, width), BF16),
            vmem((4, 16, 256), F32),
            vmem((4, 16, 256), F32),
            vmem((n_dp, 16, 256), F32),
            pltpu.SemaphoreType.DMA((16,)),
            pltpu.SemaphoreType.DMA((300 + n_dp,)),
            pltpu.SemaphoreType.DMA((260 + n_dp,)),
        ],
        compiler_params=pltpu.CompilerParams(
            collective_id=0, has_side_effects=True, vmem_limit_bytes=63 * 2**20
        ),
        name="layer",
    )
    out, grad, lora = call(
        tokens, cotangent, cut(query_proj_weight), cut(key_proj_weight), cut(value_proj_weight),
        cut(attention_out_weight), cut(up_proj_weight), cut(down_proj_weight), fold(document_lengths),
        query_adapter_down.T, value_adapter_down.T, query_adapter_up, value_adapter_up,
        fold(query_proj_bias), fold(value_proj_bias), fold(up_proj_bias), fold(attention_out_bias),
        fold(attention_norm_gain), fold(attention_norm_bias), fold(down_proj_bias), fold(feedforward_norm_gain),
        fold(feedforward_norm_bias),
    )
    lora = 2.0 * lora
    return out.astype(BF16), grad.astype(BF16), lora[:rank], lora[rank:]


def solution(mesh):
    whole, columns = P(), P(None, "tensor")
    stream = P(("dp", "tensor"), None)
    return jax.shard_map(
        shards,
        mesh=mesh,
        in_specs=(
            stream, whole, columns, P("tensor"), columns, columns, P("tensor"), whole, whole, columns, columns,
            P("tensor", None), whole, whole, whole, columns, P("tensor"), P("tensor", None), whole, whole, whole,
            stream,
        ),
        out_specs=(stream, stream, columns, columns),
        check_vma=False,
    )
```

```python
import math

import jax
import jax.numpy as jnp
from jax import lax
from jax.experimental import pallas as pl
from jax.experimental.pallas import tpu as pltpu
from jax.sharding import PartitionSpec as P

MESH = pl.DeviceIdType.MESH
HD = 64
MAXLEN = 512
GROUP = 8
LANES = 128
NORM_EPS = 1e-05
MASKED = -1e30
STEPS = {
    "S": "first", "n": "neighbours", "c": "chain1", "C": "chain2", "x": "ends", "y": "chain3", "t": "third", "l": "last",
}
PLAN_BACK = (
    "S0", "c0", "S2", "S1", "Q0", "K24", "c1", "n0", "Q4", "S3", "K20", "c3", "c2", "C0", "n1", "x0", "Q2", "x1",
    "C1", "n2", "t0", "Q6", "n3", "x2", "Kn4", "C3", "t2", "t1", "x3", "y1", "Kn0", "t3", "Kt4", "y0", "Kt0", "l0",
    "C2", "l1", "y3", "V0", "l3", "y2", "Ks0", "Ks4", "l2", "V1", "G", "L", "H", "I", "J",
)
PLAN = (
    "+q1", "+q0", "S2", "0q11", "0q01", "1q11", "0q12", "0q02", "2q11", "0q13", "0q03", "1q12", "+u0", "+u1", "S3",
    "1q03", "1q02", "+o", "1q01", "0u01", "3q11", "P20", "2q02", "c3", "S0", "0u11", "S1", "2q12", "1q13", "2q03",
    "0u02", "c1", "0u12", "1u02", "c2", "2q01", "0o1", "3q12", "n3", "0o2", "1u12", "2q13", "+d1", "1u01", "3q13",
    "0u13", "c0", "0u03", "0o3", "C3", "3q03", "n1", "2u02", "C1", "3q02", "x1", "x3", "n0", "P22", "1u03", "3q01",
    "+d0", "x0", "2u12", "n2", "P23", "P21", "3u02", "0d11", "C0", "1o2", "Pn", "A002", "1o1", "x2", "1o3", "A202",
    "C2", "1u13", "2u01", "A602", "2o2", "t0", "A402", "0d01", "0d02", "2o1", "t2", "0d12", "y3", "2u03", "1d11",
    "3u01", "t3", "2o3", "3o2", "y0", "y1", "t1", "y2", "3o1", "Ps", "Pt", "1d01", "A224", "A024", "A424", "l2",
    "1d02", "3u03", "1u11", "A624", "l1", "2d11", "l0", "1d12", "l3", "3u12", "2u13", "0d13", "2d01", "Pl", "A045",
    "2u11", "A445", "3o3", "3d01", "0d03", "A645", "A245", "2d12", "M", "1d13", "3u13", "U3", "3d11", "2d02",
    "3u11", "1d03", "U1", "2d13", "U2", "D1", "3d12", "2d03", "U0", "D0", "3d02", "3d13", "D2", "3d03", "D3",
)
F32 = jnp.float32
BF16 = jnp.bfloat16


def dot(left, right):
    return lax.dot_general(left, right, (((1,), (0,)), ((), ())), preferred_element_type=F32)


def dot_nt(left, right):
    return lax.dot_general(left, right, (((1,), (1,)), ((), ())), preferred_element_type=F32)


def tile(n):
    return pl.ds(pl.multiple_of(n * 256, 256), 256)


def layer_kernel(
    n_dp,
    x_in, cot_in, wq_in, wk_in, wv_in, wo_in, wup_in, wdn_in,
    len_in, qd_in, vd_in, qu_in, vu_in, qb_in, vb_in, ub_in, *rest
):
    small_from = (len_in, qd_in, vd_in, qu_in, vu_in, qb_in, vb_in, ub_in, *rest[:6])
    rest = rest[6:]
    (
        out_ref, dx_ref, lora_ref,
        wqkv, wo, wup, wdn, small, lora_q, lora_v, vec_in, down_in,
        xwin, uwin, qwin, kwin, vwin, dowin, stwin, mask,
        att, attf, stat, midb, norm1, stat1, hid, gelp, acc, gffn, gbuf, dq, dk_acc, dv_acc, dkv,
        lsend, lrecv1, lrecv2,
        lsem, ssem, rsem,
        *small_to,
    ) = rest
    len_in, qd_in, vd_in, qu_in, vu_in, qb_in, vb_in, ub_in, *vec_refs = small_to
    rows = x_in.shape[0]
    width = x_in.shape[1]
    pairs = width // LANES
    dp, t = lax.axis_index("dp"), lax.axis_index("tensor")
    member = lax.rem(dp, GROUP)
    core = lax.rem(member, 2)
    yx = member // 2
    yx_x = yx + 1 - 2 * lax.rem(yx, 2)
    yx_y = yx + 2 - 4 * (yx // 2)
    yx_d = 3 - yx
    x_dev = (dp + 2 * (yx_x - yx), t)
    y_dev = (dp + 2 * (yx_y - yx), t)
    c_dev = (dp + 1 - 2 * core, t)

    def shard(a):
        first = jnp.where(t == 0, 1, t - 1)
        second = jnp.where(t == 0, 2, jnp.where(t == 3, 1, t + 1))
        third = jnp.where(t < 2, 3, 0)
        return jnp.where(a == 1, first, jnp.where(a == 2, second, third))

    barrier = pltpu.get_barrier_semaphore()
    for d in range(1, 4):
        pl.semaphore_signal(barrier, inc=1, device_id=(dp, lax.rem(t + d, 4)), device_id_type=MESH)
    for d in range(1, n_dp):
        pl.semaphore_signal(barrier, inc=1, device_id=(lax.rem(dp + d, n_dp), t), device_id_type=MESH)

    count = {"send": 0, "recv": 0, "local": 0}
    pending = {}

    def alloc(kind, n):
        first = count[kind]
        count[kind] += n
        return first

    def when(pred, fn):
        if pred is None:
            fn()
        else:
            pl.when(pred)(fn)

    def remote(src, dst, recv, dev, pred=None):
        slot = alloc("send", 1) % ssem.shape[0]
        if slot in pending:
            before, copy = pending[slot]
            when(before, copy.wait_send)
        copy = pltpu.make_async_remote_copy(
            src_ref=src, dst_ref=dst, send_sem=ssem.at[slot], recv_sem=rsem.at[recv],
            device_id=dev, device_id_type=MESH,
        )
        when(pred, copy.start)
        pending[slot] = (pred, copy)

    def arrived(dst, recv, pred=None):
        copy = pltpu.make_async_remote_copy(
            src_ref=dst, dst_ref=dst, send_sem=ssem.at[0], recv_sem=rsem.at[recv],
            device_id=(dp, t), device_id_type=MESH,
        )
        when(pred, copy.wait_recv)

    def local(src, dst):
        copy = pltpu.make_async_copy(src, dst, lsem.at[alloc("local", 1)])
        copy.start()
        return copy

    ld_small = [local(a, b) for a, b in zip(small_from, small_to)]
    ld_qkv = [
        local(w, wqkv.at[t, :, :, :, pl.ds(256 * i, 256)]) for i, w in enumerate((wq_in, wk_in, wv_in))
    ]
    ld_x = [local(x_in, xwin.at[2])]
    ld_up = [local(wup_in, wup.at[t])]
    ld_o = [local(wo_in, wo.at[t])]
    ld_dn = [local(wdn_in, wdn.at[t])]
    ld_cot = [local(cot_in, gffn)]

    def done(copies):
        while copies:
            copies.pop().wait()

    class Chunk:
        def __init__(self, ref, first, size, loads):
            self.ref, self.first, self.size, self.loads = ref, first, size, loads
            self.zr = alloc("recv", 4)
            self.xr, self.yr, self.dr, self.cr = (alloc("recv", 3) - 1 for _ in range(4))

        def region(self, s, place, lo=0, size=None):
            return self.ref.at[s, place, core, pl.ds(self.first + lo, size or self.size), :]

        def send(self):
            done(self.loads)
            own = self.region(t, yx)
            remote(own, own, self.zr + t, (dp, jnp.minimum(t + 1, 3)), t < 3)
            remote(own, own, self.zr + t, (dp, jnp.maximum(t - 1, 0)), t > 0)

        def stage0(self, a):
            s = shard(a)
            own = self.region(s, yx)
            arrived(own, self.zr + s)
            onward = jnp.where(s < t, t + 1, t - 1)
            remote(
                own, own, self.zr + s, (dp, jnp.clip(onward, 0, 3)),
                jnp.logical_and(onward >= 0, onward <= 3),
            )
            remote(own, own, self.xr + a, x_dev)
            remote(own, own, self.yr + a, y_dev)

        def stage1(self, a):
            s, half = shard(a), self.size // 2
            arrived(self.region(s, yx_x), self.xr + a)
            part = self.region(s, yx_x, 0, half)
            remote(part, part, self.dr + a, y_dev)
            arrived(self.region(s, yx_y), self.yr + a)
            part = self.region(s, yx_y, half, half)
            remote(part, part, self.dr + a, x_dev)

        def stage2(self, a):
            s = shard(a)
            arrived(self.region(s, yx_d), self.dr + a)
            four = self.ref.at[s, :, core, pl.ds(self.first, self.size), :]
            remote(four, four, self.cr + a, c_dev)

        def stage3(self, a):
            s = shard(a)
            arrived(self.ref.at[s, :, 1 - core, pl.ds(self.first, self.size), :], self.cr + a)

    upward, downward = (dp, jnp.minimum(t + 1, 3)), (dp, jnp.maximum(t - 1, 0))
    after, before = (jnp.minimum(dp + 1, n_dp - 1), t), (jnp.maximum(dp - 1, 0), t)
    not_last, not_first = dp < n_dp - 1, dp > 0

    class Exchange:
        def __init__(self, ref, first, size):
            self.ref, self.low, self.size = ref, first, size
            self.base = alloc("recv", 6)

        def at(self, slot):
            return self.ref.at[slot, pl.ds(self.low, self.size), :]

        def go(self, src, dst, dev, pred):
            remote(self.at(src), self.at(dst), self.base + dst, dev, pred)

        def get(self, slot, pred):
            arrived(self.at(slot), self.base + slot, pred)

        def first(self):
            self.go(2, 1, upward, t < 3)
            self.go(2, 3, downward, t > 0)
            self.go(2, 5, after, jnp.logical_and(t == 3, not_last))
            self.go(2, 5, before, jnp.logical_and(t == 0, not_first))

        def neighbours(self):
            self.get(1, t >= 1)
            self.get(3, t <= 2)
            self.go(1, 0, upward, t == 2)
            self.go(3, 4, downward, t == 1)

        def chain1(self):
            self.get(5, jnp.logical_and(t == 3, not_first))
            self.get(5, jnp.logical_and(t == 0, not_last))
            self.go(5, 5, downward, jnp.logical_and(t == 3, not_first))
            self.go(5, 5, upward, jnp.logical_and(t == 0, not_last))

        def chain2(self):
            self.get(5, jnp.logical_and(t == 2, not_first))
            self.get(5, jnp.logical_and(t == 1, not_last))
            self.go(5, 0, downward, jnp.logical_and(t == 2, not_first))
            self.go(5, 4, upward, jnp.logical_and(t == 1, not_last))
            self.go(1, 0, upward, t == 1)
            self.go(3, 4, downward, t == 2)

        def ends(self):
            self.get(4, t == 0)
            self.get(0, t == 3)
            self.go(4, 0, after, jnp.logical_and(t == 0, not_last))
            self.go(0, 4, before, jnp.logical_and(t == 3, not_first))

        def chain3(self):
            self.get(0, jnp.logical_and(t == 1, not_first))
            self.get(4, jnp.logical_and(t == 2, not_last))
            self.go(0, 1, downward, jnp.logical_and(t == 1, not_first))
            self.go(4, 3, upward, jnp.logical_and(t == 2, not_last))

        def third(self):
            self.get(0, jnp.logical_and(t == 0, not_first))
            self.get(4, jnp.logical_and(t == 3, not_last))

        def last(self):
            self.get(1, jnp.logical_and(t == 0, not_first))
            self.get(3, jnp.logical_and(t == 3, not_last))
            self.get(4, t == 1)
            self.get(0, t == 2)

    lane = lax.broadcasted_iota(jnp.int32, (1, LANES), 1)
    first_half = lane < HD

    def vec(i):
        return vec_in[i : i + 1, :]

    def halves(block):
        zero = jnp.zeros_like(block)
        return jnp.where(first_half, block, zero), jnp.where(first_half, zero, block)

    def clear(ref):
        def fill(pred, slot):
            @pl.when(pred)
            def _():
                ref[slot] = jnp.zeros(ref.shape[1:], ref.dtype)

        fill(jnp.logical_and(dp == 0, t <= 1), 0)
        fill(jnp.logical_and(dp == 0, t == 0), 1)
        fill(jnp.logical_and(dp == n_dp - 1, t >= 2), 4)
        fill(jnp.logical_and(dp == n_dp - 1, t == 3), 3)

    def adapter(w):
        uwin[w] = dot_nt(xwin[w], down_in[...]).astype(BF16)

    def proj(w, pos, s):
        y = dot(xwin[w], wqkv[s].reshape(width, 3 * 256))
        u = uwin[w]
        place = (tile(pos), tile(s))
        q = y[:, :256] + dot(u, lora_q[s]) + small[s, 16:17, :]
        qwin[place] = (q * (1.0 / math.sqrt(HD))).astype(BF16)
        kwin[place] = y[:, 256:512].astype(BF16)
        v = y[:, 512:] + dot(u, lora_v[s]) + small[s, 17:18, :]
        vwin[place] = v.astype(BF16)

    def proj_all(w, pos):
        adapter(w)

        @pl.loop(0, 4, unroll=4)
        def _(s):
            proj(w, pos, s)

    def loop_pairs(lo, hi, body):
        @pl.loop(lo, hi, unroll=2)
        def _(p):
            body(p, pl.ds(pl.multiple_of(p * LANES, LANES), LANES))

    def column(index):
        return jnp.sum(jnp.where(lane == index, stat[...], 0.0), axis=1, keepdims=True)

    def attend(lo, hi):
        begin, end = lo * 256, hi * 256

        def body(p, cols):
            q_heads = halves(qwin[tile(1), cols])
            k, v = kwin[begin:end, cols], vwin[begin:end, cols]
            before, outs, found = attf[:, cols], [], stat[...]
            for i in range(2):
                s = dot_nt(q_heads[i], k) + mask[:, begin:end]
                top = jnp.max(s, axis=1, keepdims=True)
                if lo:
                    old = column(2 * p + i)
                    top = jnp.maximum(top, old)
                e = jnp.exp(s - top)
                total = jnp.sum(e, axis=1, keepdims=True)
                o = dot(e.astype(BF16), v)
                if lo:
                    alpha = jnp.exp(old - top)
                    total = total + column(16 + 2 * p + i) * alpha
                    o = o + before * alpha
                if hi == 5:
                    o = o * (1.0 / total)
                    top = top + jnp.log(total)
                outs.append(o)
                found = jnp.where(lane == 2 * p + i, top, jnp.where(lane == 16 + 2 * p + i, total, found))
            o = jnp.where(first_half, outs[0], outs[1])
            attf[:, cols] = o
            if hi == 5:
                att[:, cols] = o.astype(BF16)
            stat[...] = found

        return body

    def after_attention():
        @pl.loop(0, 4, unroll=4)
        def _(n):
            acc[:, tile(n)] = dot(att[...], wo[:, :, :, :, tile(n)].reshape(width, 256))

        z = xwin[2].astype(F32) + acc[...] + vec(0)
        centre = z - jnp.mean(z, axis=1, keepdims=True)
        r = lax.rsqrt(jnp.mean(centre * centre, axis=1, keepdims=True) + NORM_EPS)
        n1 = centre * r
        norm1[...] = n1
        stat1[...] = jnp.broadcast_to(r, stat1.shape)
        m = n1 * vec(1) + vec(2)
        midb[...] = m.astype(BF16)
        acc[...] = m + vec(3)

    def up(s):
        @pl.loop(0, 4, unroll=4)
        def _(n):
            b = dot(midb[...], wup[s, :, :, :, tile(n)].reshape(width, 256)) + small[s, pl.ds(18 + n, 1), :]
            cdf = 0.5 + 0.5 * lax.erf(b * (1.0 / math.sqrt(2.0)))
            hid[s, :, tile(n)] = (b * cdf).astype(BF16)
            gelp[s, :, tile(n)] = cdf + b * jnp.exp(-0.5 * b * b) * (1.0 / math.sqrt(2.0 * math.pi))

    def down(s):
        @pl.loop(0, 4, unroll=4)
        def _(n):
            acc[:, tile(n)] += dot(hid[s], wdn[s, :, :, :, tile(n)].reshape(width, 256))

    def second_norm():
        z = acc[...]
        centre = z - jnp.mean(z, axis=1, keepdims=True)
        r = lax.rsqrt(jnp.mean(centre * centre, axis=1, keepdims=True) + NORM_EPS)
        n2 = centre * r
        midb[...] = (n2 * vec(4) + vec(5)).astype(BF16)
        g = gffn[...].astype(F32) * vec(4)
        g = r * (g - jnp.mean(g, axis=1, keepdims=True) - n2 * jnp.mean(g * n2, axis=1, keepdims=True))
        acc[...] = g
        gffn[...] = g.astype(BF16)

    def ffn_back(s):
        @pl.loop(0, 4, unroll=4)
        def _(n):
            toward = dot_nt(gffn[...], wdn[s, n].reshape(256, width))
            gbuf[:, tile(n)] = (toward * gelp[s, :, tile(n)]).astype(BF16)

        @pl.loop(0, 4, unroll=4)
        def _(n):
            acc[:, tile(n)] += dot_nt(gbuf[...], wup[s, n].reshape(256, width))

    def first_norm_back():
        g = acc[...] * vec(1)
        n1 = norm1[...]
        g = g - jnp.mean(g, axis=1, keepdims=True) - n1 * jnp.mean(g * n1, axis=1, keepdims=True)
        g = stat1[:, 0:1] * g
        acc[...] = g
        gffn[...] = g.astype(BF16)

        @pl.loop(0, 4, unroll=4)
        def _(s):
            dowin[2, :, tile(s)] = dot_nt(gffn[...], wo[s].reshape(256, width)).astype(BF16)

        product = dowin[2].astype(F32) * attf[...]
        high = product.astype(BF16)
        low = (product - high.astype(F32)).astype(BF16)
        at_row = lax.broadcasted_iota(jnp.int32, (width, LANES), 0) // HD + 16
        at_lane = lax.broadcasted_iota(jnp.int32, (width, LANES), 1)
        pick = (at_row == at_lane).astype(F32).astype(BF16)
        delta = dot(high, pick) + dot(low, pick)
        both = jnp.where(lane < 16, stat[...], delta)
        stat[...] = both
        stwin[2] = both.T[0:32]

    def pass_queries(p, cols):
        q_heads, do_heads = halves(qwin[tile(1), cols]), halves(dowin[2, :, cols])
        k, v = kwin[:, cols], vwin[:, cols]
        parts = []
        for i in range(2):
            prob = jnp.exp(dot_nt(q_heads[i], k) + mask[...] - column(2 * p + i))
            ds = prob * (dot_nt(do_heads[i], v) - column(16 + 2 * p + i))
            parts.append(dot(ds.astype(BF16), k))
        dq[:, cols] = (jnp.where(first_half, parts[0], parts[1]) * (1.0 / math.sqrt(HD))).astype(BF16)

    def pass_keys(w, pos, lo, hi, at, first=False, keys=True, values=True):
        def body(p, cols):
            k_heads, v_heads = halves(kwin[tile(1), cols]), halves(vwin[tile(1), cols])
            q, do = qwin[pos * 256 + lo : pos * 256 + hi, cols], dowin[w, lo:hi, cols]
            dk, dv = [], []
            for i in range(2):
                lse = stwin[w, pl.ds(2 * p + i, 1), :][:, lo:hi]
                prob = jnp.exp(dot_nt(k_heads[i], q) + mask[:, pos * 256 + lo : pos * 256 + hi] - lse)
                if values:
                    dv.append(dot(prob.astype(BF16), do))
                if keys:
                    delta = stwin[w, pl.ds(16 + 2 * p + i, 1), :][:, lo:hi]
                    ds = prob * (dot_nt(v_heads[i], do) - delta)
                    dk.append(dot(ds.astype(BF16), q))
            for total, parts in ((dk_acc, dk), (dv_acc, dv)):
                if parts:
                    both = jnp.where(first_half, parts[0], parts[1])
                    total[:, cols] = both if first else total[:, cols] + both

        loop_pairs(at, at + 4, body)

    def lora_partial():
        u = uwin[2].astype(F32).T[0:16].astype(BF16)
        is_query = lax.broadcasted_iota(jnp.int32, (16, 1), 0) < 8
        for s in range(4):
            cols = slice(256 * s, 256 * s + 256)
            both = jnp.where(is_query, dot(u, dq[:, cols]), dot(u, dkv[1, :, cols]))
            lsend[s] = both

    def input_gradient():
        gu = jnp.zeros((rows, LANES), F32)
        for s in range(4):
            cols = slice(256 * s, 256 * s + 256)
            gu = gu + dot_nt(dq[:, cols], lora_q[s]) + dot_nt(dkv[1, :, cols], lora_v[s])
        gu = gu.astype(BF16)

        @pl.loop(0, 4, unroll=4)
        def _(n):
            total = acc[:, tile(n)] + dot(gu, down_in[:, tile(n)])
            for s in range(4):
                cols = slice(256 * s, 256 * s + 256)
                three = jnp.concatenate([dq[:, cols], dkv[0, :, cols], dkv[1, :, cols]], axis=1)
                total = total + dot_nt(three, wqkv[s, n].reshape(256, 3 * 256))
            att[:, tile(n)] = total.astype(BF16)

    def chunk(ref, first, size, loads):
        return Chunk(ref, first, size, loads)

    qkv0, qkv1 = chunk(wqkv, 0, 64, ld_qkv), chunk(wqkv, 64, 64, ld_qkv)
    up0, up1 = chunk(wup, 0, 64, ld_up), chunk(wup, 64, 64, ld_up)
    dn0, dn1 = chunk(wdn, 0, 64, ld_dn), chunk(wdn, 64, 64, ld_dn)
    o0 = chunk(wo, 0, 32, ld_o)
    half, quarter = rows // 2, rows // 4
    tok = [Exchange(xwin, i * quarter, quarter) for i in range(4)]
    small_base = alloc("recv", 4)
    wide = [Exchange(dowin, i * quarter, quarter) for i in range(4)]
    narrow = Exchange(stwin, 0, 32)
    lora1 = alloc("recv", 4)
    lora2 = alloc("recv", n_dp)

    clear(xwin)
    done(ld_small)
    for i in range(8):
        cols = slice(LANES * i, LANES * i + LANES)
        for j, ref in enumerate(vec_refs):
            vec_in[j : j + 1, cols] = ref[i : i + 1, :].astype(F32)
    own_small = [2.0 * qu_in[...].astype(F32), 2.0 * vu_in[...].astype(F32)]
    small[t, 0:8, :] = own_small[0]
    small[t, 8:16, :] = own_small[1]
    for i in range(2):
        cols = slice(LANES * i, LANES * i + LANES)
        small[t, 16:17, cols] = qb_in[i : i + 1, :].astype(F32)
        small[t, 17:18, cols] = vb_in[i : i + 1, :].astype(F32)
        for j in range(4):
            small[t, 18 + j : 19 + j, cols] = ub_in[2 * j + i : 2 * j + i + 1, :].astype(F32)
    small[t, 22:24, :] = jnp.zeros((2, 256), F32)
    maps = [qd_in[...].astype(F32), vd_in[...].astype(F32), jnp.zeros((LANES - 16, width), F32)]
    down_in[...] = jnp.concatenate(maps, axis=0).astype(BF16)
    pl.semaphore_wait(barrier, 3 + n_dp - 1)
    done(ld_x)
    for d in range(1, 4):
        remote(small.at[t], small.at[t], small_base + t, (dp, lax.rem(t + d, 4)))

    near = jnp.where(t < 3, 3, 1)
    second = jnp.where(lax.rem(t, 2) == 0, 4, 0)
    third = jnp.where(t == 0, 0, jnp.where(t == 3, 4, 1))
    final = jnp.where(t == 0, 1, jnp.where(t == 1, 4, jnp.where(t == 2, 0, 3)))
    blocks = {"n": (near, 0), "2": (2, 1), "s": (second, 2), "t": (third, 3), "l": (final, 4)}
    named = {"q0": qkv0, "q1": qkv1, "u0": up0, "u1": up1, "d0": dn0, "d1": dn1, "o": o0}
    def setup():
        lengths = len_in[...]
        docs = lengths.shape[0] * LANES
        high, low = lengths // 256, lax.rem(lengths, 256)
        upto = (
            lax.broadcasted_iota(jnp.int32, (LANES, LANES), 0)
            <= lax.broadcasted_iota(jnp.int32, (LANES, LANES), 1)
        ).astype(F32).astype(BF16)

        def summed(part):
            return dot(part.astype(F32).astype(BF16), upto)

        ends = 256.0 * summed(high) + summed(low)
        window = mask.shape[1]
        first = (dp * 4 + t) * rows - MAXLEN
        spot = lax.broadcasted_iota(jnp.int32, (1, window), 1)
        place = spot // rows
        where = place
        for slot, nth_place in blocks.values():
            where = jnp.where(place == nth_place, slot, where)
        position = first + where * rows + lax.rem(spot, rows)
        at = position.astype(F32)
        passed = jnp.zeros((1, window), F32)
        before = jnp.zeros((1, 1), F32)
        for r in range(lengths.shape[0]):
            end = ends[r : r + 1, :] + before
            before = end[:, LANES - 1 :]
            column = jnp.broadcast_to(end, (LANES, LANES)).T[:, 0:1]
            passed = passed + jnp.sum((column <= at).astype(F32), axis=0, keepdims=True)
        inside = jnp.logical_and(position >= 0, passed < docs)
        ids = jnp.where(inside, passed, -1.0)
        own = jnp.broadcast_to(ids[:, rows : 2 * rows], (LANES, rows)).T[:, 0:1]
        mask[...] = jnp.where(own == ids, 0.0, MASKED)
        stat[...] = jnp.zeros(stat.shape, F32)

    def small_ready():
        for d in range(1, 4):
            peer = lax.rem(t + d, 4)
            arrived(small.at[peer], small_base + peer)
        none = jnp.zeros((8, 256), F32)
        lora_q[:, 16:, :] = jnp.zeros((4, LANES - 16, 256), BF16)
        lora_v[:, 16:, :] = jnp.zeros((4, LANES - 16, 256), BF16)
        for s in range(4):
            lora_q[s, 0:16, :] = jnp.concatenate([small[s, 0:8, :], none], axis=0).astype(BF16)
            lora_v[s, 0:16, :] = jnp.concatenate([none, small[s, 8:16, :]], axis=0).astype(BF16)


    def part(a):
        return t if a == 0 else shard(a)

    for item in PLAN:
        kind, rest = item[0], item[1:]
        if kind == "+":
            named[rest].send()
        elif kind in "0123":
            getattr(named[rest[:-1]], "stage" + kind)(int(rest[-1]))
        elif kind in STEPS:
            getattr(tok[int(rest)], STEPS[kind])()
        elif item == "P20":
            setup()
            small_ready()
            adapter(2)
            done(ld_qkv)
            proj(2, 1, t)
        elif kind == "P" and rest[0] == "2":
            proj(2, 1, shard(int(rest[1])))
        elif kind == "P":
            proj_all(*blocks[rest])
        elif kind == "A":
            at, lo, hi = (int(i) for i in rest)
            loop_pairs(at, at + 2, attend(lo, hi))
        elif kind == "M":
            done(ld_o)
            after_attention()
        elif kind == "U":
            done(ld_up)
            up(part(int(rest)))
        elif kind == "D":
            done(ld_dn)
            down(part(int(rest)))
    for copies in (ld_qkv, ld_o, ld_up, ld_dn):
        done(copies)

    done(ld_cot)
    second_norm()
    out_copy = local(midb, out_ref)
    clear(dowin)
    clear(stwin)

    @pl.loop(0, 4, unroll=4)
    def _(s):
        ffn_back(s)

    first_norm_back()

    def swap(step, i):
        for e in [wide[i]] + ([narrow] if i == 0 else []):
            getattr(e, step)()

    for item in PLAN_BACK:
        kind, rest = item[0], item[1:]
        if kind in STEPS:
            swap(STEPS[kind], int(rest))
        elif kind == "Q":
            loop_pairs(int(rest), int(rest) + 2, pass_queries)
        elif kind == "K":
            pass_keys(*blocks[rest[0]], 0, rows, int(rest[1]), first=rest[0] == "2")
        elif kind == "V":
            lo = int(rest) * half
            for p in range(0, pairs, 4):
                pass_keys(*blocks["l"], lo, lo + half, p, keys=False)
        elif kind == "G":
            dkv[1] = dv_acc[...].astype(BF16)
            lora_partial()
            for d in range(1, 4):
                peer = lax.rem(t + d, 4)
                remote(lsend.at[peer], lrecv1.at[t], lora1 + t, (dp, peer))
            lrecv1[t] = lsend[t]
        elif kind == "L":
            for p in range(0, pairs, 4):
                pass_keys(*blocks["l"], 0, rows, p, values=False)
            dkv[0] = dk_acc[...].astype(BF16)
        elif kind == "H":
            for d in range(1, 4):
                peer = lax.rem(t + d, 4)
                arrived(lrecv1.at[peer], lora1 + peer)
            lrecv2[dp] = 2.0 * ((lrecv1[0] + lrecv1[1]) + (lrecv1[2] + lrecv1[3]))
            for d in range(1, n_dp):
                remote(lrecv2.at[dp], lrecv2.at[dp], lora2 + dp, (lax.rem(dp + d, n_dp), t))
        elif kind == "I":
            input_gradient()
    dx_copy = local(att, dx_ref)
    for d in range(1, n_dp):
        peer = lax.rem(dp + d, n_dp)
        arrived(lrecv2.at[peer], lora2 + peer)
    total = lrecv2[0]
    for i in range(1, n_dp):
        total = total + lrecv2[i]
    lora_ref[...] = total
    dx_copy.wait()
    out_copy.wait()
    for pred, copy in pending.values():
        when(pred, copy.wait_send)
    assert count["recv"] <= rsem.shape[0] and count["local"] <= lsem.shape[0]


def hand_over(out, grad, lora, out_to, grad_to, query_to, value_to, out_at, grad_at, lora_at, sems):
    rows = out.shape[0] // 2
    halves = [pl.ds(i * rows, rows) for i in range(2)]
    loads = [(lora, lora_at)]
    stores = [[(lora_at.at[0:8], query_to), (lora_at.at[8:16], value_to)]]
    for source, at, to in ((out, out_at, out_to), (grad, grad_at, grad_to)):
        for half in halves:
            loads.append((source.at[half], at.at[half]))
            stores.append([(at.at[half], to.at[half])])
    copies = [pltpu.make_async_copy(a, b, sems.at[i]) for i, (a, b) in enumerate(loads)]
    for copy in copies:
        copy.start()
    moved = []
    for copy, pairs in zip(copies, stores):
        copy.wait()
        for a, b in pairs:
            moved.append(pltpu.make_async_copy(a, b, sems.at[len(copies) + len(moved)]))
            moved[-1].start()
    for copy in moved:
        copy.wait()


def shards(
    tokens, document_lengths, query_proj_weight, query_proj_bias, key_proj_weight, value_proj_weight,
    value_proj_bias, query_adapter_down, value_adapter_down, query_adapter_up, value_adapter_up,
    attention_out_weight, attention_out_bias, attention_norm_gain, attention_norm_bias, up_proj_weight,
    up_proj_bias, down_proj_weight, down_proj_bias, feedforward_norm_gain, feedforward_norm_bias, cotangent,
):
    rows, width = tokens.shape
    n_dp = lax.axis_size("dp")
    window = rows + 2 * MAXLEN

    def fold(vector):
        return vector.reshape(vector.shape[0] // LANES, LANES)

    def cut(weight):
        return weight.reshape(4, 2, weight.shape[0] // GROUP, weight.shape[1])

    def vmem(shape, dtype):
        return pltpu.VMEM(shape, dtype)

    small_arrays = (
        fold(document_lengths), query_adapter_down.T, value_adapter_down.T, query_adapter_up, value_adapter_up,
        fold(query_proj_bias), fold(value_proj_bias), fold(up_proj_bias), fold(attention_out_bias),
        fold(attention_norm_gain), fold(attention_norm_bias), fold(down_proj_bias), fold(feedforward_norm_gain),
        fold(feedforward_norm_bias),
    )
    any_spec = pl.BlockSpec(memory_space=pl.ANY)
    vmem_spec = pl.BlockSpec(memory_space=pltpu.VMEM)
    full = (rows, width)
    rank = query_adapter_up.shape[0]
    call = pl.pallas_call(
        lambda *refs: layer_kernel(n_dp, *refs),
        out_shape=(
            jax.ShapeDtypeStruct(full, BF16),
            jax.ShapeDtypeStruct(full, BF16),
            jax.ShapeDtypeStruct((16, 256), F32),
        ),
        in_specs=[any_spec] * 22,
        out_specs=(any_spec, any_spec, vmem_spec),
        scratch_shapes=[
            vmem((4, 4, 2, 128, 768), BF16),
            vmem((4, 4, 2, 32, 1024), BF16),
            vmem((4, 4, 2, 128, 1024), BF16),
            vmem((4, 4, 2, 128, 1024), BF16),
            vmem((4, 24, 256), F32),
            vmem((4, 128, 256), BF16),
            vmem((4, 128, 256), BF16),
            vmem((8, width), F32),
            vmem((LANES, width), BF16),
            vmem((6, rows, width), BF16),
            vmem((5, rows, LANES), BF16),
            vmem((window, width), BF16),
            vmem((window, width), BF16),
            vmem((window, width), BF16),
            vmem((6, rows, width), BF16),
            vmem((6, 32, rows), F32),
            vmem((rows, window), F32),
            vmem(full, BF16),
            vmem(full, F32),
            vmem((rows, LANES), F32),
            vmem(full, BF16),
            vmem(full, F32),
            vmem((rows, LANES), F32),
            vmem((4, rows, width), BF16),
            vmem((4, rows, width), F32),
            vmem(full, F32),
            vmem(full, BF16),
            vmem(full, BF16),
            vmem(full, BF16),
            vmem(full, F32),
            vmem(full, F32),
            vmem((2, rows, width), BF16),
            vmem((4, 16, 256), F32),
            vmem((4, 16, 256), F32),
            vmem((n_dp, 16, 256), F32),
            pltpu.SemaphoreType.DMA((26,)),
            pltpu.SemaphoreType.DMA((48,)),
            pltpu.SemaphoreType.DMA((174 + n_dp,)),
        ]
        + [vmem(a.shape, a.dtype) for a in small_arrays],
        compiler_params=pltpu.CompilerParams(
            collective_id=0, has_side_effects=True, vmem_limit_bytes=63 * 2**20
        ),
        name="layer",
    )
    out, grad, lora = call(
        tokens, cotangent, cut(query_proj_weight), cut(key_proj_weight), cut(value_proj_weight),
        cut(attention_out_weight), cut(up_proj_weight), cut(down_proj_weight), *small_arrays,
    )
    lora_shape = jax.ShapeDtypeStruct((rank, 256), F32)
    return pl.pallas_call(
        hand_over,
        out_shape=(out, grad, lora_shape, lora_shape),
        in_specs=[any_spec] * 3,
        out_specs=(any_spec,) * 4,
        scratch_shapes=[
            vmem(full, BF16), vmem(full, BF16), vmem((2 * rank, 256), F32), pltpu.SemaphoreType.DMA((11,))
        ],
        name="hand_over",
    )(out, grad, lora)


def solution(mesh):
    whole, columns = P(), P(None, "tensor")
    stream = P(("dp", "tensor"), None)
    return jax.shard_map(
        shards,
        mesh=mesh,
        in_specs=(
            stream, whole, columns, P("tensor"), columns, columns, P("tensor"), whole, whole, columns, columns,
            P("tensor", None), whole, whole, whole, columns, P("tensor"), P("tensor", None), whole, whole, whole,
            stream,
        ),
        out_specs=(stream, stream, columns, columns),
        check_vma=False,
    )
```

```python
import math

import jax
import jax.numpy as jnp
from jax import lax
from jax.experimental import pallas as pl
from jax.experimental.pallas import tpu as pltpu
from jax.sharding import PartitionSpec as P

MESH = pl.DeviceIdType.MESH
HD = 64
MAXLEN = 512
GROUP = 8
LANES = 128
NORM_EPS = 1e-05
MASKED = -1e30
STEPS = {
    "S": "first", "n": "neighbours", "c": "chain1", "C": "chain2", "x": "ends", "y": "chain3", "t": "third", "l": "last",
}
PLAN_BACK = (
    "S2", "S0", "n2", "c0", "S1", "Q2", "c2", "c1", "n0", "S3", "C0", "Q6", "n1", "x2", "c3", "y0", "C2", "Q0",
    "C1", "x0", "n3", "x1", "t2", "y2", "Kn24", "C3", "Q4", "y1", "t0", "x3", "l0", "Kn20", "t3", "t1", "l1", "l2",
    "y3", "Kst0", "Kst4", "l3", "V", "G", "L", "H", "I", "J",
)
PLAN = (
    "+q1", "+q0", "S2", "0q11", "0q01", "1q11", "0q12", "0q02", "2q11", "1q01", "S3", "0q03", "+o", "+u0", "c3",
    "2q01", "1q02", "1q03", "0o1", "0o2", "0q13", "+u1", "0u01", "1q13", "+d1", "0u11", "S1", "2q13", "S0", "1u01",
    "P20", "1q12", "2q03", "0u02", "0u12", "3q11", "n2", "2q02", "n3", "c1", "C3", "3q01", "3q13", "2q12", "1u02",
    "1u11", "3q02", "2u01", "3q12", "3q03", "n1", "c2", "1o1", "n0", "x3", "+d0", "P2", "c0", "1o2", "x2", "1u12",
    "C1", "2u11", "Pn", "x1", "x0", "t2", "2o1", "2o2", "0o3", "t0", "0d11", "A002", "t1", "0u03", "3u01", "1o3",
    "0d01", "2u12", "3o1", "C2", "t3", "2u02", "3o2", "Pt", "0d02", "3u11", "y3", "2o3", "A402", "C0", "0d12",
    "0u13", "l3", "3o3", "y0", "y2", "y1", "Ps", "1u03", "l0", "1d11", "A024", "A424", "l2", "1d01", "1u13", "l1",
    "2u03", "1d02", "0d13", "2d11", "Pl", "A445", "1d12", "2d01", "0d03", "2d02", "2u13", "A045", "3u12", "M", "U1",
    "3u02", "1d13", "2d12", "3u13", "U0", "3d01", "1d03", "3d11", "D1", "3d12", "2d13", "U2", "3d02", "3u03",
    "2d03", "U3", "D2", "D0", "3d03", "3d13", "D3",
)
F32 = jnp.float32
BF16 = jnp.bfloat16


def dot(left, right):
    return lax.dot_general(left, right, (((1,), (0,)), ((), ())), preferred_element_type=F32)


def dot_nt(left, right):
    return lax.dot_general(left, right, (((1,), (1,)), ((), ())), preferred_element_type=F32)


def tile(n):
    return pl.ds(pl.multiple_of(n * 256, 256), 256)


def layer_kernel(
    n_dp,
    x_in, cot_in, wq_in, wk_in, wv_in, wo_in, wup_in, wdn_in,
    len_in, qd_in, vd_in, qu_in, vu_in, qb_in, vb_in, ub_in, *rest
):
    small_from = (len_in, qd_in, vd_in, qu_in, vu_in, qb_in, vb_in, ub_in, *rest[:6])
    rest = rest[6:]
    (
        out_ref, dx_ref, lora_ref,
        wqkv, wo, wup, wdn, small, lora_q, lora_v, vec_in, down_in,
        xwin, uwin, qwin, kwin, vwin, dowin, stwin, mask,
        att, attf, stat, midb, norm1, stat1, hid, gelp, acc, gffn, gbuf, dq, dk_acc, dv_acc, dkv,
        lsend, lrecv1, lrecv2,
        lsem, ssem, rsem,
        *small_to,
    ) = rest
    len_in, qd_in, vd_in, qu_in, vu_in, qb_in, vb_in, ub_in, *vec_refs = small_to
    rows = x_in.shape[0]
    width = x_in.shape[1]
    pairs = width // LANES
    dp, t = lax.axis_index("dp"), lax.axis_index("tensor")
    member = lax.rem(dp, GROUP)
    core = lax.rem(member, 2)
    yx = member // 2
    yx_x = yx + 1 - 2 * lax.rem(yx, 2)
    yx_y = yx + 2 - 4 * (yx // 2)
    yx_d = 3 - yx
    x_dev = (dp + 2 * (yx_x - yx), t)
    y_dev = (dp + 2 * (yx_y - yx), t)
    c_dev = (dp + 1 - 2 * core, t)

    def shard(a):
        first = jnp.where(t == 0, 1, t - 1)
        second = jnp.where(t == 0, 2, jnp.where(t == 3, 1, t + 1))
        third = jnp.where(t < 2, 3, 0)
        return jnp.where(a == 1, first, jnp.where(a == 2, second, third))

    barrier = pltpu.get_barrier_semaphore()
    for d in range(1, 4):
        pl.semaphore_signal(barrier, inc=1, device_id=(dp, lax.rem(t + d, 4)), device_id_type=MESH)
    for d in range(1, n_dp):
        pl.semaphore_signal(barrier, inc=1, device_id=(lax.rem(dp + d, n_dp), t), device_id_type=MESH)

    count = {"send": 0, "recv": 0, "local": 0}
    pending = {}

    def alloc(kind, n):
        first = count[kind]
        count[kind] += n
        return first

    def when(pred, fn):
        if pred is None:
            fn()
        else:
            pl.when(pred)(fn)

    def remote(src, dst, recv, dev, pred=None):
        slot = alloc("send", 1) % ssem.shape[0]
        if slot in pending:
            before, copy = pending[slot]
            when(before, copy.wait_send)
        copy = pltpu.make_async_remote_copy(
            src_ref=src, dst_ref=dst, send_sem=ssem.at[slot], recv_sem=rsem.at[recv],
            device_id=dev, device_id_type=MESH,
        )
        when(pred, copy.start)
        pending[slot] = (pred, copy)

    def arrived(dst, recv, pred=None):
        copy = pltpu.make_async_remote_copy(
            src_ref=dst, dst_ref=dst, send_sem=ssem.at[0], recv_sem=rsem.at[recv],
            device_id=(dp, t), device_id_type=MESH,
        )
        when(pred, copy.wait_recv)

    def local(src, dst):
        copy = pltpu.make_async_copy(src, dst, lsem.at[alloc("local", 1)])
        copy.start()
        return copy

    ld_small = [local(a, b) for a, b in zip(small_from, small_to)]
    ld_qkv = [
        local(w, wqkv.at[t, :, :, :, pl.ds(256 * i, 256)]) for i, w in enumerate((wq_in, wk_in, wv_in))
    ]
    ld_x = [local(x_in, xwin.at[2])]
    ld_up = [local(wup_in, wup.at[t])]
    ld_o = [local(wo_in, wo.at[t])]
    ld_dn = [local(wdn_in, wdn.at[t])]
    ld_cot = [local(cot_in, gffn)]

    def done(copies):
        while copies:
            copies.pop().wait()

    class Chunk:
        def __init__(self, ref, first, size, loads):
            self.ref, self.first, self.size, self.loads = ref, first, size, loads
            self.zr = alloc("recv", 4)
            self.xr, self.yr, self.dr, self.cr = (alloc("recv", 3) - 1 for _ in range(4))

        def region(self, s, place, lo=0, size=None):
            return self.ref.at[s, place, core, pl.ds(self.first + lo, size or self.size), :]

        def send(self):
            done(self.loads)
            own = self.region(t, yx)
            remote(own, own, self.zr + t, (dp, jnp.minimum(t + 1, 3)), t < 3)
            remote(own, own, self.zr + t, (dp, jnp.maximum(t - 1, 0)), t > 0)

        def stage0(self, a):
            s = shard(a)
            own = self.region(s, yx)
            arrived(own, self.zr + s)
            onward = jnp.where(s < t, t + 1, t - 1)
            remote(
                own, own, self.zr + s, (dp, jnp.clip(onward, 0, 3)),
                jnp.logical_and(onward >= 0, onward <= 3),
            )
            remote(own, own, self.xr + a, x_dev)
            remote(own, own, self.yr + a, y_dev)

        def stage1(self, a):
            s, half = shard(a), self.size // 2
            arrived(self.region(s, yx_x), self.xr + a)
            part = self.region(s, yx_x, 0, half)
            remote(part, part, self.dr + a, y_dev)
            arrived(self.region(s, yx_y), self.yr + a)
            part = self.region(s, yx_y, half, half)
            remote(part, part, self.dr + a, x_dev)

        def stage2(self, a):
            s = shard(a)
            arrived(self.region(s, yx_d), self.dr + a)
            four = self.ref.at[s, :, core, pl.ds(self.first, self.size), :]
            remote(four, four, self.cr + a, c_dev)

        def stage3(self, a):
            s = shard(a)
            arrived(self.ref.at[s, :, 1 - core, pl.ds(self.first, self.size), :], self.cr + a)

    upward, downward = (dp, jnp.minimum(t + 1, 3)), (dp, jnp.maximum(t - 1, 0))
    after, before = (jnp.minimum(dp + 1, n_dp - 1), t), (jnp.maximum(dp - 1, 0), t)
    not_last, not_first = dp < n_dp - 1, dp > 0

    class Exchange:
        def __init__(self, ref, first, size):
            self.ref, self.low, self.size = ref, first, size
            self.base = alloc("recv", 6)

        def at(self, slot):
            return self.ref.at[slot, pl.ds(self.low, self.size), :]

        def go(self, src, dst, dev, pred):
            remote(self.at(src), self.at(dst), self.base + dst, dev, pred)

        def get(self, slot, pred):
            arrived(self.at(slot), self.base + slot, pred)

        def first(self):
            self.go(2, 1, upward, t < 3)
            self.go(2, 3, downward, t > 0)
            self.go(2, 5, after, jnp.logical_and(t == 3, not_last))
            self.go(2, 5, before, jnp.logical_and(t == 0, not_first))

        def neighbours(self):
            self.get(1, t >= 1)
            self.get(3, t <= 2)
            self.go(1, 0, upward, t == 2)
            self.go(3, 4, downward, t == 1)

        def chain1(self):
            self.get(5, jnp.logical_and(t == 3, not_first))
            self.get(5, jnp.logical_and(t == 0, not_last))
            self.go(5, 5, downward, jnp.logical_and(t == 3, not_first))
            self.go(5, 5, upward, jnp.logical_and(t == 0, not_last))

        def chain2(self):
            self.get(5, jnp.logical_and(t == 2, not_first))
            self.get(5, jnp.logical_and(t == 1, not_last))
            self.go(5, 0, downward, jnp.logical_and(t == 2, not_first))
            self.go(5, 4, upward, jnp.logical_and(t == 1, not_last))
            self.go(1, 0, upward, t == 1)
            self.go(3, 4, downward, t == 2)

        def ends(self):
            self.get(4, t == 0)
            self.get(0, t == 3)
            self.go(4, 0, after, jnp.logical_and(t == 0, not_last))
            self.go(0, 4, before, jnp.logical_and(t == 3, not_first))

        def chain3(self):
            self.get(0, jnp.logical_and(t == 1, not_first))
            self.get(4, jnp.logical_and(t == 2, not_last))
            self.go(0, 1, downward, jnp.logical_and(t == 1, not_first))
            self.go(4, 3, upward, jnp.logical_and(t == 2, not_last))

        def third(self):
            self.get(0, jnp.logical_and(t == 0, not_first))
            self.get(4, jnp.logical_and(t == 3, not_last))

        def last(self):
            self.get(1, jnp.logical_and(t == 0, not_first))
            self.get(3, jnp.logical_and(t == 3, not_last))
            self.get(4, t == 1)
            self.get(0, t == 2)

    lane = lax.broadcasted_iota(jnp.int32, (1, LANES), 1)
    first_half = lane < HD

    def vec(i):
        return vec_in[i : i + 1, :]

    def halves(block):
        zero = jnp.zeros_like(block)
        return jnp.where(first_half, block, zero), jnp.where(first_half, zero, block)

    def clear(ref):
        def fill(pred, slot):
            @pl.when(pred)
            def _():
                ref[slot] = jnp.zeros(ref.shape[1:], ref.dtype)

        fill(jnp.logical_and(dp == 0, t <= 1), 0)
        fill(jnp.logical_and(dp == 0, t == 0), 1)
        fill(jnp.logical_and(dp == n_dp - 1, t >= 2), 4)
        fill(jnp.logical_and(dp == n_dp - 1, t == 3), 3)

    def adapter(w):
        uwin[w] = dot_nt(xwin[w], down_in[...]).astype(BF16)

    def proj(w, pos, s):
        y = dot(xwin[w], wqkv[s].reshape(width, 3 * 256))
        u = uwin[w]
        place = (tile(pos), tile(s))
        q = y[:, :256] + dot(u, lora_q[s]) + small[s, 16:17, :]
        qwin[place] = (q * (1.0 / math.sqrt(HD))).astype(BF16)
        kwin[place] = y[:, 256:512].astype(BF16)
        v = y[:, 512:] + dot(u, lora_v[s]) + small[s, 17:18, :]
        vwin[place] = v.astype(BF16)

    def proj_all(w, pos):
        adapter(w)

        @pl.loop(0, 4)
        def _(s):
            proj(w, pos, s)

    def loop_pairs(lo, hi, body, unroll=1):
        @pl.loop(lo, hi, unroll=unroll)
        def _(p):
            body(p, pl.ds(pl.multiple_of(p * LANES, LANES), LANES))

    def column(index):
        return jnp.sum(jnp.where(lane == index, stat[...], 0.0), axis=1, keepdims=True)

    def attend(lo, hi):
        begin, end = lo * 256, hi * 256

        def body(p, cols):
            q_heads = halves(qwin[tile(1), cols])
            k, v = kwin[begin:end, cols], vwin[begin:end, cols]
            before, outs, found = attf[:, cols], [], stat[...]
            for i in range(2):
                s = dot_nt(q_heads[i], k) + mask[:, begin:end]
                top = jnp.max(s, axis=1, keepdims=True)
                if lo:
                    old = column(2 * p + i)
                    top = jnp.maximum(top, old)
                e = jnp.exp(s - top)
                total = jnp.sum(e, axis=1, keepdims=True)
                o = dot(e.astype(BF16), v)
                if lo:
                    alpha = jnp.exp(old - top)
                    total = total + column(16 + 2 * p + i) * alpha
                    o = o + before * alpha
                if hi == 5:
                    o = o * (1.0 / total)
                    top = top + jnp.log(total)
                outs.append(o)
                found = jnp.where(lane == 2 * p + i, top, jnp.where(lane == 16 + 2 * p + i, total, found))
            o = jnp.where(first_half, outs[0], outs[1])
            attf[:, cols] = o
            if hi == 5:
                att[:, cols] = o.astype(BF16)
            stat[...] = found

        return body

    def after_attention():
        @pl.loop(0, 4, unroll=4)
        def _(n):
            acc[:, tile(n)] = dot(att[...], wo[:, :, :, :, tile(n)].reshape(width, 256))

        z = xwin[2].astype(F32) + acc[...] + vec(0)
        centre = z - jnp.mean(z, axis=1, keepdims=True)
        r = lax.rsqrt(jnp.mean(centre * centre, axis=1, keepdims=True) + NORM_EPS)
        n1 = centre * r
        norm1[...] = n1
        stat1[...] = jnp.broadcast_to(r, stat1.shape)
        m = n1 * vec(1) + vec(2)
        midb[...] = m.astype(BF16)
        acc[...] = m + vec(3)

    def up(s):
        @pl.loop(0, 4, unroll=4)
        def _(n):
            b = dot(midb[...], wup[s, :, :, :, tile(n)].reshape(width, 256)) + small[s, pl.ds(18 + n, 1), :]
            cdf = 0.5 + 0.5 * lax.erf(b * (1.0 / math.sqrt(2.0)))
            hid[s, :, tile(n)] = (b * cdf).astype(BF16)
            gelp[s, :, tile(n)] = cdf + b * jnp.exp(-0.5 * b * b) * (1.0 / math.sqrt(2.0 * math.pi))

    def down(s):
        @pl.loop(0, 4, unroll=4)
        def _(n):
            acc[:, tile(n)] += dot(hid[s], wdn[s, :, :, :, tile(n)].reshape(width, 256))

    def second_norm():
        z = acc[...]
        centre = z - jnp.mean(z, axis=1, keepdims=True)
        r = lax.rsqrt(jnp.mean(centre * centre, axis=1, keepdims=True) + NORM_EPS)
        n2 = centre * r
        midb[...] = (n2 * vec(4) + vec(5)).astype(BF16)
        g = gffn[...].astype(F32) * vec(4)
        g = r * (g - jnp.mean(g, axis=1, keepdims=True) - n2 * jnp.mean(g * n2, axis=1, keepdims=True))
        acc[...] = g
        gffn[...] = g.astype(BF16)

    def ffn_back(s):
        @pl.loop(0, 4, unroll=4)
        def _(n):
            toward = dot_nt(gffn[...], wdn[s, n].reshape(256, width))
            gbuf[:, tile(n)] = (toward * gelp[s, :, tile(n)]).astype(BF16)

        @pl.loop(0, 4, unroll=4)
        def _(n):
            acc[:, tile(n)] += dot_nt(gbuf[...], wup[s, n].reshape(256, width))

    def first_norm_back():
        g = acc[...] * vec(1)
        n1 = norm1[...]
        g = g - jnp.mean(g, axis=1, keepdims=True) - n1 * jnp.mean(g * n1, axis=1, keepdims=True)
        g = stat1[:, 0:1] * g
        acc[...] = g
        gffn[...] = g.astype(BF16)

        @pl.loop(0, 4, unroll=4)
        def _(s):
            dowin[2, :, tile(s)] = dot_nt(gffn[...], wo[s].reshape(256, width)).astype(BF16)

        product = dowin[2].astype(F32) * attf[...]
        high = product.astype(BF16)
        low = (product - high.astype(F32)).astype(BF16)
        at_row = lax.broadcasted_iota(jnp.int32, (width, LANES), 0) // HD + 16
        at_lane = lax.broadcasted_iota(jnp.int32, (width, LANES), 1)
        pick = (at_row == at_lane).astype(F32).astype(BF16)
        delta = dot(high, pick) + dot(low, pick)
        both = jnp.where(lane < 16, stat[...], delta)
        stat[...] = both
        stwin[2] = both.T[0:32]

    def pass_queries(p, cols):
        q_heads, do_heads = halves(qwin[tile(1), cols]), halves(dowin[2, :, cols])
        k, v = kwin[:, cols], vwin[:, cols]
        parts = []
        for i in range(2):
            prob = jnp.exp(dot_nt(q_heads[i], k) + mask[...] - column(2 * p + i))
            ds = prob * (dot_nt(do_heads[i], v) - column(16 + 2 * p + i))
            parts.append(dot(ds.astype(BF16), k))
        dq[:, cols] = (jnp.where(first_half, parts[0], parts[1]) * (1.0 / math.sqrt(HD))).astype(BF16)

    def pass_keys(names, at, end, first=False, keys=True, values=True, unroll=1):
        slots = [blocks[name][0] for name in names]
        begin = blocks[names[0]][1] * rows
        window = slice(begin, begin + len(names) * rows)

        def line(index):
            parts = [stwin[w, pl.ds(index, 1), :] for w in slots]
            return parts[0] if len(parts) == 1 else jnp.concatenate(parts, axis=1)

        def body(p, cols):
            k_heads, v_heads = halves(kwin[tile(1), cols]), halves(vwin[tile(1), cols])
            q, do = qwin[window, cols], [dowin[w, :, cols] for w in slots]
            do = do[0] if len(do) == 1 else jnp.concatenate(do, axis=0)
            if len(slots) == 1:
                scores = dot_nt(jnp.concatenate(k_heads, axis=0), q)
                scores = [scores[:256], scores[256:]]
                if keys:
                    grads = dot_nt(jnp.concatenate(v_heads, axis=0), do)
                    grads = [grads[:256], grads[256:]]
            else:
                scores = [dot_nt(k, q) for k in k_heads]
                grads = [dot_nt(v, do) for v in v_heads]
            probs, ds = [], []
            for i in range(2):
                prob = jnp.exp(scores[i] + mask[:, window] - line(2 * p + i))
                if keys:
                    ds.append((prob * (grads[i] - line(16 + 2 * p + i))).astype(BF16))
                probs.append(prob.astype(BF16))
            for total, lefts, right, wanted in ((dk_acc, ds, q, keys), (dv_acc, probs, do, values)):
                if wanted:
                    if len(slots) == 1:
                        both = dot(jnp.concatenate(lefts, axis=0), right)
                        both = jnp.where(first_half, both[:256], both[256:])
                    else:
                        both = jnp.where(first_half, dot(lefts[0], right), dot(lefts[1], right))
                    total[:, cols] = both if first else total[:, cols] + both

        loop_pairs(at, end, body, unroll)

    def lora_partial():
        u = uwin[2].astype(F32).T[0:16].astype(BF16)
        is_query = lax.broadcasted_iota(jnp.int32, (16, 1), 0) < 8
        for s in range(4):
            cols = slice(256 * s, 256 * s + 256)
            both = jnp.where(is_query, dot(u, dq[:, cols]), dot(u, dkv[1, :, cols]))
            lsend[s] = both

    def input_gradient():
        gu = jnp.zeros((rows, LANES), F32)
        for s in range(4):
            cols = slice(256 * s, 256 * s + 256)
            gu = gu + dot_nt(dq[:, cols], lora_q[s]) + dot_nt(dkv[1, :, cols], lora_v[s])
        gu = gu.astype(BF16)

        @pl.loop(0, 4, unroll=4)
        def _(n):
            total = acc[:, tile(n)] + dot(gu, down_in[:, tile(n)])
            for s in range(4):
                cols = slice(256 * s, 256 * s + 256)
                three = jnp.concatenate([dq[:, cols], dkv[0, :, cols], dkv[1, :, cols]], axis=1)
                total = total + dot_nt(three, wqkv[s, n].reshape(256, 3 * 256))
            att[:, tile(n)] = total.astype(BF16)

    def chunk(ref, first, size, loads):
        return Chunk(ref, first, size, loads)

    qkv0, qkv1 = chunk(wqkv, 0, 64, ld_qkv), chunk(wqkv, 64, 64, ld_qkv)
    up0, up1 = chunk(wup, 0, 64, ld_up), chunk(wup, 64, 64, ld_up)
    dn0, dn1 = chunk(wdn, 0, 64, ld_dn), chunk(wdn, 64, 64, ld_dn)
    o0 = chunk(wo, 0, 32, ld_o)
    quarter = rows // 4
    tok = [Exchange(xwin, i * quarter, quarter) for i in range(4)]
    small_base = alloc("recv", 4)
    wide = [Exchange(dowin, i * quarter, quarter) for i in range(4)]
    narrow = Exchange(stwin, 0, 32)
    lora1 = alloc("recv", 4)
    lora2 = alloc("recv", n_dp)

    clear(xwin)
    done(ld_small)
    for i in range(8):
        cols = slice(LANES * i, LANES * i + LANES)
        for j, ref in enumerate(vec_refs):
            vec_in[j : j + 1, cols] = ref[i : i + 1, :].astype(F32)
    own_small = [2.0 * qu_in[...].astype(F32), 2.0 * vu_in[...].astype(F32)]
    small[t, 0:8, :] = own_small[0]
    small[t, 8:16, :] = own_small[1]
    for i in range(2):
        cols = slice(LANES * i, LANES * i + LANES)
        small[t, 16:17, cols] = qb_in[i : i + 1, :].astype(F32)
        small[t, 17:18, cols] = vb_in[i : i + 1, :].astype(F32)
        for j in range(4):
            small[t, 18 + j : 19 + j, cols] = ub_in[2 * j + i : 2 * j + i + 1, :].astype(F32)
    small[t, 22:24, :] = jnp.zeros((2, 256), F32)
    maps = [qd_in[...].astype(F32), vd_in[...].astype(F32), jnp.zeros((LANES - 16, width), F32)]
    down_in[...] = jnp.concatenate(maps, axis=0).astype(BF16)
    pl.semaphore_wait(barrier, 3 + n_dp - 1)
    done(ld_x)
    for d in range(1, 4):
        remote(small.at[t], small.at[t], small_base + t, (dp, lax.rem(t + d, 4)))

    near = jnp.where(t < 3, 3, 1)
    second = jnp.where(lax.rem(t, 2) == 0, 4, 0)
    third = jnp.where(t == 0, 0, jnp.where(t == 3, 4, 1))
    final = jnp.where(t == 0, 1, jnp.where(t == 1, 4, jnp.where(t == 2, 0, 3)))
    blocks = {"n": (near, 0), "2": (2, 1), "s": (second, 2), "t": (third, 3), "l": (final, 4)}
    named = {"q0": qkv0, "q1": qkv1, "u0": up0, "u1": up1, "d0": dn0, "d1": dn1, "o": o0}
    def setup():
        lengths = len_in[...]
        docs = lengths.shape[0] * LANES
        high, low = lengths // 256, lax.rem(lengths, 256)
        upto = (
            lax.broadcasted_iota(jnp.int32, (LANES, LANES), 0)
            <= lax.broadcasted_iota(jnp.int32, (LANES, LANES), 1)
        ).astype(F32).astype(BF16)

        def summed(part):
            return dot(part.astype(F32).astype(BF16), upto)

        ends = 256.0 * summed(high) + summed(low)
        window = mask.shape[1]
        first = (dp * 4 + t) * rows - MAXLEN
        spot = lax.broadcasted_iota(jnp.int32, (1, window), 1)
        place = spot // rows
        where = place
        for slot, nth_place in blocks.values():
            where = jnp.where(place == nth_place, slot, where)
        position = first + where * rows + lax.rem(spot, rows)
        at = position.astype(F32)
        passed = jnp.zeros((1, window), F32)
        before = jnp.zeros((1, 1), F32)
        for r in range(lengths.shape[0]):
            end = ends[r : r + 1, :] + before
            before = end[:, LANES - 1 :]
            column = jnp.broadcast_to(end, (LANES, LANES)).T[:, 0:1]
            passed = passed + jnp.sum((column <= at).astype(F32), axis=0, keepdims=True)
        inside = jnp.logical_and(position >= 0, passed < docs)
        ids = jnp.where(inside, passed, -1.0)
        own = jnp.broadcast_to(ids[:, rows : 2 * rows], (LANES, rows)).T[:, 0:1]
        mask[...] = jnp.where(own == ids, 0.0, MASKED)
        stat[...] = jnp.zeros(stat.shape, F32)

    def small_ready():
        for d in range(1, 4):
            peer = lax.rem(t + d, 4)
            arrived(small.at[peer], small_base + peer)
        none = jnp.zeros((8, 256), F32)
        lora_q[:, 16:, :] = jnp.zeros((4, LANES - 16, 256), BF16)
        lora_v[:, 16:, :] = jnp.zeros((4, LANES - 16, 256), BF16)
        for s in range(4):
            lora_q[s, 0:16, :] = jnp.concatenate([small[s, 0:8, :], none], axis=0).astype(BF16)
            lora_v[s, 0:16, :] = jnp.concatenate([none, small[s, 8:16, :]], axis=0).astype(BF16)


    def part(a):
        return t if a == 0 else shard(a)

    for item in PLAN:
        kind, rest = item[0], item[1:]
        if kind == "+":
            named[rest].send()
        elif kind in "0123":
            getattr(named[rest[:-1]], "stage" + kind)(int(rest[-1]))
        elif kind in STEPS:
            getattr(tok[int(rest)], STEPS[kind])()
        elif item == "P20":
            setup()
            small_ready()
            adapter(2)
            done(ld_qkv)
            proj(2, 1, t)
        elif item == "P2":

            @pl.loop(1, 4)
            def _(a):
                proj(2, 1, shard(a))

        elif kind == "P":
            proj_all(*blocks[rest])
        elif kind == "A":
            at, lo, hi = (int(i) for i in rest)
            loop_pairs(at, at + 4, attend(lo, hi))
        elif kind == "M":
            done(ld_o)
            after_attention()
        elif kind == "U":
            done(ld_up)
            up(part(int(rest)))
        elif kind == "D":
            done(ld_dn)
            down(part(int(rest)))
    for copies in (ld_qkv, ld_o, ld_up, ld_dn):
        done(copies)

    done(ld_cot)
    second_norm()
    out_copy = local(midb, out_ref)
    clear(dowin)
    clear(stwin)

    @pl.loop(0, 4)
    def _(s):
        ffn_back(s)

    first_norm_back()

    def swap(step, i):
        for e in [wide[i]] + ([narrow] if i == 0 else []):
            getattr(e, step)()

    for item in PLAN_BACK:
        kind, rest = item[0], item[1:]
        if kind in STEPS:
            swap(STEPS[kind], int(rest))
        elif kind == "Q":
            loop_pairs(int(rest), int(rest) + 2, pass_queries)
        elif kind == "K":
            names, at = rest[:2], int(rest[2])
            pass_keys(names, at, at + 4, first=names == "n2")
        elif kind == "V":
            pass_keys("l", 0, pairs, keys=False, unroll=2)
        elif kind == "G":
            dkv[1] = dv_acc[...].astype(BF16)
            lora_partial()
            for d in range(1, 4):
                peer = lax.rem(t + d, 4)
                remote(lsend.at[peer], lrecv1.at[t], lora1 + t, (dp, peer))
            lrecv1[t] = lsend[t]
        elif kind == "L":
            pass_keys("l", 0, pairs, values=False, unroll=2)
            dkv[0] = dk_acc[...].astype(BF16)
        elif kind == "H":
            for d in range(1, 4):
                peer = lax.rem(t + d, 4)
                arrived(lrecv1.at[peer], lora1 + peer)
            lrecv2[dp] = 2.0 * ((lrecv1[0] + lrecv1[1]) + (lrecv1[2] + lrecv1[3]))
            for d in range(1, n_dp):
                remote(lrecv2.at[dp], lrecv2.at[dp], lora2 + dp, (lax.rem(dp + d, n_dp), t))
        elif kind == "I":
            input_gradient()
    dx_copy = local(att, dx_ref)
    for d in range(1, n_dp):
        peer = lax.rem(dp + d, n_dp)
        arrived(lrecv2.at[peer], lora2 + peer)
    total = lrecv2[0]
    for i in range(1, n_dp):
        total = total + lrecv2[i]
    lora_ref[...] = total
    dx_copy.wait()
    out_copy.wait()
    for pred, copy in pending.values():
        when(pred, copy.wait_send)
    assert count["recv"] <= rsem.shape[0] and count["local"] <= lsem.shape[0]


def hand_over(out, grad, lora, out_to, grad_to, query_to, value_to, out_at, grad_at, lora_at, sems):
    rows = out.shape[0] // 2
    halves = [pl.ds(i * rows, rows) for i in range(2)]
    loads = [(lora, lora_at)]
    stores = [[(lora_at.at[0:8], query_to), (lora_at.at[8:16], value_to)]]
    for source, at, to in ((out, out_at, out_to), (grad, grad_at, grad_to)):
        for half in halves:
            loads.append((source.at[half], at.at[half]))
            stores.append([(at.at[half], to.at[half])])
    copies = [pltpu.make_async_copy(a, b, sems.at[i]) for i, (a, b) in enumerate(loads)]
    for copy in copies:
        copy.start()
    moved = []
    for copy, pairs in zip(copies, stores):
        copy.wait()
        for a, b in pairs:
            moved.append(pltpu.make_async_copy(a, b, sems.at[len(copies) + len(moved)]))
            moved[-1].start()
    for copy in moved:
        copy.wait()


def shards(
    tokens, document_lengths, query_proj_weight, query_proj_bias, key_proj_weight, value_proj_weight,
    value_proj_bias, query_adapter_down, value_adapter_down, query_adapter_up, value_adapter_up,
    attention_out_weight, attention_out_bias, attention_norm_gain, attention_norm_bias, up_proj_weight,
    up_proj_bias, down_proj_weight, down_proj_bias, feedforward_norm_gain, feedforward_norm_bias, cotangent,
):
    rows, width = tokens.shape
    n_dp = lax.axis_size("dp")
    window = rows + 2 * MAXLEN

    def fold(vector):
        return vector.reshape(vector.shape[0] // LANES, LANES)

    def cut(weight):
        return weight.reshape(4, 2, weight.shape[0] // GROUP, weight.shape[1])

    def vmem(shape, dtype):
        return pltpu.VMEM(shape, dtype)

    small_arrays = (
        fold(document_lengths), query_adapter_down.T, value_adapter_down.T, query_adapter_up, value_adapter_up,
        fold(query_proj_bias), fold(value_proj_bias), fold(up_proj_bias), fold(attention_out_bias),
        fold(attention_norm_gain), fold(attention_norm_bias), fold(down_proj_bias), fold(feedforward_norm_gain),
        fold(feedforward_norm_bias),
    )
    any_spec = pl.BlockSpec(memory_space=pl.ANY)
    vmem_spec = pl.BlockSpec(memory_space=pltpu.VMEM)
    full = (rows, width)
    rank = query_adapter_up.shape[0]
    call = pl.pallas_call(
        lambda *refs: layer_kernel(n_dp, *refs),
        out_shape=(
            jax.ShapeDtypeStruct(full, BF16),
            jax.ShapeDtypeStruct(full, BF16),
            jax.ShapeDtypeStruct((16, 256), F32),
        ),
        in_specs=[any_spec] * 22,
        out_specs=(any_spec, any_spec, vmem_spec),
        scratch_shapes=[
            vmem((4, 4, 2, 128, 768), BF16),
            vmem((4, 4, 2, 32, 1024), BF16),
            vmem((4, 4, 2, 128, 1024), BF16),
            vmem((4, 4, 2, 128, 1024), BF16),
            vmem((4, 24, 256), F32),
            vmem((4, 128, 256), BF16),
            vmem((4, 128, 256), BF16),
            vmem((8, width), F32),
            vmem((LANES, width), BF16),
            vmem((6, rows, width), BF16),
            vmem((5, rows, LANES), BF16),
            vmem((window, width), BF16),
            vmem((window, width), BF16),
            vmem((window, width), BF16),
            vmem((6, rows, width), BF16),
            vmem((6, 32, rows), F32),
            vmem((rows, window), F32),
            vmem(full, BF16),
            vmem(full, F32),
            vmem((rows, LANES), F32),
            vmem(full, BF16),
            vmem(full, F32),
            vmem((rows, LANES), F32),
            vmem((4, rows, width), BF16),
            vmem((4, rows, width), F32),
            vmem(full, F32),
            vmem(full, BF16),
            vmem(full, BF16),
            vmem(full, BF16),
            vmem(full, F32),
            vmem(full, F32),
            vmem((2, rows, width), BF16),
            vmem((4, 16, 256), F32),
            vmem((4, 16, 256), F32),
            vmem((n_dp, 16, 256), F32),
            pltpu.SemaphoreType.DMA((26,)),
            pltpu.SemaphoreType.DMA((48,)),
            pltpu.SemaphoreType.DMA((174 + n_dp,)),
        ]
        + [vmem(a.shape, a.dtype) for a in small_arrays],
        compiler_params=pltpu.CompilerParams(
            collective_id=0, has_side_effects=True, vmem_limit_bytes=63 * 2**20
        ),
        name="layer",
    )
    out, grad, lora = call(
        tokens, cotangent, cut(query_proj_weight), cut(key_proj_weight), cut(value_proj_weight),
        cut(attention_out_weight), cut(up_proj_weight), cut(down_proj_weight), *small_arrays,
    )
    lora_shape = jax.ShapeDtypeStruct((rank, 256), F32)
    return pl.pallas_call(
        hand_over,
        out_shape=(out, grad, lora_shape, lora_shape),
        in_specs=[any_spec] * 3,
        out_specs=(any_spec,) * 4,
        scratch_shapes=[
            vmem(full, BF16), vmem(full, BF16), vmem((2 * rank, 256), F32), pltpu.SemaphoreType.DMA((11,))
        ],
        name="hand_over",
    )(out, grad, lora)


def solution(mesh):
    whole, columns = P(), P(None, "tensor")
    stream = P(("dp", "tensor"), None)
    return jax.shard_map(
        shards,
        mesh=mesh,
        in_specs=(
            stream, whole, columns, P("tensor"), columns, columns, P("tensor"), whole, whole, columns, columns,
            P("tensor", None), whole, whole, whole, columns, P("tensor"), P("tensor", None), whole, whole, whole,
            stream,
        ),
        out_specs=(stream, stream, columns, columns),
        check_vma=False,
    )
```

```python
import math

import jax
import jax.numpy as jnp
from jax import lax
from jax.experimental import pallas as pl
from jax.experimental.pallas import tpu as pltpu
from jax.sharding import PartitionSpec as P

MESH = pl.DeviceIdType.MESH
HD = 64
MAXLEN = 512
GROUP = 8
LANES = 128
NORM_EPS = 1e-05
MASKED = -1e30
STEPS = {
    "S": "first", "n": "neighbours", "c": "chain1", "C": "chain2", "x": "ends", "y": "chain3", "t": "third", "l": "last",
}
PLAN_BACK = (
    "S1", "S0", "c1", "Q2", "n1", "S3", "c0", "Q0", "S2", "C1", "Q6", "n0", "n3", "Q4", "C0", "G", "x0", "n2", "c2",
    "Kn20", "c3", "y0", "y1", "x1", "C2", "x3", "i", "Kn24", "t0", "t1", "C3", "l0", "x2", "y2", "Kx0", "H", "t2",
    "l1", "t3", "l2", "y3", "Kx1", "l3", "Kl", "I", "J",
)
PLAN = (
    "+q1", "+q0", "+u0", "S3", "0q11", "0q01", "1q11", "0u01", "1q01", "0q12", "0q02", "S2", "c3", "2q01", "1u01",
    "1q12", "0u02", "S0", "2q11", "0q03", "0q13", "+o", "+u1", "S1", "n0", "1q03", "1q13", "1u02", "c2", "2q03",
    "0o1", "1q02", "0u11", "2q12", "2u02", "0o2", "x0", "c1", "+d0", "2q13", "1o1", "P20", "0u12", "2q02", "0o3",
    "n3", "3q11", "C3", "3q12", "3u02", "3q03", "n2", "3q13", "3q02", "1o2", "t0", "3q01", "n1", "x3", "P2", "C2",
    "2u01", "1u12", "x2", "1u11", "c0", "1o3", "2o1", "0d01", "x1", "t3", "Pn", "0d02", "A002", "2o2", "2o3",
    "2u12", "A402", "C1", "3u01", "0u03", "t1", "3u12", "C0", "t2", "Pt", "0u13", "0d03", "1d01", "2u11", "y3",
    "y1", "+d1", "1u03", "y0", "y2", "Ps", "l1", "3o1", "1d02", "A424", "l3", "1d03", "A024", "0d11", "3o2", "1u13",
    "2d02", "l0", "2d01", "3u11", "2u03", "l2", "Pl", "3o3", "0d12", "1d11", "A045", "2u13", "A445", "0d13", "1d12",
    "3u13", "2d03", "M", "U0", "2d11", "U2", "1d13", "U1", "3u03", "3d01", "3d02", "2d12", "U3", "3d11", "3d03",
    "2d13", "D1", "D0", "3d12", "D2", "3d13", "D3",
)
F32 = jnp.float32
BF16 = jnp.bfloat16


def dot(left, right):
    return lax.dot_general(left, right, (((1,), (0,)), ((), ())), preferred_element_type=F32)


def dot_nt(left, right):
    return lax.dot_general(left, right, (((1,), (1,)), ((), ())), preferred_element_type=F32)


def tile(n):
    return pl.ds(pl.multiple_of(n * 256, 256), 256)


def layer_kernel(
    n_dp,
    x_in, cot_in, wq_in, wk_in, wv_in, wo_in, wup_in, wdn_in,
    len_in, qd_in, vd_in, qu_in, vu_in, qb_in, vb_in, ub_in, *rest
):
    small_from = (len_in, qd_in, vd_in, qu_in, vu_in, qb_in, vb_in, ub_in, *rest[:6])
    rest = rest[6:]
    (
        out_ref, dx_ref, lora_ref,
        wqkv, wo, wup, wdn, small, lora_q, lora_v, vec_in, down_in,
        xwin, uwin, qwin, kwin, vwin, dowin, stwin, mask, mixed,
        att, attf, stat, midb, norm1, stat1, hid, gelp, acc, gffn, gbuf, dq, dk_acc, dv_acc, dkv,
        lsend, lrecv1, lrecv2,
        lsem, ssem, rsem,
        *small_to,
    ) = rest
    len_in, qd_in, vd_in, qu_in, vu_in, qb_in, vb_in, ub_in, *vec_refs = small_to
    rows = x_in.shape[0]
    width = x_in.shape[1]
    pairs = width // LANES
    dp, t = lax.axis_index("dp"), lax.axis_index("tensor")
    member = lax.rem(dp, GROUP)
    core = lax.rem(member, 2)
    yx = member // 2
    yx_x = yx + 1 - 2 * lax.rem(yx, 2)
    yx_y = yx + 2 - 4 * (yx // 2)
    yx_d = 3 - yx
    x_dev = (dp + 2 * (yx_x - yx), t)
    y_dev = (dp + 2 * (yx_y - yx), t)
    c_dev = (dp + 1 - 2 * core, t)

    def shard(a):
        first = jnp.where(t == 0, 1, t - 1)
        second = jnp.where(t == 0, 2, jnp.where(t == 3, 1, t + 1))
        third = jnp.where(t < 2, 3, 0)
        return jnp.where(a == 1, first, jnp.where(a == 2, second, third))

    barrier = pltpu.get_barrier_semaphore()
    for d in range(1, 4):
        pl.semaphore_signal(barrier, inc=1, device_id=(dp, lax.rem(t + d, 4)), device_id_type=MESH)
    for d in range(1, n_dp):
        pl.semaphore_signal(barrier, inc=1, device_id=(lax.rem(dp + d, n_dp), t), device_id_type=MESH)

    count = {"send": 0, "recv": 0, "local": 0}
    pending = {}

    def alloc(kind, n):
        first = count[kind]
        count[kind] += n
        return first

    def when(pred, fn):
        if pred is None:
            fn()
        else:
            pl.when(pred)(fn)

    def remote(src, dst, recv, dev, pred=None):
        slot = alloc("send", 1) % ssem.shape[0]
        if slot in pending:
            before, copy = pending[slot]
            when(before, copy.wait_send)
        copy = pltpu.make_async_remote_copy(
            src_ref=src, dst_ref=dst, send_sem=ssem.at[slot], recv_sem=rsem.at[recv],
            device_id=dev, device_id_type=MESH,
        )
        when(pred, copy.start)
        pending[slot] = (pred, copy)

    def arrived(dst, recv, pred=None):
        copy = pltpu.make_async_remote_copy(
            src_ref=dst, dst_ref=dst, send_sem=ssem.at[0], recv_sem=rsem.at[recv],
            device_id=(dp, t), device_id_type=MESH,
        )
        when(pred, copy.wait_recv)

    def local(src, dst):
        copy = pltpu.make_async_copy(src, dst, lsem.at[alloc("local", 1)])
        copy.start()
        return copy

    ld_small = [local(a, b) for a, b in zip(small_from, small_to)]
    ld_qkv = [
        local(w, wqkv.at[t, :, :, :, pl.ds(256 * i, 256)]) for i, w in enumerate((wq_in, wk_in, wv_in))
    ]
    ld_x = [local(x_in, xwin.at[2])]
    ld_up = [local(wup_in, wup.at[t])]
    ld_o = [local(wo_in, wo.at[t])]
    ld_dn = [local(wdn_in, wdn.at[t])]
    ld_cot = [local(cot_in, gffn)]

    def done(copies):
        while copies:
            copies.pop().wait()

    class Chunk:
        def __init__(self, ref, first, size, loads):
            self.ref, self.first, self.size, self.loads = ref, first, size, loads
            self.zr = alloc("recv", 4)
            self.xr, self.yr, self.dr, self.cr = (alloc("recv", 3) - 1 for _ in range(4))

        def region(self, s, place, lo=0, size=None):
            return self.ref.at[s, place, core, pl.ds(self.first + lo, size or self.size), :]

        def send(self):
            done(self.loads)
            own = self.region(t, yx)
            remote(own, own, self.zr + t, (dp, jnp.minimum(t + 1, 3)), t < 3)
            remote(own, own, self.zr + t, (dp, jnp.maximum(t - 1, 0)), t > 0)

        def stage0(self, a):
            s = shard(a)
            own = self.region(s, yx)
            arrived(own, self.zr + s)
            onward = jnp.where(s < t, t + 1, t - 1)
            remote(
                own, own, self.zr + s, (dp, jnp.clip(onward, 0, 3)),
                jnp.logical_and(onward >= 0, onward <= 3),
            )
            remote(own, own, self.xr + a, x_dev)
            remote(own, own, self.yr + a, y_dev)

        def stage1(self, a):
            s, half = shard(a), self.size // 2
            arrived(self.region(s, yx_x), self.xr + a)
            part = self.region(s, yx_x, 0, half)
            remote(part, part, self.dr + a, y_dev)
            arrived(self.region(s, yx_y), self.yr + a)
            part = self.region(s, yx_y, half, half)
            remote(part, part, self.dr + a, x_dev)

        def stage2(self, a):
            s = shard(a)
            arrived(self.region(s, yx_d), self.dr + a)
            four = self.ref.at[s, :, core, pl.ds(self.first, self.size), :]
            remote(four, four, self.cr + a, c_dev)

        def stage3(self, a):
            s = shard(a)
            arrived(self.ref.at[s, :, 1 - core, pl.ds(self.first, self.size), :], self.cr + a)

    upward, downward = (dp, jnp.minimum(t + 1, 3)), (dp, jnp.maximum(t - 1, 0))
    after, before = (jnp.minimum(dp + 1, n_dp - 1), t), (jnp.maximum(dp - 1, 0), t)
    not_last, not_first = dp < n_dp - 1, dp > 0

    class Exchange:
        def __init__(self, ref, first, size):
            self.ref, self.low, self.size = ref, first, size
            self.base = alloc("recv", 6)

        def at(self, slot):
            return self.ref.at[slot, pl.ds(self.low, self.size), :]

        def go(self, src, dst, dev, pred):
            remote(self.at(src), self.at(dst), self.base + dst, dev, pred)

        def get(self, slot, pred):
            arrived(self.at(slot), self.base + slot, pred)

        def first(self):
            self.go(2, 1, upward, t < 3)
            self.go(2, 3, downward, t > 0)
            self.go(2, 5, after, jnp.logical_and(t == 3, not_last))
            self.go(2, 5, before, jnp.logical_and(t == 0, not_first))

        def neighbours(self):
            self.get(1, t >= 1)
            self.get(3, t <= 2)
            self.go(1, 0, upward, t == 2)
            self.go(3, 4, downward, t == 1)

        def chain1(self):
            self.get(5, jnp.logical_and(t == 3, not_first))
            self.get(5, jnp.logical_and(t == 0, not_last))
            self.go(5, 5, downward, jnp.logical_and(t == 3, not_first))
            self.go(5, 5, upward, jnp.logical_and(t == 0, not_last))

        def chain2(self):
            self.get(5, jnp.logical_and(t == 2, not_first))
            self.get(5, jnp.logical_and(t == 1, not_last))
            self.go(5, 0, downward, jnp.logical_and(t == 2, not_first))
            self.go(5, 4, upward, jnp.logical_and(t == 1, not_last))
            self.go(1, 0, upward, t == 1)
            self.go(3, 4, downward, t == 2)

        def ends(self):
            self.get(4, t == 0)
            self.get(0, t == 3)
            self.go(4, 0, after, jnp.logical_and(t == 0, not_last))
            self.go(0, 4, before, jnp.logical_and(t == 3, not_first))

        def chain3(self):
            self.get(0, jnp.logical_and(t == 1, not_first))
            self.get(4, jnp.logical_and(t == 2, not_last))
            self.go(0, 1, downward, jnp.logical_and(t == 1, not_first))
            self.go(4, 3, upward, jnp.logical_and(t == 2, not_last))

        def third(self):
            self.get(0, jnp.logical_and(t == 0, not_first))
            self.get(4, jnp.logical_and(t == 3, not_last))

        def last(self):
            self.get(1, jnp.logical_and(t == 0, not_first))
            self.get(3, jnp.logical_and(t == 3, not_last))
            self.get(4, t == 1)
            self.get(0, t == 2)

    lane = lax.broadcasted_iota(jnp.int32, (1, LANES), 1)
    first_half = lane < HD

    def vec(i):
        return vec_in[i : i + 1, :]

    def halves(block):
        zero = jnp.zeros_like(block)
        return jnp.where(first_half, block, zero), jnp.where(first_half, zero, block)

    def clear(ref):
        def fill(pred, slot):
            @pl.when(pred)
            def _():
                ref[slot] = jnp.zeros(ref.shape[1:], ref.dtype)

        fill(jnp.logical_and(dp == 0, t <= 1), 0)
        fill(jnp.logical_and(dp == 0, t == 0), 1)
        fill(jnp.logical_and(dp == n_dp - 1, t >= 2), 4)
        fill(jnp.logical_and(dp == n_dp - 1, t == 3), 3)

    def adapter(w, pos):
        uwin[tile(pos)] = dot_nt(xwin[w], down_in[...]).astype(BF16)

    def proj(w, pos, s):
        y = dot(xwin[w], wqkv[s].reshape(width, 3 * 256))
        u = uwin[tile(pos), 0:LANES]
        place = (tile(pos), tile(s))
        q = y[:, :256] + dot(u, lora_q[s]) + small[s, 16:17, :]
        qwin[place] = (q * (1.0 / math.sqrt(HD))).astype(BF16)
        kwin[place] = y[:, 256:512].astype(BF16)
        v = y[:, 512:] + dot(u, lora_v[s]) + small[s, 17:18, :]
        vwin[place] = v.astype(BF16)

    def proj_all(w, pos):
        adapter(w, pos)

        @pl.loop(0, 4)
        def _(s):
            proj(w, pos, s)

    def loop_pairs(lo, hi, body, unroll=1):
        @pl.loop(lo, hi, unroll=unroll)
        def _(p):
            body(p, pl.ds(pl.multiple_of(p * LANES, LANES), LANES))

    def column(index):
        return jnp.sum(jnp.where(lane == index, stat[...], 0.0), axis=1, keepdims=True)

    def attend(lo, hi):
        begin, end = lo * 256, hi * 256

        def body(p, cols):
            q_heads = halves(qwin[tile(1), cols])
            k = kwin[begin:end, cols]
            v = jnp.concatenate([vwin[begin:end, cols], uwin[begin:end, LANES:]], axis=1)
            before, outs, found, inputs = attf[:, cols], [], stat[...], mixed[...]
            for i in range(2):
                s = dot_nt(q_heads[i], k) + mask[:, begin:end]
                top = jnp.max(s, axis=1, keepdims=True)
                if lo:
                    old = column(2 * p + i)
                    top = jnp.maximum(top, old)
                e = jnp.exp(s - top)
                total = jnp.sum(e, axis=1, keepdims=True)
                o = dot(e.astype(BF16), v)
                o, extra = o[:, :LANES], o[:, LANES:]
                if lo:
                    alpha = jnp.exp(old - top)
                    total = total + column(16 + 2 * p + i) * alpha
                    o = o + before * alpha
                    extra = extra + inputs * alpha
                if hi == 5:
                    o = o * (1.0 / total)
                    extra = extra * (1.0 / total)
                    top = top + jnp.log(total)
                outs.append(o)
                inputs = jnp.where(lane // 8 == 2 * p + i, extra, inputs)
                found = jnp.where(lane == 2 * p + i, top, jnp.where(lane == 16 + 2 * p + i, total, found))
            o = jnp.where(first_half, outs[0], outs[1])
            attf[:, cols] = o
            if hi == 5:
                att[:, cols] = o.astype(BF16)
            stat[...] = found
            mixed[...] = inputs

        return body

    def after_attention():
        @pl.loop(0, 4, unroll=4)
        def _(n):
            acc[:, tile(n)] = dot(att[...], wo[:, :, :, :, tile(n)].reshape(width, 256))

        z = xwin[2].astype(F32) + acc[...] + vec(0)
        centre = z - jnp.mean(z, axis=1, keepdims=True)
        r = lax.rsqrt(jnp.mean(centre * centre, axis=1, keepdims=True) + NORM_EPS)
        n1 = centre * r
        norm1[...] = n1
        stat1[...] = jnp.broadcast_to(r, stat1.shape)
        m = n1 * vec(1) + vec(2)
        midb[...] = m.astype(BF16)
        acc[...] = m + vec(3)

    def up(s):
        @pl.loop(0, 4, unroll=4)
        def _(n):
            b = dot(midb[...], wup[s, :, :, :, tile(n)].reshape(width, 256)) + small[s, pl.ds(18 + n, 1), :]
            cdf = 0.5 + 0.5 * lax.erf(b * (1.0 / math.sqrt(2.0)))
            hid[s, :, tile(n)] = (b * cdf).astype(BF16)
            gelp[s, :, tile(n)] = cdf + b * jnp.exp(-0.5 * b * b) * (1.0 / math.sqrt(2.0 * math.pi))

    def down(s):
        @pl.loop(0, 4, unroll=4)
        def _(n):
            acc[:, tile(n)] += dot(hid[s], wdn[s, :, :, :, tile(n)].reshape(width, 256))

    def second_norm():
        z = acc[...]
        centre = z - jnp.mean(z, axis=1, keepdims=True)
        r = lax.rsqrt(jnp.mean(centre * centre, axis=1, keepdims=True) + NORM_EPS)
        n2 = centre * r
        midb[...] = (n2 * vec(4) + vec(5)).astype(BF16)
        g = gffn[...].astype(F32) * vec(4)
        g = r * (g - jnp.mean(g, axis=1, keepdims=True) - n2 * jnp.mean(g * n2, axis=1, keepdims=True))
        acc[...] = g
        gffn[...] = g.astype(BF16)

    def ffn_back(s):
        @pl.loop(0, 4, unroll=4)
        def _(n):
            toward = dot_nt(gffn[...], wdn[s, n].reshape(256, width))
            gbuf[:, tile(n)] = (toward * gelp[s, :, tile(n)]).astype(BF16)

        @pl.loop(0, 4, unroll=4)
        def _(n):
            acc[:, tile(n)] += dot_nt(gbuf[...], wup[s, n].reshape(256, width))

    def first_norm_back():
        g = acc[...] * vec(1)
        n1 = norm1[...]
        g = g - jnp.mean(g, axis=1, keepdims=True) - n1 * jnp.mean(g * n1, axis=1, keepdims=True)
        g = stat1[:, 0:1] * g
        acc[...] = g
        gffn[...] = g.astype(BF16)

        @pl.loop(0, 4, unroll=4)
        def _(s):
            dowin[2, :, tile(s)] = dot_nt(gffn[...], wo[s].reshape(256, width)).astype(BF16)

        product = dowin[2].astype(F32) * attf[...]
        high = product.astype(BF16)
        low = (product - high.astype(F32)).astype(BF16)
        at_row = lax.broadcasted_iota(jnp.int32, (width, LANES), 0) // HD + 16
        at_lane = lax.broadcasted_iota(jnp.int32, (width, LANES), 1)
        pick = (at_row == at_lane).astype(F32).astype(BF16)
        delta = dot(high, pick) + dot(low, pick)
        both = jnp.where(lane < 16, stat[...], delta)
        stat[...] = both
        stwin[2] = both.T[0:32]

    def pass_queries(p, cols):
        q_heads, do_heads = halves(qwin[tile(1), cols]), halves(dowin[2, :, cols])
        k, v = kwin[:, cols], vwin[:, cols]
        parts = []
        for i in range(2):
            prob = jnp.exp(dot_nt(q_heads[i], k) + mask[...] - column(2 * p + i))
            ds = prob * (dot_nt(do_heads[i], v) - column(16 + 2 * p + i))
            parts.append(dot(ds.astype(BF16), k))
        dq[:, cols] = (jnp.where(first_half, parts[0], parts[1]) * (1.0 / math.sqrt(HD))).astype(BF16)

    def pass_keys(pieces, at, end, first=False, unroll=1):
        def joined(parts, axis):
            return parts[0] if len(parts) == 1 else jnp.concatenate(parts, axis=axis)

        windows = [slice(blocks[name][1] * rows + lo, blocks[name][1] * rows + hi) for name, lo, hi in pieces]
        few = sum(hi - lo for _, lo, hi in pieces) <= 256

        def line(index):
            return joined([stwin[blocks[name][0], pl.ds(index, 1), :][:, lo:hi] for name, lo, hi in pieces], 1)

        def products(heads, right):
            if few:
                both = dot_nt(jnp.concatenate(heads, axis=0), right)
                return both[:256], both[256:]
            return [dot_nt(head, right) for head in heads]

        def body(p, cols):
            k_heads, v_heads = halves(kwin[tile(1), cols]), halves(vwin[tile(1), cols])
            q = joined([qwin[window, cols] for window in windows], 0)
            do = joined([dowin[blocks[name][0], lo:hi, cols] for name, lo, hi in pieces], 0)
            scores = products(k_heads, q)
            grads = products(v_heads, do)
            apart = joined([mask[:, window] for window in windows], 1)
            probs, ds = [], []
            for i in range(2):
                prob = jnp.exp(scores[i] + apart - line(2 * p + i))
                ds.append((prob * (grads[i] - line(16 + 2 * p + i))).astype(BF16))
                probs.append(prob.astype(BF16))
            for total, lefts, right in ((dk_acc, ds, q), (dv_acc, probs, do)):
                if few:
                    both = dot(jnp.concatenate(lefts, axis=0), right)
                    both = jnp.where(first_half, both[:256], both[256:])
                else:
                    both = jnp.where(first_half, dot(lefts[0], right), dot(lefts[1], right))
                total[:, cols] = both if first else total[:, cols] + both

        loop_pairs(at, end, body, unroll)

    def lora_partial():
        u = uwin[tile(1), 0:LANES].astype(F32).T[0:16].astype(BF16)
        of_queries = dot(u, dq[...])
        each = dot(mixed[...].T.astype(BF16), dowin[2])
        row_head = lax.broadcasted_iota(jnp.int32, each.shape, 0) // 8
        column_head = lax.broadcasted_iota(jnp.int32, each.shape, 1) // HD
        each = jnp.where(row_head == column_head, each, 0.0)
        of_values = each[0:8]
        for h in range(1, 16):
            of_values = of_values + each[8 * h : 8 * h + 8]
        both = jnp.concatenate([of_queries[0:8], of_values], axis=0)
        for s in range(4):
            lsend[s] = both[:, 256 * s : 256 * s + 256]

    def query_gradient():
        gu = jnp.zeros((rows, LANES), F32)
        for s in range(4):
            gu = gu + dot_nt(dq[:, 256 * s : 256 * s + 256], lora_q[s])
        stat1[...] = gu

        @pl.loop(0, 4, unroll=4)
        def _(n):
            total = acc[:, tile(n)]
            for s in range(4):
                weight = wqkv[s, n, :, :, 0:256].reshape(256, 256)
                total = total + dot_nt(dq[:, 256 * s : 256 * s + 256], weight)
            acc[:, tile(n)] = total

    def input_gradient():
        gu = stat1[...]
        for s in range(4):
            gu = gu + dot_nt(dkv[1, :, 256 * s : 256 * s + 256], lora_v[s])
        gu = gu.astype(BF16)

        @pl.loop(0, 4, unroll=4)
        def _(n):
            total = acc[:, tile(n)] + dot(gu, down_in[0:LANES, tile(n)])
            for s in range(4):
                cols = slice(256 * s, 256 * s + 256)
                two = jnp.concatenate([dkv[0, :, cols], dkv[1, :, cols]], axis=1)
                total = total + dot_nt(two, wqkv[s, n, :, :, 256:].reshape(256, 512))
            att[:, tile(n)] = total.astype(BF16)

    def chunk(ref, first, size, loads):
        return Chunk(ref, first, size, loads)

    qkv0, qkv1 = chunk(wqkv, 0, 64, ld_qkv), chunk(wqkv, 64, 64, ld_qkv)
    up0, up1 = chunk(wup, 0, 64, ld_up), chunk(wup, 64, 64, ld_up)
    dn0, dn1 = chunk(wdn, 0, 64, ld_dn), chunk(wdn, 64, 64, ld_dn)
    o0 = chunk(wo, 0, 32, ld_o)
    half, quarter = rows // 2, rows // 4
    tok = [Exchange(xwin, i * quarter, quarter) for i in range(4)]
    small_base = alloc("recv", 4)
    wide = [Exchange(dowin, i * quarter, quarter) for i in range(4)]
    narrow = Exchange(stwin, 0, 32)
    lora1 = alloc("recv", 4)
    lora2 = alloc("recv", n_dp)

    clear(xwin)
    done(ld_small)
    for i in range(8):
        cols = slice(LANES * i, LANES * i + LANES)
        for j, ref in enumerate(vec_refs):
            vec_in[j : j + 1, cols] = ref[i : i + 1, :].astype(F32)
    own_small = [2.0 * qu_in[...].astype(F32), 2.0 * vu_in[...].astype(F32)]
    small[t, 0:8, :] = own_small[0]
    small[t, 8:16, :] = own_small[1]
    for i in range(2):
        cols = slice(LANES * i, LANES * i + LANES)
        small[t, 16:17, cols] = qb_in[i : i + 1, :].astype(F32)
        small[t, 17:18, cols] = vb_in[i : i + 1, :].astype(F32)
        for j in range(4):
            small[t, 18 + j : 19 + j, cols] = ub_in[2 * j + i : 2 * j + i + 1, :].astype(F32)
    small[t, 22:24, :] = jnp.zeros((2, 256), F32)
    value_map = vd_in[...].astype(F32)
    maps = [qd_in[...].astype(F32), value_map, jnp.zeros((LANES - 16, width), F32)] + [value_map] * 16
    down_in[...] = jnp.concatenate(maps, axis=0).astype(BF16)
    pl.semaphore_wait(barrier, 3 + n_dp - 1)
    done(ld_x)
    for d in range(1, 4):
        remote(small.at[t], small.at[t], small_base + t, (dp, lax.rem(t + d, 4)))

    near = jnp.where(t < 3, 3, 1)
    second = jnp.where(lax.rem(t, 2) == 0, 4, 0)
    third = jnp.where(t == 0, 0, jnp.where(t == 3, 4, 1))
    final = jnp.where(t == 0, 1, jnp.where(t == 1, 4, jnp.where(t == 2, 0, 3)))
    blocks = {"n": (near, 0), "2": (2, 1), "s": (second, 2), "t": (third, 3), "l": (final, 4)}
    named = {"q0": qkv0, "q1": qkv1, "u0": up0, "u1": up1, "d0": dn0, "d1": dn1, "o": o0}
    def setup():
        lengths = len_in[...]
        docs = lengths.shape[0] * LANES
        high, low = lengths // 256, lax.rem(lengths, 256)
        upto = (
            lax.broadcasted_iota(jnp.int32, (LANES, LANES), 0)
            <= lax.broadcasted_iota(jnp.int32, (LANES, LANES), 1)
        ).astype(F32).astype(BF16)

        def summed(part):
            return dot(part.astype(F32).astype(BF16), upto)

        ends = 256.0 * summed(high) + summed(low)
        window = mask.shape[1]
        first = (dp * 4 + t) * rows - MAXLEN
        spot = lax.broadcasted_iota(jnp.int32, (1, window), 1)
        place = spot // rows
        where = place
        for slot, nth_place in blocks.values():
            where = jnp.where(place == nth_place, slot, where)
        position = first + where * rows + lax.rem(spot, rows)
        at = position.astype(F32)
        passed = jnp.zeros((1, window), F32)
        before = jnp.zeros((1, 1), F32)
        for r in range(lengths.shape[0]):
            end = ends[r : r + 1, :] + before
            before = end[:, LANES - 1 :]
            column = jnp.broadcast_to(end, (LANES, LANES)).T[:, 0:1]
            passed = passed + jnp.sum((column <= at).astype(F32), axis=0, keepdims=True)
        inside = jnp.logical_and(position >= 0, passed < docs)
        ids = jnp.where(inside, passed, -1.0)
        own = jnp.broadcast_to(ids[:, rows : 2 * rows], (LANES, rows)).T[:, 0:1]
        mask[...] = jnp.where(own == ids, 0.0, MASKED)
        stat[...] = jnp.zeros(stat.shape, F32)

    def small_ready():
        for d in range(1, 4):
            peer = lax.rem(t + d, 4)
            arrived(small.at[peer], small_base + peer)
        none = jnp.zeros((8, 256), F32)
        lora_q[:, 16:, :] = jnp.zeros((4, LANES - 16, 256), BF16)
        lora_v[:, 16:, :] = jnp.zeros((4, LANES - 16, 256), BF16)
        for s in range(4):
            lora_q[s, 0:16, :] = jnp.concatenate([small[s, 0:8, :], none], axis=0).astype(BF16)
            lora_v[s, 0:16, :] = jnp.concatenate([none, small[s, 8:16, :]], axis=0).astype(BF16)


    def part(a):
        return t if a == 0 else shard(a)

    for item in PLAN:
        kind, rest = item[0], item[1:]
        if kind == "+":
            named[rest].send()
        elif kind in "0123":
            getattr(named[rest[:-1]], "stage" + kind)(int(rest[-1]))
        elif kind in STEPS:
            getattr(tok[int(rest)], STEPS[kind])()
        elif item == "P20":
            setup()
            small_ready()
            adapter(2, 1)
            done(ld_qkv)
            proj(2, 1, t)
        elif item == "P2":

            @pl.loop(1, 4)
            def _(a):
                proj(2, 1, shard(a))

        elif kind == "P":
            proj_all(*blocks[rest])
        elif kind == "A":
            at, lo, hi = (int(i) for i in rest)
            loop_pairs(at, at + 4, attend(lo, hi))
        elif kind == "M":
            done(ld_o)
            after_attention()
        elif kind == "U":
            done(ld_up)
            up(part(int(rest)))
        elif kind == "D":
            done(ld_dn)
            down(part(int(rest)))
    for copies in (ld_qkv, ld_o, ld_up, ld_dn):
        done(copies)

    done(ld_cot)
    second_norm()
    out_copy = local(midb, out_ref)
    clear(dowin)
    clear(stwin)

    @pl.loop(0, 4)
    def _(s):
        ffn_back(s)

    first_norm_back()

    def swap(step, i):
        for e in [wide[i]] + ([narrow] if i == 0 else []):
            getattr(e, step)()

    for item in PLAN_BACK:
        kind, rest = item[0], item[1:]
        if kind in STEPS:
            swap(STEPS[kind], int(rest))
        elif kind == "Q":
            loop_pairs(int(rest), int(rest) + 2, pass_queries)
        elif kind == "K":
            if rest[0] == "x":
                lo = int(rest[1]) * half
                pass_keys([("s", lo, lo + half), ("t", lo, lo + half)], 0, pairs, unroll=2)
            elif rest[0] == "l":
                pass_keys([("l", 0, rows)], 0, pairs, unroll=2)
            else:
                at = int(rest[2])
                pass_keys([("n", 0, rows), ("2", 0, rows)], at, at + 4, first=True)
        elif kind == "G":
            lora_partial()
            for d in range(1, 4):
                peer = lax.rem(t + d, 4)
                remote(lsend.at[peer], lrecv1.at[t], lora1 + t, (dp, peer))
            lrecv1[t] = lsend[t]
        elif kind == "H":
            for d in range(1, 4):
                peer = lax.rem(t + d, 4)
                arrived(lrecv1.at[peer], lora1 + peer)
            lrecv2[dp] = 2.0 * ((lrecv1[0] + lrecv1[1]) + (lrecv1[2] + lrecv1[3]))
            for d in range(1, n_dp):
                remote(lrecv2.at[dp], lrecv2.at[dp], lora2 + dp, (lax.rem(dp + d, n_dp), t))
        elif kind == "i":
            query_gradient()
        elif kind == "I":
            dkv[0] = dk_acc[...].astype(BF16)
            dkv[1] = dv_acc[...].astype(BF16)
            input_gradient()
    dx_copy = local(att, dx_ref)
    for d in range(1, n_dp):
        peer = lax.rem(dp + d, n_dp)
        arrived(lrecv2.at[peer], lora2 + peer)
    total = lrecv2[0]
    for i in range(1, n_dp):
        total = total + lrecv2[i]
    lora_ref[...] = total
    dx_copy.wait()
    out_copy.wait()
    for pred, copy in pending.values():
        when(pred, copy.wait_send)
    assert count["recv"] <= rsem.shape[0] and count["local"] <= lsem.shape[0]


def hand_over(out, grad, lora, out_to, grad_to, query_to, value_to, out_at, grad_at, lora_at, sems):
    rows = out.shape[0] // 2
    halves = [pl.ds(i * rows, rows) for i in range(2)]
    loads = [(lora, lora_at)]
    stores = [[(lora_at.at[0:8], query_to), (lora_at.at[8:16], value_to)]]
    for source, at, to in ((out, out_at, out_to), (grad, grad_at, grad_to)):
        for half in halves:
            loads.append((source.at[half], at.at[half]))
            stores.append([(at.at[half], to.at[half])])
    copies = [pltpu.make_async_copy(a, b, sems.at[i]) for i, (a, b) in enumerate(loads)]
    for copy in copies:
        copy.start()
    moved = []
    for copy, pairs in zip(copies, stores):
        copy.wait()
        for a, b in pairs:
            moved.append(pltpu.make_async_copy(a, b, sems.at[len(copies) + len(moved)]))
            moved[-1].start()
    for copy in moved:
        copy.wait()


def shards(
    tokens, document_lengths, query_proj_weight, query_proj_bias, key_proj_weight, value_proj_weight,
    value_proj_bias, query_adapter_down, value_adapter_down, query_adapter_up, value_adapter_up,
    attention_out_weight, attention_out_bias, attention_norm_gain, attention_norm_bias, up_proj_weight,
    up_proj_bias, down_proj_weight, down_proj_bias, feedforward_norm_gain, feedforward_norm_bias, cotangent,
):
    rows, width = tokens.shape
    n_dp = lax.axis_size("dp")
    window = rows + 2 * MAXLEN

    def fold(vector):
        return vector.reshape(vector.shape[0] // LANES, LANES)

    def cut(weight):
        return weight.reshape(4, 2, weight.shape[0] // GROUP, weight.shape[1])

    def vmem(shape, dtype):
        return pltpu.VMEM(shape, dtype)

    small_arrays = (
        fold(document_lengths), query_adapter_down.T, value_adapter_down.T, query_adapter_up, value_adapter_up,
        fold(query_proj_bias), fold(value_proj_bias), fold(up_proj_bias), fold(attention_out_bias),
        fold(attention_norm_gain), fold(attention_norm_bias), fold(down_proj_bias), fold(feedforward_norm_gain),
        fold(feedforward_norm_bias),
    )
    any_spec = pl.BlockSpec(memory_space=pl.ANY)
    vmem_spec = pl.BlockSpec(memory_space=pltpu.VMEM)
    full = (rows, width)
    rank = query_adapter_up.shape[0]
    call = pl.pallas_call(
        lambda *refs: layer_kernel(n_dp, *refs),
        out_shape=(
            jax.ShapeDtypeStruct(full, BF16),
            jax.ShapeDtypeStruct(full, BF16),
            jax.ShapeDtypeStruct((16, 256), F32),
        ),
        in_specs=[any_spec] * 22,
        out_specs=(any_spec, any_spec, vmem_spec),
        scratch_shapes=[
            vmem((4, 4, 2, 128, 768), BF16),
            vmem((4, 4, 2, 32, 1024), BF16),
            vmem((4, 4, 2, 128, 1024), BF16),
            vmem((4, 4, 2, 128, 1024), BF16),
            vmem((4, 24, 256), F32),
            vmem((4, 128, 256), BF16),
            vmem((4, 128, 256), BF16),
            vmem((8, width), F32),
            vmem((2 * LANES, width), BF16),
            vmem((6, rows, width), BF16),
            vmem((window, 2 * LANES), BF16),
            vmem((window, width), BF16),
            vmem((window, width), BF16),
            vmem((window, width), BF16),
            vmem((6, rows, width), BF16),
            vmem((6, 32, rows), F32),
            vmem((rows, window), F32),
            vmem((rows, LANES), F32),
            vmem(full, BF16),
            vmem(full, F32),
            vmem((rows, LANES), F32),
            vmem(full, BF16),
            vmem(full, F32),
            vmem((rows, LANES), F32),
            vmem((4, rows, width), BF16),
            vmem((4, rows, width), F32),
            vmem(full, F32),
            vmem(full, BF16),
            vmem(full, BF16),
            vmem(full, BF16),
            vmem(full, F32),
            vmem(full, F32),
            vmem((2, rows, width), BF16),
            vmem((4, 16, 256), F32),
            vmem((4, 16, 256), F32),
            vmem((n_dp, 16, 256), F32),
            pltpu.SemaphoreType.DMA((26,)),
            pltpu.SemaphoreType.DMA((48,)),
            pltpu.SemaphoreType.DMA((174 + n_dp,)),
        ]
        + [vmem(a.shape, a.dtype) for a in small_arrays],
        compiler_params=pltpu.CompilerParams(
            collective_id=0, has_side_effects=True, vmem_limit_bytes=63 * 2**20
        ),
        name="layer",
    )
    out, grad, lora = call(
        tokens, cotangent, cut(query_proj_weight), cut(key_proj_weight), cut(value_proj_weight),
        cut(attention_out_weight), cut(up_proj_weight), cut(down_proj_weight), *small_arrays,
    )
    lora_shape = jax.ShapeDtypeStruct((rank, 256), F32)
    return pl.pallas_call(
        hand_over,
        out_shape=(out, grad, lora_shape, lora_shape),
        in_specs=[any_spec] * 3,
        out_specs=(any_spec,) * 4,
        scratch_shapes=[
            vmem(full, BF16), vmem(full, BF16), vmem((2 * rank, 256), F32), pltpu.SemaphoreType.DMA((11,))
        ],
        name="hand_over",
    )(out, grad, lora)


def solution(mesh):
    whole, columns = P(), P(None, "tensor")
    stream = P(("dp", "tensor"), None)
    return jax.shard_map(
        shards,
        mesh=mesh,
        in_specs=(
            stream, whole, columns, P("tensor"), columns, columns, P("tensor"), whole, whole, columns, columns,
            P("tensor", None), whole, whole, whole, columns, P("tensor"), P("tensor", None), whole, whole, whole,
            stream,
        ),
        out_specs=(stream, stream, columns, columns),
        check_vma=False,
    )
```

```python
import math

import jax
import jax.numpy as jnp
from jax import lax
from jax.experimental import pallas as pl
from jax.experimental.pallas import tpu as pltpu
from jax.sharding import PartitionSpec as P

MESH = pl.DeviceIdType.MESH
HD = 64
MAXLEN = 512
GROUP = 8
LANES = 128
NORM_EPS = 1e-05
MASKED = -1e30
STEPS = {
    "S": "first", "n": "neighbours", "c": "chain1", "C": "chain2", "x": "ends", "y": "chain3", "t": "third", "l": "last",
}
PLAN_BACK = (
    "S1", "T", "c1", "S0", "Q6", "S2", "n1", "c0", "Q4", "S3", "Q0", "x1", "C1", "c2", "n0", "Q2", "G", "c3", "x0",
    "n2", "C0", "n3", "Kn20", "y1", "i", "x3", "t0", "C2", "y0", "H", "Kn24", "t3", "l1", "C3", "t1", "y2", "x2",
    "Kx0", "l2", "y3", "t2", "Kx1", "l3", "l0", "J", "Kl", "I",
)
PLAN = (
    "+q1", "+q0", "+u0", "S3", "Z", "0q11", "0q01", "1q11", "0u01", "1q01", "0q12", "0q02", "S2", "c3", "2q01",
    "1u01", "0u02", "1q12", "S0", "2q11", "0q03", "0q13", "+o", "+u1", "S1", "n0", "1q03", "1q13", "1u02", "c2",
    "2q03", "0o1", "1q02", "0u11", "2q12", "2u02", "0o2", "x0", "c1", "+d0", "2q13", "1o1", "P0", "0u12", "2q02",
    "0o3", "n3", "3q11", "C3", "3q12", "3u02", "3q03", "n2", "3q13", "2u01", "3q02", "1o2", "t0", "3q01", "n1",
    "x3", "C2", "1u12", "x2", "1u11", "Pn", "c0", "1o3", "2o1", "0d01", "x1", "t3", "0d02", "A002", "2o2", "2o3",
    "2u12", "A402", "C1", "3u01", "0u03", "t1", "3u12", "C0", "t2", "0u13", "0d03", "1d01", "2u11", "y3", "y1",
    "+d1", "1u03", "y0", "y2", "Ps", "l1", "3o1", "1d02", "A424", "l3", "0d11", "1d03", "A024", "3o2", "1u13",
    "2d02", "l0", "2d01", "3u11", "2u03", "l2", "Pl", "3o3", "0d12", "1d11", "A045", "2u13", "A445", "0d13", "M",
    "1d12", "3u13", "2d03", "U0", "2d11", "U2", "1d13", "U1", "3u03", "3d01", "3d02", "2d12", "U3", "3d11", "3d03",
    "2d13", "D1", "D0", "3d12", "D2", "3d13", "D3",
)
F32 = jnp.float32
BF16 = jnp.bfloat16


def dot(left, right):
    return lax.dot_general(left, right, (((1,), (0,)), ((), ())), preferred_element_type=F32)


def dot_nt(left, right):
    return lax.dot_general(left, right, (((1,), (1,)), ((), ())), preferred_element_type=F32)


def tile(n):
    return pl.ds(pl.multiple_of(n * 256, 256), 256)


def layer_kernel(
    n_dp,
    x_in, cot_in, wq_in, wk_in, wv_in, wo_in, wup_in, wdn_in,
    len_in, qd_in, vd_in, qu_in, vu_in, qb_in, vb_in, ub_in, *rest
):
    small_from = (len_in, qd_in, vd_in, qu_in, vu_in, qb_in, vb_in, ub_in, *rest[:6])
    rest = rest[6:]
    (
        out_ref, dx_ref, lora_ref,
        wqkv, wo, wup, wdn, small, lora_q, lora_v, vec_in, down_in,
        xwin, uwin, qwin, kwin, vwin, dowin, stwin, mask, mixed,
        att, attf, stat, midb, norm1, stat1, hid, gelp, acc, gffn, gbuf, dq, dk_acc, dv_acc, dkv,
        lsend, lrecv1, lrecv2,
        lsem, ssem, rsem,
        *small_to,
    ) = rest
    len_in, qd_in, vd_in, qu_in, vu_in, qb_in, vb_in, ub_in, *vec_refs = small_to
    rows = x_in.shape[0]
    width = x_in.shape[1]
    pairs = width // LANES
    dp, t = lax.axis_index("dp"), lax.axis_index("tensor")
    member = lax.rem(dp, GROUP)
    core = lax.rem(member, 2)
    yx = member // 2
    yx_x = yx + 1 - 2 * lax.rem(yx, 2)
    yx_y = yx + 2 - 4 * (yx // 2)
    yx_d = 3 - yx
    x_dev = (dp + 2 * (yx_x - yx), t)
    y_dev = (dp + 2 * (yx_y - yx), t)
    c_dev = (dp + 1 - 2 * core, t)

    def shard(a):
        first = jnp.where(t == 0, 1, t - 1)
        second = jnp.where(t == 0, 2, jnp.where(t == 3, 1, t + 1))
        third = jnp.where(t < 2, 3, 0)
        return jnp.where(a == 1, first, jnp.where(a == 2, second, third))

    barrier = pltpu.get_barrier_semaphore()
    for d in range(1, 4):
        pl.semaphore_signal(barrier, inc=1, device_id=(dp, lax.rem(t + d, 4)), device_id_type=MESH)
    for d in range(1, n_dp):
        pl.semaphore_signal(barrier, inc=1, device_id=(lax.rem(dp + d, n_dp), t), device_id_type=MESH)

    count = {"send": 0, "recv": 0, "local": 0}
    pending = {}

    def alloc(kind, n):
        first = count[kind]
        count[kind] += n
        return first

    def when(pred, fn):
        if pred is None:
            fn()
        else:
            pl.when(pred)(fn)

    def remote(src, dst, recv, dev, pred=None):
        slot = alloc("send", 1) % ssem.shape[0]
        if slot in pending:
            before, copy = pending[slot]
            when(before, copy.wait_send)
        copy = pltpu.make_async_remote_copy(
            src_ref=src, dst_ref=dst, send_sem=ssem.at[slot], recv_sem=rsem.at[recv],
            device_id=dev, device_id_type=MESH,
        )
        when(pred, copy.start)
        pending[slot] = (pred, copy)

    def arrived(dst, recv, pred=None):
        copy = pltpu.make_async_remote_copy(
            src_ref=dst, dst_ref=dst, send_sem=ssem.at[0], recv_sem=rsem.at[recv],
            device_id=(dp, t), device_id_type=MESH,
        )
        when(pred, copy.wait_recv)

    def settle():
        for pred, copy in pending.values():
            when(pred, copy.wait_send)
        pending.clear()

    def local(src, dst):
        copy = pltpu.make_async_copy(src, dst, lsem.at[alloc("local", 1)])
        copy.start()
        return copy

    ld_small = [local(a, b) for a, b in zip(small_from, small_to)]
    ld_qkv = [
        local(w, wqkv.at[t, :, :, :, pl.ds(256 * i, 256)]) for i, w in enumerate((wq_in, wk_in, wv_in))
    ]
    ld_x = [local(x_in, xwin.at[2])]
    ld_up = [local(wup_in, wup.at[t])]
    ld_o = [local(wo_in, wo.at[t])]
    ld_dn = [local(wdn_in, wdn.at[t])]
    ld_cot = [local(cot_in, gffn)]

    def done(copies):
        while copies:
            copies.pop().wait()

    class Chunk:
        def __init__(self, ref, first, size, loads, by_y=None):
            self.ref, self.first, self.size, self.loads = ref, first, size, loads
            self.by_y = by_y or size // 2
            self.zr = alloc("recv", 4)
            self.xr, self.yr, self.dr, self.cr = (alloc("recv", 3) - 1 for _ in range(4))

        def region(self, s, place, lo=0, size=None):
            return self.ref.at[s, place, core, pl.ds(self.first + lo, size or self.size), :]

        def send(self):
            done(self.loads)
            own = self.region(t, yx)
            remote(own, own, self.zr + t, (dp, jnp.minimum(t + 1, 3)), t < 3)
            remote(own, own, self.zr + t, (dp, jnp.maximum(t - 1, 0)), t > 0)

        def stage0(self, a):
            s = shard(a)
            own = self.region(s, yx)
            arrived(own, self.zr + s)
            onward = jnp.where(s < t, t + 1, t - 1)
            remote(
                own, own, self.zr + s, (dp, jnp.clip(onward, 0, 3)),
                jnp.logical_and(onward >= 0, onward <= 3),
            )
            remote(own, own, self.xr + a, x_dev)
            remote(own, own, self.yr + a, y_dev)

        def stage1(self, a):
            s = shard(a)
            arrived(self.region(s, yx_x), self.xr + a)
            part = self.region(s, yx_x, 0, self.by_y)
            remote(part, part, self.dr + a, y_dev)
            arrived(self.region(s, yx_y), self.yr + a)
            part = self.region(s, yx_y, self.by_y, self.size - self.by_y)
            remote(part, part, self.dr + a, x_dev)

        def stage2(self, a):
            s = shard(a)
            arrived(self.region(s, yx_d), self.dr + a)
            four = self.ref.at[s, :, core, pl.ds(self.first, self.size), :]
            remote(four, four, self.cr + a, c_dev)

        def stage3(self, a):
            s = shard(a)
            arrived(self.ref.at[s, :, 1 - core, pl.ds(self.first, self.size), :], self.cr + a)

    upward, downward = (dp, jnp.minimum(t + 1, 3)), (dp, jnp.maximum(t - 1, 0))
    after, before = (jnp.minimum(dp + 1, n_dp - 1), t), (jnp.maximum(dp - 1, 0), t)
    not_last, not_first = dp < n_dp - 1, dp > 0

    class Exchange:
        def __init__(self, ref, first, size):
            self.ref, self.low, self.size = ref, first, size
            self.base = alloc("recv", 6)

        def at(self, slot):
            return self.ref.at[slot, pl.ds(self.low, self.size), :]

        def go(self, src, dst, dev, pred):
            remote(self.at(src), self.at(dst), self.base + dst, dev, pred)

        def get(self, slot, pred):
            arrived(self.at(slot), self.base + slot, pred)

        def first(self):
            self.go(2, 1, upward, t < 3)
            self.go(2, 3, downward, t > 0)
            self.go(2, 5, after, jnp.logical_and(t == 3, not_last))
            self.go(2, 5, before, jnp.logical_and(t == 0, not_first))

        def neighbours(self):
            self.get(1, t >= 1)
            self.get(3, t <= 2)
            self.go(1, 0, upward, t == 2)
            self.go(3, 4, downward, t == 1)

        def chain1(self):
            self.get(5, jnp.logical_and(t == 3, not_first))
            self.get(5, jnp.logical_and(t == 0, not_last))
            self.go(5, 5, downward, jnp.logical_and(t == 3, not_first))
            self.go(5, 5, upward, jnp.logical_and(t == 0, not_last))

        def chain2(self):
            self.get(5, jnp.logical_and(t == 2, not_first))
            self.get(5, jnp.logical_and(t == 1, not_last))
            self.go(5, 0, downward, jnp.logical_and(t == 2, not_first))
            self.go(5, 4, upward, jnp.logical_and(t == 1, not_last))
            self.go(1, 0, upward, t == 1)
            self.go(3, 4, downward, t == 2)

        def ends(self):
            self.get(4, t == 0)
            self.get(0, t == 3)
            self.go(4, 0, after, jnp.logical_and(t == 0, not_last))
            self.go(0, 4, before, jnp.logical_and(t == 3, not_first))

        def chain3(self):
            self.get(0, jnp.logical_and(t == 1, not_first))
            self.get(4, jnp.logical_and(t == 2, not_last))
            self.go(0, 1, downward, jnp.logical_and(t == 1, not_first))
            self.go(4, 3, upward, jnp.logical_and(t == 2, not_last))

        def third(self):
            self.get(0, jnp.logical_and(t == 0, not_first))
            self.get(4, jnp.logical_and(t == 3, not_last))

        def last(self):
            self.get(1, jnp.logical_and(t == 0, not_first))
            self.get(3, jnp.logical_and(t == 3, not_last))
            self.get(4, t == 1)
            self.get(0, t == 2)

    lane = lax.broadcasted_iota(jnp.int32, (1, LANES), 1)
    first_half = lane < HD

    def vec(i):
        return vec_in[i : i + 1, :]

    def halves(block):
        zero = jnp.zeros_like(block)
        return jnp.where(first_half, block, zero), jnp.where(first_half, zero, block)

    def clear(ref):
        def fill(pred, slot):
            @pl.when(pred)
            def _():
                ref[slot] = jnp.zeros(ref.shape[1:], ref.dtype)

        fill(jnp.logical_and(dp == 0, t <= 1), 0)
        fill(jnp.logical_and(dp == 0, t == 0), 1)
        fill(jnp.logical_and(dp == n_dp - 1, t >= 2), 4)
        fill(jnp.logical_and(dp == n_dp - 1, t == 3), 3)

    def project(names):
        begin = blocks[names[0]][1] * rows
        place = slice(begin, begin + len(names) * rows)

        def tokens():
            parts = [xwin[blocks[name][0]] for name in names]
            return parts[0] if len(parts) == 1 else jnp.concatenate(parts, axis=0)

        uwin[place] = dot_nt(tokens(), down_in[...]).astype(BF16)

        @pl.loop(0, 4)
        def _(s):
            y = dot(tokens(), wqkv[s].reshape(width, 3 * 256))
            u = uwin[place, 0:LANES]
            q = y[:, :256] + dot(u, lora_q[s]) + small[s, 16:17, :]
            qwin[place, tile(s)] = (q * (1.0 / math.sqrt(HD))).astype(BF16)
            kwin[place, tile(s)] = y[:, 256:512].astype(BF16)
            v = y[:, 512:] + dot(u, lora_v[s]) + small[s, 17:18, :]
            vwin[place, tile(s)] = v.astype(BF16)

    def loop_pairs(lo, hi, body, unroll=1):
        @pl.loop(lo, hi, unroll=unroll)
        def _(p):
            body(p, pl.ds(pl.multiple_of(p * LANES, LANES), LANES))

    def column(index):
        return jnp.sum(jnp.where(lane == index, stat[...], 0.0), axis=1, keepdims=True)

    def attend(lo, hi):
        begin, end = lo * 256, hi * 256

        def body(p, cols):
            q_heads = halves(qwin[tile(1), cols])
            k = kwin[begin:end, cols]
            v = jnp.concatenate([vwin[begin:end, cols], uwin[begin:end, LANES:]], axis=1)
            before, outs, found, inputs = attf[:, cols], [], stat[...], mixed[...]
            for i in range(2):
                s = dot_nt(q_heads[i], k) + mask[:, begin:end]
                top = jnp.max(s, axis=1, keepdims=True)
                if lo:
                    old = column(2 * p + i)
                    top = jnp.maximum(top, old)
                e = jnp.exp(s - top)
                total = jnp.sum(e, axis=1, keepdims=True)
                o = dot(e.astype(BF16), v)
                o, extra = o[:, :LANES], o[:, LANES:]
                if lo:
                    alpha = jnp.exp(old - top)
                    total = total + column(16 + 2 * p + i) * alpha
                    o = o + before * alpha
                    extra = extra + inputs * alpha
                if hi == 5:
                    o = o * (1.0 / total)
                    extra = extra * (1.0 / total)
                    top = top + jnp.log(total)
                outs.append(o)
                inputs = jnp.where(lane // 8 == 2 * p + i, extra, inputs)
                found = jnp.where(lane == 2 * p + i, top, jnp.where(lane == 16 + 2 * p + i, total, found))
            o = jnp.where(first_half, outs[0], outs[1])
            attf[:, cols] = o
            if hi == 5:
                att[:, cols] = o.astype(BF16)
            stat[...] = found
            mixed[...] = inputs

        return body

    def after_attention():
        @pl.loop(0, 4, unroll=4)
        def _(n):
            acc[:, tile(n)] = dot(att[...], wo[:, :, :, :, tile(n)].reshape(width, 256))

        z = xwin[2].astype(F32) + acc[...] + vec(0)
        centre = z - jnp.mean(z, axis=1, keepdims=True)
        r = lax.rsqrt(jnp.mean(centre * centre, axis=1, keepdims=True) + NORM_EPS)
        n1 = centre * r
        norm1[...] = n1
        stat1[...] = jnp.broadcast_to(r, stat1.shape)
        m = n1 * vec(1) + vec(2)
        midb[...] = m.astype(BF16)
        acc[...] = m + vec(3)

    def up(s):
        @pl.loop(0, 4, unroll=4)
        def _(n):
            b = dot(midb[...], wup[s, :, :, :, tile(n)].reshape(width, 256)) + small[s, pl.ds(18 + n, 1), :]
            cdf = 0.5 + 0.5 * lax.erf(b * (1.0 / math.sqrt(2.0)))
            hid[s, :, tile(n)] = (b * cdf).astype(BF16)
            gelp[s, :, tile(n)] = cdf + b * jnp.exp(-0.5 * b * b) * (1.0 / math.sqrt(2.0 * math.pi))

    def down(s):
        @pl.loop(0, 4, unroll=4)
        def _(n):
            acc[:, tile(n)] += dot(hid[s], wdn[s, :, :, :, tile(n)].reshape(width, 256))

    def second_norm():
        z = acc[...]
        centre = z - jnp.mean(z, axis=1, keepdims=True)
        r = lax.rsqrt(jnp.mean(centre * centre, axis=1, keepdims=True) + NORM_EPS)
        n2 = centre * r
        midb[...] = (n2 * vec(4) + vec(5)).astype(BF16)
        g = gffn[...].astype(F32) * vec(4)
        g = r * (g - jnp.mean(g, axis=1, keepdims=True) - n2 * jnp.mean(g * n2, axis=1, keepdims=True))
        acc[...] = g
        gffn[...] = g.astype(BF16)

    def ffn_back(s):
        @pl.loop(0, 4, unroll=4)
        def _(n):
            toward = dot_nt(gffn[...], wdn[s, n].reshape(256, width))
            gbuf[:, tile(n)] = (toward * gelp[s, :, tile(n)]).astype(BF16)

        @pl.loop(0, 4, unroll=4)
        def _(n):
            acc[:, tile(n)] += dot_nt(gbuf[...], wup[s, n].reshape(256, width))

    def first_norm_back():
        g = acc[...] * vec(1)
        n1 = norm1[...]
        g = g - jnp.mean(g, axis=1, keepdims=True) - n1 * jnp.mean(g * n1, axis=1, keepdims=True)
        g = stat1[:, 0:1] * g
        acc[...] = g
        gffn[...] = g.astype(BF16)

        @pl.loop(0, 4, unroll=4)
        def _(s):
            dowin[2, :, tile(s)] = dot_nt(gffn[...], wo[s].reshape(256, width)).astype(BF16)

    def statistics():
        product = dowin[2].astype(F32) * attf[...]
        high = product.astype(BF16)
        low = (product - high.astype(F32)).astype(BF16)
        at_row = lax.broadcasted_iota(jnp.int32, (width, LANES), 0) // HD + 16
        at_lane = lax.broadcasted_iota(jnp.int32, (width, LANES), 1)
        pick = (at_row == at_lane).astype(F32).astype(BF16)
        delta = dot(high, pick) + dot(low, pick)
        both = jnp.where(lane < 16, stat[...], delta)
        stat[...] = both
        stwin[2] = both.T[0:32]

    def pass_queries(p, cols):
        q_heads, do_heads = halves(qwin[tile(1), cols]), halves(dowin[2, :, cols])
        k, v = kwin[:, cols], vwin[:, cols]
        parts = []
        for i in range(2):
            prob = jnp.exp(dot_nt(q_heads[i], k) + mask[...] - column(2 * p + i))
            ds = prob * (dot_nt(do_heads[i], v) - column(16 + 2 * p + i))
            parts.append(dot(ds.astype(BF16), k))
        dq[:, cols] = (jnp.where(first_half, parts[0], parts[1]) * (1.0 / math.sqrt(HD))).astype(BF16)

    def pass_keys(pieces, at, end, first=False, unroll=1):
        def joined(parts, axis):
            return parts[0] if len(parts) == 1 else jnp.concatenate(parts, axis=axis)

        windows = [slice(blocks[name][1] * rows + lo, blocks[name][1] * rows + hi) for name, lo, hi in pieces]
        few = sum(hi - lo for _, lo, hi in pieces) <= 256

        def line(index):
            return joined([stwin[blocks[name][0], pl.ds(index, 1), :][:, lo:hi] for name, lo, hi in pieces], 1)

        def products(heads, right):
            if few:
                both = dot_nt(jnp.concatenate(heads, axis=0), right)
                return both[:256], both[256:]
            return [dot_nt(head, right) for head in heads]

        def body(p, cols):
            k_heads, v_heads = halves(kwin[tile(1), cols]), halves(vwin[tile(1), cols])
            q = joined([qwin[window, cols] for window in windows], 0)
            do = joined([dowin[blocks[name][0], lo:hi, cols] for name, lo, hi in pieces], 0)
            scores = products(k_heads, q)
            grads = products(v_heads, do)
            apart = joined([mask[:, window] for window in windows], 1)
            probs, ds = [], []
            for i in range(2):
                prob = jnp.exp(scores[i] + apart - line(2 * p + i))
                ds.append((prob * (grads[i] - line(16 + 2 * p + i))).astype(BF16))
                probs.append(prob.astype(BF16))
            for total, lefts, right in ((dk_acc, ds, q), (dv_acc, probs, do)):
                if few:
                    both = dot(jnp.concatenate(lefts, axis=0), right)
                    both = jnp.where(first_half, both[:256], both[256:])
                else:
                    both = jnp.where(first_half, dot(lefts[0], right), dot(lefts[1], right))
                total[:, cols] = both if first else total[:, cols] + both

        loop_pairs(at, end, body, unroll)

    def lora_partial():
        u = uwin[tile(1), 0:LANES].astype(F32).T[0:16].astype(BF16)
        of_queries = dot(u, dq[...])
        each = dot(mixed[...].T.astype(BF16), dowin[2])
        row_head = lax.broadcasted_iota(jnp.int32, each.shape, 0) // 8
        column_head = lax.broadcasted_iota(jnp.int32, each.shape, 1) // HD
        each = jnp.where(row_head == column_head, each, 0.0)
        of_values = each[0:8]
        for h in range(1, 16):
            of_values = of_values + each[8 * h : 8 * h + 8]
        both = jnp.concatenate([of_queries[0:8], of_values], axis=0)
        for s in range(4):
            lsend[s] = both[:, 256 * s : 256 * s + 256]

    def query_gradient():
        gu = jnp.zeros((rows, LANES), F32)
        for s in range(4):
            gu = gu + dot_nt(dq[:, 256 * s : 256 * s + 256], lora_q[s])
        stat1[...] = gu

        @pl.loop(0, 4, unroll=4)
        def _(n):
            total = acc[:, tile(n)]
            for s in range(4):
                weight = wqkv[s, n, :, :, 0:256].reshape(256, 256)
                total = total + dot_nt(dq[:, 256 * s : 256 * s + 256], weight)
            acc[:, tile(n)] = total

    def input_gradient():
        gu = stat1[...]
        for s in range(4):
            gu = gu + dot_nt(dkv[1, :, 256 * s : 256 * s + 256], lora_v[s])
        gu = gu.astype(BF16)
        for n in range(4):
            total = acc[:, tile(n)] + dot(gu, down_in[0:LANES, tile(n)])
            for s in range(4):
                cols = slice(256 * s, 256 * s + 256)
                two = jnp.concatenate([dkv[0, :, cols], dkv[1, :, cols]], axis=1)
                total = total + dot_nt(two, wqkv[s, n, :, :, 256:].reshape(256, 512))
            att[:, tile(n)] = total.astype(BF16)
            final.append(local(att.at[:, tile(n)], dx_ref.at[:, tile(n)]))

    def chunk(*args):
        return Chunk(*args)

    qkv0, qkv1 = chunk(wqkv, 0, 64, ld_qkv), chunk(wqkv, 64, 64, ld_qkv)
    up0, up1 = chunk(wup, 0, 64, ld_up), chunk(wup, 64, 64, ld_up)
    dn0, dn1 = chunk(wdn, 0, 64, ld_dn), chunk(wdn, 64, 64, ld_dn)
    o0 = chunk(wo, 0, 32, ld_o)
    half, quarter = rows // 2, rows // 4
    tok = [Exchange(xwin, i * quarter, quarter) for i in range(4)]
    small_base = alloc("recv", 4)
    wide = [Exchange(dowin, i * quarter, quarter) for i in range(4)]
    narrow = Exchange(stwin, 0, 32)
    lora1 = alloc("recv", 4)
    lora2 = alloc("recv", n_dp)

    def prepare():
        for ref in (xwin, dowin, stwin):
            clear(ref)
        done(ld_small)
        for i in range(8):
            cols = slice(LANES * i, LANES * i + LANES)
            for j, ref in enumerate(vec_refs):
                vec_in[j : j + 1, cols] = ref[i : i + 1, :].astype(F32)
        own_small = [2.0 * qu_in[...].astype(F32), 2.0 * vu_in[...].astype(F32)]
        small[t, 0:8, :] = own_small[0]
        small[t, 8:16, :] = own_small[1]
        for i in range(2):
            cols = slice(LANES * i, LANES * i + LANES)
            small[t, 16:17, cols] = qb_in[i : i + 1, :].astype(F32)
            small[t, 17:18, cols] = vb_in[i : i + 1, :].astype(F32)
            for j in range(4):
                small[t, 18 + j : 19 + j, cols] = ub_in[2 * j + i : 2 * j + i + 1, :].astype(F32)
        small[t, 22:24, :] = jnp.zeros((2, 256), F32)
        value_map = vd_in[...].astype(F32)
        maps = [qd_in[...].astype(F32), value_map, jnp.zeros((LANES - 16, width), F32)] + [value_map] * 16
        down_in[...] = jnp.concatenate(maps, axis=0).astype(BF16)
        for d in range(1, 4):
            remote(small.at[t], small.at[t], small_base + t, (dp, lax.rem(t + d, 4)))

    pl.semaphore_wait(barrier, 3 + n_dp - 1)
    near = jnp.where(t < 3, 3, 1)
    second = jnp.where(lax.rem(t, 2) == 0, 4, 0)
    third = jnp.where(t == 0, 0, jnp.where(t == 3, 4, 1))
    final = jnp.where(t == 0, 1, jnp.where(t == 1, 4, jnp.where(t == 2, 0, 3)))
    blocks = {"n": (near, 0), "2": (2, 1), "s": (second, 2), "t": (third, 3), "l": (final, 4)}
    named = {"q0": qkv0, "q1": qkv1, "u0": up0, "u1": up1, "d0": dn0, "d1": dn1, "o": o0}
    def setup():
        lengths = len_in[...]
        docs = lengths.shape[0] * LANES
        high, low = lengths // 256, lax.rem(lengths, 256)
        upto = (
            lax.broadcasted_iota(jnp.int32, (LANES, LANES), 0)
            <= lax.broadcasted_iota(jnp.int32, (LANES, LANES), 1)
        ).astype(F32).astype(BF16)

        def summed(part):
            return dot(part.astype(F32).astype(BF16), upto)

        ends = 256.0 * summed(high) + summed(low)
        window = mask.shape[1]
        first = (dp * 4 + t) * rows - MAXLEN
        spot = lax.broadcasted_iota(jnp.int32, (1, window), 1)
        place = spot // rows
        where = place
        for slot, nth_place in blocks.values():
            where = jnp.where(place == nth_place, slot, where)
        position = first + where * rows + lax.rem(spot, rows)
        at = position.astype(F32)
        passed = jnp.zeros((1, window), F32)
        before = jnp.zeros((1, 1), F32)
        for r in range(lengths.shape[0]):
            end = ends[r : r + 1, :] + before
            before = end[:, LANES - 1 :]
            column = jnp.broadcast_to(end, (LANES, LANES)).T[:, 0:1]
            passed = passed + jnp.sum((column <= at).astype(F32), axis=0, keepdims=True)
        inside = jnp.logical_and(position >= 0, passed < docs)
        ids = jnp.where(inside, passed, -1.0)
        own = jnp.broadcast_to(ids[:, rows : 2 * rows], (LANES, rows)).T[:, 0:1]
        mask[...] = jnp.where(own == ids, 0.0, MASKED)
        stat[...] = jnp.zeros(stat.shape, F32)

    def small_ready():
        for d in range(1, 4):
            peer = lax.rem(t + d, 4)
            arrived(small.at[peer], small_base + peer)
        none = jnp.zeros((8, 256), F32)
        lora_q[:, 16:, :] = jnp.zeros((4, LANES - 16, 256), BF16)
        lora_v[:, 16:, :] = jnp.zeros((4, LANES - 16, 256), BF16)
        for s in range(4):
            lora_q[s, 0:16, :] = jnp.concatenate([small[s, 0:8, :], none], axis=0).astype(BF16)
            lora_v[s, 0:16, :] = jnp.concatenate([none, small[s, 8:16, :]], axis=0).astype(BF16)


    def part(a):
        return t if a == 0 else shard(a)

    for item in PLAN:
        kind, rest = item[0], item[1:]
        if kind == "+":
            named[rest].send()
        elif kind in "0123":
            getattr(named[rest[:-1]], "stage" + kind)(int(rest[-1]))
        elif kind in STEPS:
            done(ld_x)
            getattr(tok[int(rest)], STEPS[kind])()
        elif kind == "Z":
            prepare()
        elif item == "P0":
            setup()
            small_ready()
        elif kind == "P":
            done(ld_qkv)
            project({"n": "n2", "s": "st", "l": "l"}[rest])
        elif kind == "A":
            at, lo, hi = (int(i) for i in rest)
            loop_pairs(at, at + 4, attend(lo, hi))
        elif kind == "M":
            done(ld_o)
            after_attention()
        elif kind == "U":
            done(ld_up)
            up(part(int(rest)))
        elif kind == "D":
            done(ld_dn)
            down(part(int(rest)))
    for copies in (ld_qkv, ld_o, ld_up, ld_dn):
        done(copies)

    done(ld_cot)
    second_norm()
    final = [local(midb, out_ref)]

    @pl.loop(0, 4)
    def _(s):
        ffn_back(s)

    first_norm_back()

    def swap(step, i):
        for e in [wide[i]] + ([narrow] if i == 0 else []):
            getattr(e, step)()

    for item in PLAN_BACK:
        kind, rest = item[0], item[1:]
        if item == "l3":
            settle()
        if kind in STEPS:
            swap(STEPS[kind], int(rest))
        elif kind == "T":
            statistics()
        elif kind == "Q":
            loop_pairs(int(rest), int(rest) + 2, pass_queries)
        elif kind == "K":
            if rest[0] == "x":
                lo = int(rest[1]) * half
                pass_keys([("s", lo, lo + half), ("t", lo, lo + half)], 0, pairs, unroll=2)
            elif rest[0] == "l":
                pass_keys([("l", 0, rows)], 0, pairs, unroll=2)
            else:
                at = int(rest[2])
                pass_keys([("n", 0, rows), ("2", 0, rows)], at, at + 4, first=True)
        elif kind == "G":
            lora_partial()
            for d in range(1, 4):
                peer = lax.rem(t + d, 4)
                remote(lsend.at[peer], lrecv1.at[t], lora1 + t, (dp, peer))
            lrecv1[t] = lsend[t]
        elif kind == "H":
            for d in range(1, 4):
                peer = lax.rem(t + d, 4)
                arrived(lrecv1.at[peer], lora1 + peer)
            lrecv2[dp] = 2.0 * ((lrecv1[0] + lrecv1[1]) + (lrecv1[2] + lrecv1[3]))
            for d in range(1, n_dp):
                remote(lrecv2.at[dp], lrecv2.at[dp], lora2 + dp, (lax.rem(dp + d, n_dp), t))
        elif kind == "J":
            for d in range(1, n_dp):
                peer = lax.rem(dp + d, n_dp)
                arrived(lrecv2.at[peer], lora2 + peer)
            total = lrecv2[0]
            for i in range(1, n_dp):
                total = total + lrecv2[i]
            lsend[0] = total
            final.append(local(lsend.at[0], lora_ref))
        elif kind == "i":
            query_gradient()
        elif kind == "I":
            dkv[0] = dk_acc[...].astype(BF16)
            dkv[1] = dv_acc[...].astype(BF16)
            input_gradient()
    settle()
    done(final)
    assert count["recv"] <= rsem.shape[0] and count["local"] <= lsem.shape[0]


def hand_over(out, grad, lora, out_to, grad_to, query_to, value_to, out_at, grad_at, lora_at, sems):
    rows = out.shape[0] // 4
    parts = [pl.ds(i * rows, rows) for i in range(4)]
    loads = [(lora, lora_at)]
    stores = [[(lora_at.at[0:8], query_to), (lora_at.at[8:16], value_to)]]
    for source, at, to in ((out, out_at, out_to), (grad, grad_at, grad_to)):
        for part in parts:
            loads.append((source.at[part], at.at[part]))
            stores.append([(at.at[part], to.at[part])])
    copies = [pltpu.make_async_copy(a, b, sems.at[i]) for i, (a, b) in enumerate(loads)]
    for copy in copies:
        copy.start()
    moved = []
    for copy, pairs in zip(copies, stores):
        copy.wait()
        for a, b in pairs:
            moved.append(pltpu.make_async_copy(a, b, sems.at[len(copies) + len(moved)]))
            moved[-1].start()
    for copy in moved:
        copy.wait()


def shards(
    tokens, document_lengths, query_proj_weight, query_proj_bias, key_proj_weight, value_proj_weight,
    value_proj_bias, query_adapter_down, value_adapter_down, query_adapter_up, value_adapter_up,
    attention_out_weight, attention_out_bias, attention_norm_gain, attention_norm_bias, up_proj_weight,
    up_proj_bias, down_proj_weight, down_proj_bias, feedforward_norm_gain, feedforward_norm_bias, cotangent,
):
    rows, width = tokens.shape
    n_dp = lax.axis_size("dp")
    window = rows + 2 * MAXLEN

    def fold(vector):
        return vector.reshape(vector.shape[0] // LANES, LANES)

    def cut(weight):
        return weight.reshape(4, 2, weight.shape[0] // GROUP, weight.shape[1])

    def vmem(shape, dtype):
        return pltpu.VMEM(shape, dtype)

    small_arrays = (
        fold(document_lengths), query_adapter_down.T, value_adapter_down.T, query_adapter_up, value_adapter_up,
        fold(query_proj_bias), fold(value_proj_bias), fold(up_proj_bias), fold(attention_out_bias),
        fold(attention_norm_gain), fold(attention_norm_bias), fold(down_proj_bias), fold(feedforward_norm_gain),
        fold(feedforward_norm_bias),
    )
    any_spec = pl.BlockSpec(memory_space=pl.ANY)
    vmem_spec = pl.BlockSpec(memory_space=pltpu.VMEM)
    full = (rows, width)
    rank = query_adapter_up.shape[0]
    call = pl.pallas_call(
        lambda *refs: layer_kernel(n_dp, *refs),
        out_shape=(
            jax.ShapeDtypeStruct(full, BF16),
            jax.ShapeDtypeStruct(full, BF16),
            jax.ShapeDtypeStruct((16, 256), F32),
        ),
        in_specs=[any_spec] * 22,
        out_specs=(any_spec,) * 3,
        scratch_shapes=[
            vmem((4, 4, 2, 128, 768), BF16),
            vmem((4, 4, 2, 32, 1024), BF16),
            vmem((4, 4, 2, 128, 1024), BF16),
            vmem((4, 4, 2, 128, 1024), BF16),
            vmem((4, 24, 256), F32),
            vmem((4, 128, 256), BF16),
            vmem((4, 128, 256), BF16),
            vmem((8, width), F32),
            vmem((2 * LANES, width), BF16),
            vmem((6, rows, width), BF16),
            vmem((window, 2 * LANES), BF16),
            vmem((window, width), BF16),
            vmem((window, width), BF16),
            vmem((window, width), BF16),
            vmem((6, rows, width), BF16),
            vmem((6, 32, rows), F32),
            vmem((rows, window), F32),
            vmem((rows, LANES), F32),
            vmem(full, BF16),
            vmem(full, F32),
            vmem((rows, LANES), F32),
            vmem(full, BF16),
            vmem(full, F32),
            vmem((rows, LANES), F32),
            vmem((4, rows, width), BF16),
            vmem((4, rows, width), F32),
            vmem(full, F32),
            vmem(full, BF16),
            vmem(full, BF16),
            vmem(full, BF16),
            vmem(full, F32),
            vmem(full, F32),
            vmem((2, rows, width), BF16),
            vmem((4, 16, 256), F32),
            vmem((4, 16, 256), F32),
            vmem((n_dp, 16, 256), F32),
            pltpu.SemaphoreType.DMA((30,)),
            pltpu.SemaphoreType.DMA((48,)),
            pltpu.SemaphoreType.DMA((174 + n_dp,)),
        ]
        + [vmem(a.shape, a.dtype) for a in small_arrays],
        compiler_params=pltpu.CompilerParams(
            collective_id=0, has_side_effects=True, vmem_limit_bytes=63 * 2**20
        ),
        name="layer",
    )
    out, grad, lora = call(
        tokens, cotangent, cut(query_proj_weight), cut(key_proj_weight), cut(value_proj_weight),
        cut(attention_out_weight), cut(up_proj_weight), cut(down_proj_weight), *small_arrays,
    )
    lora_shape = jax.ShapeDtypeStruct((rank, 256), F32)
    return pl.pallas_call(
        hand_over,
        out_shape=(out, grad, lora_shape, lora_shape),
        in_specs=[any_spec] * 3,
        out_specs=(any_spec,) * 4,
        scratch_shapes=[
            vmem(full, BF16), vmem(full, BF16), vmem((2 * rank, 256), F32), pltpu.SemaphoreType.DMA((19,))
        ],
        name="hand_over",
    )(out, grad, lora)


def solution(mesh):
    whole, columns = P(), P(None, "tensor")
    stream = P(("dp", "tensor"), None)
    return jax.shard_map(
        shards,
        mesh=mesh,
        in_specs=(
            stream, whole, columns, P("tensor"), columns, columns, P("tensor"), whole, whole, columns, columns,
            P("tensor", None), whole, whole, whole, columns, P("tensor"), P("tensor", None), whole, whole, whole,
            stream,
        ),
        out_specs=(stream, stream, columns, columns),
        check_vma=False,
    )
```

```python
import math

import jax
import jax.numpy as jnp
from jax import lax
from jax.experimental import pallas as pl
from jax.experimental.pallas import tpu as pltpu
from jax.sharding import PartitionSpec as P

MESH = pl.DeviceIdType.MESH
HD = 64
MAXLEN = 512
GROUP = 8
LANES = 128
NORM_EPS = 1e-05
MASKED = -1e30
STEPS = {
    "S": "first", "n": "neighbours", "c": "chain1", "C": "chain2", "x": "ends", "y": "chain3", "t": "third", "l": "last",
}
PLAN_BACK = (
    "S1", "T", "c1", "S0", "Q6", "S2", "n1", "c0", "Q4", "S3", "Q0", "x1", "C1", "c2", "n0", "Q2", "G", "c3", "x0",
    "n2", "C0", "n3", "Kn20", "y1", "i", "x3", "t0", "C2", "y0", "H", "Kn24", "t3", "l1", "C3", "t1", "y2", "x2",
    "Kx0", "l2", "y3", "t2", "Kx1", "l3", "l0", "J", "Kl", "I",
)
PLAN = (
    "+q1", "+q0", "+u0", "S3", "Z", "0q11", "0q01", "1q11", "0u01", "1q01", "0q12", "0q02", "S2", "c3", "2q01",
    "1u01", "0u02", "1q12", "S0", "2q11", "0q03", "0q13", "+o", "+u1", "S1", "n0", "1q03", "1q13", "1u02", "c2",
    "2q03", "0o1", "1q02", "0u11", "2q12", "2u02", "0o2", "x0", "c1", "+d0", "2q13", "1o1", "P0", "0u12", "2q02",
    "0o3", "n3", "3q11", "C3", "3q12", "3u02", "3q03", "n2", "3q13", "2u01", "3q02", "1o2", "t0", "3q01", "n1",
    "x3", "C2", "1u12", "x2", "1u11", "Pn", "c0", "1o3", "2o1", "0d01", "x1", "t3", "0d02", "A002", "2o2", "2o3",
    "2u12", "A402", "C1", "3u01", "0u03", "t1", "3u12", "C0", "t2", "0u13", "0d03", "1d01", "2u11", "y3", "y1",
    "+d1", "1u03", "y0", "y2", "Ps", "l1", "3o1", "1d02", "A424", "l3", "0d11", "1d03", "A024", "3o2", "1u13",
    "2d02", "l0", "2d01", "3u11", "2u03", "l2", "Pl", "3o3", "0d12", "1d11", "A045", "2u13", "A445", "0d13", "M",
    "1d12", "3u13", "2d03", "U0", "2d11", "U2", "1d13", "U1", "3u03", "3d01", "3d02", "2d12", "U3", "3d11", "3d03",
    "2d13", "D1", "D0", "3d12", "D2", "3d13", "D3",
)
F32 = jnp.float32
BF16 = jnp.bfloat16


def dot(left, right):
    return lax.dot_general(left, right, (((1,), (0,)), ((), ())), preferred_element_type=F32)


def dot_nt(left, right):
    return lax.dot_general(left, right, (((1,), (1,)), ((), ())), preferred_element_type=F32)


def tile(n):
    return pl.ds(pl.multiple_of(n * 256, 256), 256)


def layer_kernel(
    n_dp,
    x_in, cot_in, wq_in, wk_in, wv_in, wo_in, wup_in, wdn_in,
    len_in, qd_in, vd_in, qu_in, vu_in, qb_in, vb_in, ub_in, *rest
):
    vec_refs, rest = rest[:6], rest[6:]
    (
        out_ref, dx_ref, lora_ref,
        wqkv, wo, wup, wdn, small, lora_q, lora_v, vec_in, down_in,
        xwin, uwin, qwin, kwin, vwin, dowin, stwin, mask, mixed,
        att, attf, stat, midb, norm1, stat1, hid, gelp, acc, gffn, gbuf, dq, dk_acc, dv_acc, dkv,
        lsend, lrecv1, lrecv2,
        lsem, ssem, rsem,
    ) = rest
    rows = x_in.shape[0]
    width = x_in.shape[1]
    pairs = width // LANES
    dp, t = lax.axis_index("dp"), lax.axis_index("tensor")
    member = lax.rem(dp, GROUP)
    core = lax.rem(member, 2)
    yx = member // 2
    yx_x = yx + 1 - 2 * lax.rem(yx, 2)
    yx_y = yx + 2 - 4 * (yx // 2)
    yx_d = 3 - yx
    x_dev = (dp + 2 * (yx_x - yx), t)
    y_dev = (dp + 2 * (yx_y - yx), t)
    c_dev = (dp + 1 - 2 * core, t)

    def shard(a):
        first = jnp.where(t == 0, 1, t - 1)
        second = jnp.where(t == 0, 2, jnp.where(t == 3, 1, t + 1))
        third = jnp.where(t < 2, 3, 0)
        return jnp.where(a == 1, first, jnp.where(a == 2, second, third))

    barrier = pltpu.get_barrier_semaphore()
    for d in range(1, 4):
        pl.semaphore_signal(barrier, inc=1, device_id=(dp, lax.rem(t + d, 4)), device_id_type=MESH)
    for d in range(1, n_dp):
        pl.semaphore_signal(barrier, inc=1, device_id=(lax.rem(dp + d, n_dp), t), device_id_type=MESH)

    count = {"send": 0, "recv": 0, "local": 0}
    pending = {}

    def alloc(kind, n):
        first = count[kind]
        count[kind] += n
        return first

    def when(pred, fn):
        if pred is None:
            fn()
        else:
            pl.when(pred)(fn)

    def remote(src, dst, recv, dev, pred=None):
        slot = alloc("send", 1) % ssem.shape[0]
        if slot in pending:
            before, copy = pending[slot]
            when(before, copy.wait_send)
        copy = pltpu.make_async_remote_copy(
            src_ref=src, dst_ref=dst, send_sem=ssem.at[slot], recv_sem=rsem.at[recv],
            device_id=dev, device_id_type=MESH,
        )
        when(pred, copy.start)
        pending[slot] = (pred, copy)

    def arrived(dst, recv, pred=None):
        copy = pltpu.make_async_remote_copy(
            src_ref=dst, dst_ref=dst, send_sem=ssem.at[0], recv_sem=rsem.at[recv],
            device_id=(dp, t), device_id_type=MESH,
        )
        when(pred, copy.wait_recv)

    def settle():
        for pred, copy in pending.values():
            when(pred, copy.wait_send)
        pending.clear()

    def local(src, dst):
        copy = pltpu.make_async_copy(src, dst, lsem.at[alloc("local", 1)])
        copy.start()
        return copy

    ld_qkv = [
        local(w, wqkv.at[t, :, :, :, pl.ds(256 * i, 256)]) for i, w in enumerate((wq_in, wk_in, wv_in))
    ]
    ld_x = [local(x_in, xwin.at[2])]
    ld_up = [local(wup_in, wup.at[t])]
    ld_o = [local(wo_in, wo.at[t])]
    ld_dn = [local(wdn_in, wdn.at[t])]
    ld_cot = [local(cot_in, gffn)]

    def done(copies):
        while copies:
            copies.pop().wait()

    class Chunk:
        def __init__(self, ref, first, size, loads, by_y=None):
            self.ref, self.first, self.size, self.loads = ref, first, size, loads
            self.by_y = by_y or size // 2
            self.zr = alloc("recv", 4)
            self.xr, self.yr, self.dr, self.cr = (alloc("recv", 3) - 1 for _ in range(4))

        def region(self, s, place, lo=0, size=None):
            return self.ref.at[s, place, core, pl.ds(self.first + lo, size or self.size), :]

        def send(self):
            done(self.loads)
            own = self.region(t, yx)
            remote(own, own, self.zr + t, (dp, jnp.minimum(t + 1, 3)), t < 3)
            remote(own, own, self.zr + t, (dp, jnp.maximum(t - 1, 0)), t > 0)

        def stage0(self, a):
            s = shard(a)
            own = self.region(s, yx)
            arrived(own, self.zr + s)
            onward = jnp.where(s < t, t + 1, t - 1)
            remote(
                own, own, self.zr + s, (dp, jnp.clip(onward, 0, 3)),
                jnp.logical_and(onward >= 0, onward <= 3),
            )
            remote(own, own, self.xr + a, x_dev)
            remote(own, own, self.yr + a, y_dev)

        def stage1(self, a):
            s = shard(a)
            arrived(self.region(s, yx_x), self.xr + a)
            part = self.region(s, yx_x, 0, self.by_y)
            remote(part, part, self.dr + a, y_dev)
            arrived(self.region(s, yx_y), self.yr + a)
            part = self.region(s, yx_y, self.by_y, self.size - self.by_y)
            remote(part, part, self.dr + a, x_dev)

        def stage2(self, a):
            s = shard(a)
            arrived(self.region(s, yx_d), self.dr + a)
            four = self.ref.at[s, :, core, pl.ds(self.first, self.size), :]
            remote(four, four, self.cr + a, c_dev)

        def stage3(self, a):
            s = shard(a)
            arrived(self.ref.at[s, :, 1 - core, pl.ds(self.first, self.size), :], self.cr + a)

    upward, downward = (dp, jnp.minimum(t + 1, 3)), (dp, jnp.maximum(t - 1, 0))
    after, before = (jnp.minimum(dp + 1, n_dp - 1), t), (jnp.maximum(dp - 1, 0), t)
    not_last, not_first = dp < n_dp - 1, dp > 0

    class Exchange:
        def __init__(self, ref, first, size):
            self.ref, self.low, self.size = ref, first, size
            self.base = alloc("recv", 6)

        def at(self, slot):
            return self.ref.at[slot, pl.ds(self.low, self.size), :]

        def go(self, src, dst, dev, pred):
            remote(self.at(src), self.at(dst), self.base + dst, dev, pred)

        def get(self, slot, pred):
            arrived(self.at(slot), self.base + slot, pred)

        def first(self):
            self.go(2, 1, upward, t < 3)
            self.go(2, 3, downward, t > 0)
            self.go(2, 5, after, jnp.logical_and(t == 3, not_last))
            self.go(2, 5, before, jnp.logical_and(t == 0, not_first))

        def neighbours(self):
            self.get(1, t >= 1)
            self.get(3, t <= 2)
            self.go(1, 0, upward, t == 2)
            self.go(3, 4, downward, t == 1)

        def chain1(self):
            self.get(5, jnp.logical_and(t == 3, not_first))
            self.get(5, jnp.logical_and(t == 0, not_last))
            self.go(5, 5, downward, jnp.logical_and(t == 3, not_first))
            self.go(5, 5, upward, jnp.logical_and(t == 0, not_last))

        def chain2(self):
            self.get(5, jnp.logical_and(t == 2, not_first))
            self.get(5, jnp.logical_and(t == 1, not_last))
            self.go(5, 0, downward, jnp.logical_and(t == 2, not_first))
            self.go(5, 4, upward, jnp.logical_and(t == 1, not_last))
            self.go(1, 0, upward, t == 1)
            self.go(3, 4, downward, t == 2)

        def ends(self):
            self.get(4, t == 0)
            self.get(0, t == 3)
            self.go(4, 0, after, jnp.logical_and(t == 0, not_last))
            self.go(0, 4, before, jnp.logical_and(t == 3, not_first))

        def chain3(self):
            self.get(0, jnp.logical_and(t == 1, not_first))
            self.get(4, jnp.logical_and(t == 2, not_last))
            self.go(0, 1, downward, jnp.logical_and(t == 1, not_first))
            self.go(4, 3, upward, jnp.logical_and(t == 2, not_last))

        def third(self):
            self.get(0, jnp.logical_and(t == 0, not_first))
            self.get(4, jnp.logical_and(t == 3, not_last))

        def last(self):
            self.get(1, jnp.logical_and(t == 0, not_first))
            self.get(3, jnp.logical_and(t == 3, not_last))
            self.get(4, t == 1)
            self.get(0, t == 2)

    lane = lax.broadcasted_iota(jnp.int32, (1, LANES), 1)
    first_half = lane < HD

    def vec(i):
        return vec_in[i : i + 1, :]

    def halves(block):
        zero = jnp.zeros_like(block)
        return jnp.where(first_half, block, zero), jnp.where(first_half, zero, block)

    def clear(ref):
        def fill(pred, slot):
            @pl.when(pred)
            def _():
                ref[slot] = jnp.zeros(ref.shape[1:], ref.dtype)

        fill(jnp.logical_and(dp == 0, t <= 1), 0)
        fill(jnp.logical_and(dp == 0, t == 0), 1)
        fill(jnp.logical_and(dp == n_dp - 1, t >= 2), 4)
        fill(jnp.logical_and(dp == n_dp - 1, t == 3), 3)

    def project(names):
        begin = blocks[names[0]][1] * rows
        place = slice(begin, begin + len(names) * rows)

        def tokens():
            parts = [xwin[blocks[name][0]] for name in names]
            return parts[0] if len(parts) == 1 else jnp.concatenate(parts, axis=0)

        uwin[place] = dot_nt(tokens(), down_in[...]).astype(BF16)

        @pl.loop(0, 4)
        def _(s):
            y = dot(tokens(), wqkv[s].reshape(width, 3 * 256))
            u = uwin[place, 0:LANES]
            q = y[:, :256] + dot(u, lora_q[s]) + small[s, 16:17, :]
            qwin[place, tile(s)] = (q * (1.0 / math.sqrt(HD))).astype(BF16)
            kwin[place, tile(s)] = y[:, 256:512].astype(BF16)
            v = y[:, 512:] + dot(u, lora_v[s]) + small[s, 17:18, :]
            vwin[place, tile(s)] = v.astype(BF16)

    def loop_pairs(lo, hi, body, unroll=1):
        @pl.loop(lo, hi, unroll=unroll)
        def _(p):
            body(p, pl.ds(pl.multiple_of(p * LANES, LANES), LANES))

    def column(index):
        return jnp.sum(jnp.where(lane == index, stat[...], 0.0), axis=1, keepdims=True)

    def attend(lo, hi):
        begin, end = lo * 256, hi * 256

        def body(p, cols):
            q_heads = halves(qwin[tile(1), cols])
            k = kwin[begin:end, cols]
            v = jnp.concatenate([vwin[begin:end, cols], uwin[begin:end, LANES:]], axis=1)
            before, outs, found, inputs = attf[:, cols], [], stat[...], mixed[...]
            for i in range(2):
                s = dot_nt(q_heads[i], k) + mask[:, begin:end]
                top = jnp.max(s, axis=1, keepdims=True)
                if lo:
                    old = column(2 * p + i)
                    top = jnp.maximum(top, old)
                e = jnp.exp(s - top)
                total = jnp.sum(e, axis=1, keepdims=True)
                o = dot(e.astype(BF16), v)
                o, extra = o[:, :LANES], o[:, LANES:]
                if lo:
                    alpha = jnp.exp(old - top)
                    total = total + column(16 + 2 * p + i) * alpha
                    o = o + before * alpha
                    extra = extra + inputs * alpha
                if hi == 5:
                    o = o * (1.0 / total)
                    extra = extra * (1.0 / total)
                    top = top + jnp.log(total)
                outs.append(o)
                inputs = jnp.where(lane // 8 == 2 * p + i, extra, inputs)
                found = jnp.where(lane == 2 * p + i, top, jnp.where(lane == 16 + 2 * p + i, total, found))
            o = jnp.where(first_half, outs[0], outs[1])
            attf[:, cols] = o
            if hi == 5:
                att[:, cols] = o.astype(BF16)
            stat[...] = found
            mixed[...] = inputs

        return body

    def after_attention():
        @pl.loop(0, 4, unroll=4)
        def _(n):
            acc[:, tile(n)] = dot(att[...], wo[:, :, :, :, tile(n)].reshape(width, 256))

        z = xwin[2].astype(F32) + acc[...] + vec(0)
        centre = z - jnp.mean(z, axis=1, keepdims=True)
        r = lax.rsqrt(jnp.mean(centre * centre, axis=1, keepdims=True) + NORM_EPS)
        n1 = centre * r
        norm1[...] = n1
        stat1[...] = jnp.broadcast_to(r, stat1.shape)
        m = n1 * vec(1) + vec(2)
        midb[...] = m.astype(BF16)
        acc[...] = m + vec(3)

    def up(s):
        @pl.loop(0, 4, unroll=4)
        def _(n):
            b = dot(midb[...], wup[s, :, :, :, tile(n)].reshape(width, 256)) + small[s, pl.ds(18 + n, 1), :]
            cdf = 0.5 + 0.5 * lax.erf(b * (1.0 / math.sqrt(2.0)))
            hid[s, :, tile(n)] = (b * cdf).astype(BF16)
            gelp[s, :, tile(n)] = cdf + b * jnp.exp(-0.5 * b * b) * (1.0 / math.sqrt(2.0 * math.pi))

    def down(s):
        @pl.loop(0, 4, unroll=4)
        def _(n):
            acc[:, tile(n)] += dot(hid[s], wdn[s, :, :, :, tile(n)].reshape(width, 256))

    def second_norm():
        z = acc[...]
        centre = z - jnp.mean(z, axis=1, keepdims=True)
        r = lax.rsqrt(jnp.mean(centre * centre, axis=1, keepdims=True) + NORM_EPS)
        n2 = centre * r
        midb[...] = (n2 * vec(4) + vec(5)).astype(BF16)
        g = gffn[...].astype(F32) * vec(4)
        g = r * (g - jnp.mean(g, axis=1, keepdims=True) - n2 * jnp.mean(g * n2, axis=1, keepdims=True))
        acc[...] = g
        gffn[...] = g.astype(BF16)

    def ffn_back(s):
        @pl.loop(0, 4, unroll=4)
        def _(n):
            toward = dot_nt(gffn[...], wdn[s, n].reshape(256, width))
            gbuf[:, tile(n)] = (toward * gelp[s, :, tile(n)]).astype(BF16)

        @pl.loop(0, 4, unroll=4)
        def _(n):
            acc[:, tile(n)] += dot_nt(gbuf[...], wup[s, n].reshape(256, width))

    def first_norm_back():
        g = acc[...] * vec(1)
        n1 = norm1[...]
        g = g - jnp.mean(g, axis=1, keepdims=True) - n1 * jnp.mean(g * n1, axis=1, keepdims=True)
        g = stat1[:, 0:1] * g
        acc[...] = g
        gffn[...] = g.astype(BF16)

        @pl.loop(0, 4, unroll=4)
        def _(s):
            dowin[2, :, tile(s)] = dot_nt(gffn[...], wo[s].reshape(256, width)).astype(BF16)

    def statistics():
        product = dowin[2].astype(F32) * attf[...]
        high = product.astype(BF16)
        low = (product - high.astype(F32)).astype(BF16)
        at_row = lax.broadcasted_iota(jnp.int32, (width, LANES), 0) // HD + 16
        at_lane = lax.broadcasted_iota(jnp.int32, (width, LANES), 1)
        pick = (at_row == at_lane).astype(F32).astype(BF16)
        delta = dot(high, pick) + dot(low, pick)
        both = jnp.where(lane < 16, stat[...], delta)
        stat[...] = both
        stwin[2] = both.T[0:32]

    def pass_queries(p, cols):
        q_heads, do_heads = halves(qwin[tile(1), cols]), halves(dowin[2, :, cols])
        k, v = kwin[:, cols], vwin[:, cols]
        parts = []
        for i in range(2):
            prob = jnp.exp(dot_nt(q_heads[i], k) + mask[...] - column(2 * p + i))
            ds = prob * (dot_nt(do_heads[i], v) - column(16 + 2 * p + i))
            parts.append(dot(ds.astype(BF16), k))
        dq[:, cols] = (jnp.where(first_half, parts[0], parts[1]) * (1.0 / math.sqrt(HD))).astype(BF16)

    def pass_keys(pieces, at, end, first=False, unroll=1):
        def joined(parts, axis):
            return parts[0] if len(parts) == 1 else jnp.concatenate(parts, axis=axis)

        windows = [slice(blocks[name][1] * rows + lo, blocks[name][1] * rows + hi) for name, lo, hi in pieces]
        few = sum(hi - lo for _, lo, hi in pieces) <= 256

        def line(index):
            return joined([stwin[blocks[name][0], pl.ds(index, 1), :][:, lo:hi] for name, lo, hi in pieces], 1)

        def products(heads, right):
            if few:
                both = dot_nt(jnp.concatenate(heads, axis=0), right)
                return both[:256], both[256:]
            return [dot_nt(head, right) for head in heads]

        def body(p, cols):
            k_heads, v_heads = halves(kwin[tile(1), cols]), halves(vwin[tile(1), cols])
            q = joined([qwin[window, cols] for window in windows], 0)
            do = joined([dowin[blocks[name][0], lo:hi, cols] for name, lo, hi in pieces], 0)
            scores = products(k_heads, q)
            grads = products(v_heads, do)
            apart = joined([mask[:, window] for window in windows], 1)
            probs, ds = [], []
            for i in range(2):
                prob = jnp.exp(scores[i] + apart - line(2 * p + i))
                ds.append((prob * (grads[i] - line(16 + 2 * p + i))).astype(BF16))
                probs.append(prob.astype(BF16))
            for total, lefts, right in ((dk_acc, ds, q), (dv_acc, probs, do)):
                if few:
                    both = dot(jnp.concatenate(lefts, axis=0), right)
                    both = jnp.where(first_half, both[:256], both[256:])
                else:
                    both = jnp.where(first_half, dot(lefts[0], right), dot(lefts[1], right))
                total[:, cols] = both if first else total[:, cols] + both

        loop_pairs(at, end, body, unroll)

    def lora_partial():
        u = uwin[tile(1), 0:LANES].astype(F32).T[0:16].astype(BF16)
        of_queries = dot(u, dq[...])
        each = dot(mixed[...].T.astype(BF16), dowin[2])
        row_head = lax.broadcasted_iota(jnp.int32, each.shape, 0) // 8
        column_head = lax.broadcasted_iota(jnp.int32, each.shape, 1) // HD
        each = jnp.where(row_head == column_head, each, 0.0)
        of_values = each[0:8]
        for h in range(1, 16):
            of_values = of_values + each[8 * h : 8 * h + 8]
        both = jnp.concatenate([of_queries[0:8], of_values], axis=0)
        for s in range(4):
            lsend[s] = both[:, 256 * s : 256 * s + 256]

    def query_gradient():
        gu = jnp.zeros((rows, LANES), F32)
        for s in range(4):
            gu = gu + dot_nt(dq[:, 256 * s : 256 * s + 256], lora_q[s])
        stat1[...] = gu

        @pl.loop(0, 4, unroll=4)
        def _(n):
            total = acc[:, tile(n)]
            for s in range(4):
                weight = wqkv[s, n, :, :, 0:256].reshape(256, 256)
                total = total + dot_nt(dq[:, 256 * s : 256 * s + 256], weight)
            acc[:, tile(n)] = total

    def input_gradient():
        gu = stat1[...]
        for s in range(4):
            gu = gu + dot_nt(dkv[1, :, 256 * s : 256 * s + 256], lora_v[s])
        gu = gu.astype(BF16)
        for n in range(4):
            total = acc[:, tile(n)] + dot(gu, down_in[0:LANES, tile(n)])
            for s in range(4):
                cols = slice(256 * s, 256 * s + 256)
                two = jnp.concatenate([dkv[0, :, cols], dkv[1, :, cols]], axis=1)
                total = total + dot_nt(two, wqkv[s, n, :, :, 256:].reshape(256, 512))
            att[:, tile(n)] = total.astype(BF16)
            final.append(local(att.at[:, tile(n)], dx_ref.at[:, tile(n)]))

    def chunk(*args):
        return Chunk(*args)

    qkv0, qkv1 = chunk(wqkv, 0, 64, ld_qkv), chunk(wqkv, 64, 64, ld_qkv)
    up0, up1 = chunk(wup, 0, 64, ld_up), chunk(wup, 64, 64, ld_up)
    dn0, dn1 = chunk(wdn, 0, 64, ld_dn), chunk(wdn, 64, 64, ld_dn)
    o0 = chunk(wo, 0, 32, ld_o)
    half, quarter = rows // 2, rows // 4
    tok = [Exchange(xwin, i * quarter, quarter) for i in range(4)]
    small_base = alloc("recv", 4)
    wide = [Exchange(dowin, i * quarter, quarter) for i in range(4)]
    narrow = Exchange(stwin, 0, 32)
    lora1 = alloc("recv", 4)
    lora2 = alloc("recv", n_dp)

    def prepare():
        for ref in (xwin, dowin, stwin):
            clear(ref)
        for i in range(8):
            cols = slice(LANES * i, LANES * i + LANES)
            for j, ref in enumerate(vec_refs):
                vec_in[j : j + 1, cols] = ref[i : i + 1, :].astype(F32)
        own_small = [2.0 * qu_in[...].astype(F32), 2.0 * vu_in[...].astype(F32)]
        small[t, 0:8, :] = own_small[0]
        small[t, 8:16, :] = own_small[1]
        for i in range(2):
            cols = slice(LANES * i, LANES * i + LANES)
            small[t, 16:17, cols] = qb_in[i : i + 1, :].astype(F32)
            small[t, 17:18, cols] = vb_in[i : i + 1, :].astype(F32)
            for j in range(4):
                small[t, 18 + j : 19 + j, cols] = ub_in[2 * j + i : 2 * j + i + 1, :].astype(F32)
        small[t, 22:24, :] = jnp.zeros((2, 256), F32)
        value_map = vd_in[...].astype(F32)
        maps = [qd_in[...].astype(F32), value_map, jnp.zeros((LANES - 16, width), F32)] + [value_map] * 16
        down_in[...] = jnp.concatenate(maps, axis=0).astype(BF16)
        for d in range(1, 4):
            remote(small.at[t], small.at[t], small_base + t, (dp, lax.rem(t + d, 4)))

    pl.semaphore_wait(barrier, 3 + n_dp - 1)
    near = jnp.where(t < 3, 3, 1)
    second = jnp.where(lax.rem(t, 2) == 0, 4, 0)
    third = jnp.where(t == 0, 0, jnp.where(t == 3, 4, 1))
    final = jnp.where(t == 0, 1, jnp.where(t == 1, 4, jnp.where(t == 2, 0, 3)))
    blocks = {"n": (near, 0), "2": (2, 1), "s": (second, 2), "t": (third, 3), "l": (final, 4)}
    named = {"q0": qkv0, "q1": qkv1, "u0": up0, "u1": up1, "d0": dn0, "d1": dn1, "o": o0}
    def setup():
        lengths = len_in[...]
        docs = lengths.shape[0] * LANES
        high, low = lengths // 256, lax.rem(lengths, 256)
        upto = (
            lax.broadcasted_iota(jnp.int32, (LANES, LANES), 0)
            <= lax.broadcasted_iota(jnp.int32, (LANES, LANES), 1)
        ).astype(F32).astype(BF16)

        def summed(part):
            return dot(part.astype(F32).astype(BF16), upto)

        ends = 256.0 * summed(high) + summed(low)
        window = mask.shape[1]
        first = (dp * 4 + t) * rows - MAXLEN
        spot = lax.broadcasted_iota(jnp.int32, (1, window), 1)
        place = spot // rows
        where = place
        for slot, nth_place in blocks.values():
            where = jnp.where(place == nth_place, slot, where)
        position = first + where * rows + lax.rem(spot, rows)
        at = position.astype(F32)
        passed = jnp.zeros((1, window), F32)
        before = jnp.zeros((1, 1), F32)
        for r in range(lengths.shape[0]):
            end = ends[r : r + 1, :] + before
            before = end[:, LANES - 1 :]
            column = jnp.broadcast_to(end, (LANES, LANES)).T[:, 0:1]
            passed = passed + jnp.sum((column <= at).astype(F32), axis=0, keepdims=True)
        inside = jnp.logical_and(position >= 0, passed < docs)
        ids = jnp.where(inside, passed, -1.0)
        own = jnp.broadcast_to(ids[:, rows : 2 * rows], (LANES, rows)).T[:, 0:1]
        mask[...] = jnp.where(own == ids, 0.0, MASKED)
        stat[...] = jnp.zeros(stat.shape, F32)

    def small_ready():
        for d in range(1, 4):
            peer = lax.rem(t + d, 4)
            arrived(small.at[peer], small_base + peer)
        none = jnp.zeros((8, 256), F32)
        lora_q[:, 16:, :] = jnp.zeros((4, LANES - 16, 256), BF16)
        lora_v[:, 16:, :] = jnp.zeros((4, LANES - 16, 256), BF16)
        for s in range(4):
            lora_q[s, 0:16, :] = jnp.concatenate([small[s, 0:8, :], none], axis=0).astype(BF16)
            lora_v[s, 0:16, :] = jnp.concatenate([none, small[s, 8:16, :]], axis=0).astype(BF16)


    def part(a):
        return t if a == 0 else shard(a)

    for item in PLAN:
        kind, rest = item[0], item[1:]
        if kind == "+":
            named[rest].send()
        elif kind in "0123":
            getattr(named[rest[:-1]], "stage" + kind)(int(rest[-1]))
        elif kind in STEPS:
            done(ld_x)
            getattr(tok[int(rest)], STEPS[kind])()
        elif kind == "Z":
            prepare()
        elif item == "P0":
            setup()
            small_ready()
        elif kind == "P":
            done(ld_qkv)
            project({"n": "n2", "s": "st", "l": "l"}[rest])
        elif kind == "A":
            at, lo, hi = (int(i) for i in rest)
            loop_pairs(at, at + 4, attend(lo, hi), 2)
        elif kind == "M":
            done(ld_o)
            after_attention()
        elif kind == "U":
            done(ld_up)
            up(part(int(rest)))
        elif kind == "D":
            done(ld_dn)
            down(part(int(rest)))
    for copies in (ld_qkv, ld_o, ld_up, ld_dn):
        done(copies)

    done(ld_cot)
    second_norm()
    final = [local(midb, out_ref)]

    @pl.loop(0, 4)
    def _(s):
        ffn_back(s)

    first_norm_back()

    def swap(step, i):
        for e in [wide[i]] + ([narrow] if i == 0 else []):
            getattr(e, step)()

    for item in PLAN_BACK:
        kind, rest = item[0], item[1:]
        if item == "l3":
            settle()
        if kind in STEPS:
            swap(STEPS[kind], int(rest))
        elif kind == "T":
            statistics()
        elif kind == "Q":
            loop_pairs(int(rest), int(rest) + 2, pass_queries)
        elif kind == "K":
            if rest[0] == "x":
                lo = int(rest[1]) * half
                pass_keys([("s", lo, lo + half), ("t", lo, lo + half)], 0, pairs, unroll=2)
            elif rest[0] == "l":
                pass_keys([("l", 0, rows)], 0, pairs, unroll=2)
            else:
                at = int(rest[2])
                pass_keys([("n", 0, rows), ("2", 0, rows)], at, at + 4, first=True)
        elif kind == "G":
            lora_partial()
            for d in range(1, 4):
                peer = lax.rem(t + d, 4)
                remote(lsend.at[peer], lrecv1.at[t], lora1 + t, (dp, peer))
            lrecv1[t] = lsend[t]
        elif kind == "H":
            for d in range(1, 4):
                peer = lax.rem(t + d, 4)
                arrived(lrecv1.at[peer], lora1 + peer)
            lrecv2[dp] = 2.0 * ((lrecv1[0] + lrecv1[1]) + (lrecv1[2] + lrecv1[3]))
            for d in range(1, n_dp):
                remote(lrecv2.at[dp], lrecv2.at[dp], lora2 + dp, (lax.rem(dp + d, n_dp), t))
        elif kind == "J":
            for d in range(1, n_dp):
                peer = lax.rem(dp + d, n_dp)
                arrived(lrecv2.at[peer], lora2 + peer)
            total = lrecv2[0]
            for i in range(1, n_dp):
                total = total + lrecv2[i]
            lsend[0] = total
            final.append(local(lsend.at[0], lora_ref))
        elif kind == "i":
            query_gradient()
        elif kind == "I":
            dkv[0] = dk_acc[...].astype(BF16)
            dkv[1] = dv_acc[...].astype(BF16)
            input_gradient()
    settle()
    done(final)
    assert count["recv"] <= rsem.shape[0] and count["local"] <= lsem.shape[0]


def hand_over(out, grad, lora, out_to, grad_to, query_to, value_to, out_at, grad_at, lora_at, sems):
    rows = out.shape[0] // 4
    parts = [pl.ds(i * rows, rows) for i in range(4)]
    loads = [(lora, lora_at)]
    stores = [[(lora_at.at[0:8], query_to), (lora_at.at[8:16], value_to)]]
    for source, at, to in ((out, out_at, out_to), (grad, grad_at, grad_to)):
        for part in parts:
            loads.append((source.at[part], at.at[part]))
            stores.append([(at.at[part], to.at[part])])
    copies = [pltpu.make_async_copy(a, b, sems.at[i]) for i, (a, b) in enumerate(loads)]
    for copy in copies:
        copy.start()
    moved = []
    for copy, pairs in zip(copies, stores):
        copy.wait()
        for a, b in pairs:
            moved.append(pltpu.make_async_copy(a, b, sems.at[len(copies) + len(moved)]))
            moved[-1].start()
    for copy in moved:
        copy.wait()


def shards(
    tokens, document_lengths, query_proj_weight, query_proj_bias, key_proj_weight, value_proj_weight,
    value_proj_bias, query_adapter_down, value_adapter_down, query_adapter_up, value_adapter_up,
    attention_out_weight, attention_out_bias, attention_norm_gain, attention_norm_bias, up_proj_weight,
    up_proj_bias, down_proj_weight, down_proj_bias, feedforward_norm_gain, feedforward_norm_bias, cotangent,
):
    rows, width = tokens.shape
    n_dp = lax.axis_size("dp")
    window = rows + 2 * MAXLEN

    def fold(vector):
        return vector.reshape(vector.shape[0] // LANES, LANES)

    def cut(weight):
        return weight.reshape(4, 2, weight.shape[0] // GROUP, weight.shape[1])

    def vmem(shape, dtype):
        return pltpu.VMEM(shape, dtype)

    small_arrays = (
        fold(document_lengths), query_adapter_down.T, value_adapter_down.T, query_adapter_up, value_adapter_up,
        fold(query_proj_bias), fold(value_proj_bias), fold(up_proj_bias), fold(attention_out_bias),
        fold(attention_norm_gain), fold(attention_norm_bias), fold(down_proj_bias), fold(feedforward_norm_gain),
        fold(feedforward_norm_bias),
    )
    any_spec = pl.BlockSpec(memory_space=pl.ANY)
    vmem_spec = pl.BlockSpec(memory_space=pltpu.VMEM)
    full = (rows, width)
    rank = query_adapter_up.shape[0]
    call = pl.pallas_call(
        lambda *refs: layer_kernel(n_dp, *refs),
        out_shape=(
            jax.ShapeDtypeStruct(full, BF16),
            jax.ShapeDtypeStruct(full, BF16),
            jax.ShapeDtypeStruct((16, 256), F32),
        ),
        in_specs=[any_spec] * 8 + [vmem_spec] * 14,
        out_specs=(any_spec,) * 3,
        scratch_shapes=[
            vmem((4, 4, 2, 128, 768), BF16),
            vmem((4, 4, 2, 32, 1024), BF16),
            vmem((4, 4, 2, 128, 1024), BF16),
            vmem((4, 4, 2, 128, 1024), BF16),
            vmem((4, 24, 256), F32),
            vmem((4, 128, 256), BF16),
            vmem((4, 128, 256), BF16),
            vmem((8, width), F32),
            vmem((2 * LANES, width), BF16),
            vmem((6, rows, width), BF16),
            vmem((window, 2 * LANES), BF16),
            vmem((window, width), BF16),
            vmem((window, width), BF16),
            vmem((window, width), BF16),
            vmem((6, rows, width), BF16),
            vmem((6, 32, rows), F32),
            vmem((rows, window), F32),
            vmem((rows, LANES), F32),
            vmem(full, BF16),
            vmem(full, F32),
            vmem((rows, LANES), F32),
            vmem(full, BF16),
            vmem(full, F32),
            vmem((rows, LANES), F32),
            vmem((4, rows, width), BF16),
            vmem((4, rows, width), F32),
            vmem(full, F32),
            vmem(full, BF16),
            vmem(full, BF16),
            vmem(full, BF16),
            vmem(full, F32),
            vmem(full, F32),
            vmem((2, rows, width), BF16),
            vmem((4, 16, 256), F32),
            vmem((4, 16, 256), F32),
            vmem((n_dp, 16, 256), F32),
            pltpu.SemaphoreType.DMA((16,)),
            pltpu.SemaphoreType.DMA((48,)),
            pltpu.SemaphoreType.DMA((174 + n_dp,)),
        ],
        compiler_params=pltpu.CompilerParams(
            collective_id=0, has_side_effects=True, vmem_limit_bytes=63 * 2**20
        ),
        name="layer",
    )
    out, grad, lora = call(
        tokens, cotangent, cut(query_proj_weight), cut(key_proj_weight), cut(value_proj_weight),
        cut(attention_out_weight), cut(up_proj_weight), cut(down_proj_weight), *small_arrays,
    )
    lora_shape = jax.ShapeDtypeStruct((rank, 256), F32)
    return pl.pallas_call(
        hand_over,
        out_shape=(out, grad, lora_shape, lora_shape),
        in_specs=[any_spec] * 3,
        out_specs=(any_spec,) * 4,
        scratch_shapes=[
            vmem(full, BF16), vmem(full, BF16), vmem((2 * rank, 256), F32), pltpu.SemaphoreType.DMA((19,))
        ],
        name="hand_over",
    )(out, grad, lora)


def solution(mesh):
    whole, columns = P(), P(None, "tensor")
    stream = P(("dp", "tensor"), None)
    return jax.shard_map(
        shards,
        mesh=mesh,
        in_specs=(
            stream, whole, columns, P("tensor"), columns, columns, P("tensor"), whole, whole, columns, columns,
            P("tensor", None), whole, whole, whole, columns, P("tensor"), P("tensor", None), whole, whole, whole,
            stream,
        ),
        out_specs=(stream, stream, columns, columns),
        check_vma=False,
    )
```

```python
import math

import jax
import jax.numpy as jnp
from jax import lax
from jax.experimental import pallas as pl
from jax.experimental.pallas import tpu as pltpu
from jax.sharding import PartitionSpec as P

MESH = pl.DeviceIdType.MESH
HD = 64
MAXLEN = 512
GROUP = 8
LANES = 128
NORM_EPS = 1e-05
MASKED = -1e30
STEPS = {
    "S": "first", "n": "neighbours", "c": "chain1", "C": "chain2", "x": "ends", "y": "chain3", "t": "third", "l": "last",
}
PLAN_BACK = (
    "S1", "T", "c1", "S0", "Q6", "S2", "n1", "c0", "Q4", "S3", "Q0", "x1", "C1", "c2", "n0", "Q2", "G", "c3", "x0",
    "n2", "C0", "n3", "Kn20", "y1", "i", "x3", "t0", "C2", "y0", "H", "Kn24", "t3", "l1", "C3", "t1", "y2", "x2",
    "Kx0", "l2", "y3", "t2", "Kx1", "l3", "l0", "J", "Kl", "I",
)
PLAN = (
    "+q1", "+q0", "+u0", "S3", "Z", "0q11", "0q01", "1q11", "0u01", "1q01", "0q12", "0q02", "S2", "c3", "2q01",
    "1u01", "0u02", "1q12", "S0", "2q11", "0q03", "0q13", "+o", "+u1", "S1", "n0", "1q03", "1q13", "1u02", "c2",
    "2q03", "0o1", "1q02", "0u11", "2q12", "2u02", "0o2", "x0", "c1", "+d0", "2q13", "1o1", "P0", "0u12", "2q02",
    "0o3", "n3", "3q11", "C3", "3q12", "3u02", "3q03", "n2", "3q13", "2u01", "3q02", "1o2", "t0", "3q01", "n1",
    "x3", "C2", "1u12", "x2", "1u11", "Pn", "c0", "1o3", "2o1", "0d01", "x1", "t3", "0d02", "A002", "2o2", "2o3",
    "2u12", "A402", "C1", "3u01", "0u03", "t1", "3u12", "C0", "t2", "0u13", "0d03", "1d01", "2u11", "y3", "y1",
    "+d1", "1u03", "y0", "y2", "Ps", "l1", "3o1", "1d02", "A424", "l3", "0d11", "1d03", "A024", "3o2", "1u13",
    "2d02", "l0", "2d01", "3u11", "2u03", "l2", "Pl", "3o3", "0d12", "1d11", "A045", "2u13", "A445", "0d13", "M",
    "1d12", "3u13", "2d03", "U0", "2d11", "U2", "1d13", "U1", "3u03", "3d01", "3d02", "2d12", "U3", "3d11", "3d03",
    "2d13", "D1", "D0", "3d12", "D2", "3d13", "D3",
)
F32 = jnp.float32
BF16 = jnp.bfloat16


def dot(left, right):
    return lax.dot_general(left, right, (((1,), (0,)), ((), ())), preferred_element_type=F32)


def dot_nt(left, right):
    return lax.dot_general(left, right, (((1,), (1,)), ((), ())), preferred_element_type=F32)


def tile(n):
    return pl.ds(pl.multiple_of(n * 256, 256), 256)


def layer_kernel(
    n_dp,
    x_in, cot_in, wq_in, wk_in, wv_in, wo_in, wup_in, wdn_in,
    len_in, qd_in, vd_in, qu_in, vu_in, qb_in, vb_in, ub_in, *rest
):
    vec_refs, rest = rest[:6], rest[6:]
    (
        out_ref, dx_ref, lora_ref,
        wqkv, wo, wup, wdn, small, lora_q, lora_v, vec_in, down_in,
        xwin, uwin, qwin, kwin, vwin, dowin, stwin, mask, mixed,
        att, attf, stat, midb, norm1, stat1, hid, gelp, acc, gffn, gbuf, dq, dk_acc, dv_acc, dkv,
        lsend, lrecv1, lrecv2,
        lsem, ssem, rsem,
    ) = rest
    rows = x_in.shape[0]
    width = x_in.shape[1]
    pairs = width // LANES
    dp, t = lax.axis_index("dp"), lax.axis_index("tensor")
    member = lax.rem(dp, GROUP)
    core = lax.rem(member, 2)
    yx = member // 2
    yx_x = yx + 1 - 2 * lax.rem(yx, 2)
    yx_y = yx + 2 - 4 * (yx // 2)
    yx_d = 3 - yx
    x_dev = (dp + 2 * (yx_x - yx), t)
    y_dev = (dp + 2 * (yx_y - yx), t)
    c_dev = (dp + 1 - 2 * core, t)

    def shard(a):
        first = jnp.where(t == 0, 1, t - 1)
        second = jnp.where(t == 0, 2, jnp.where(t == 3, 1, t + 1))
        third = jnp.where(t < 2, 3, 0)
        return jnp.where(a == 1, first, jnp.where(a == 2, second, third))

    barrier = pltpu.get_barrier_semaphore()
    for d in range(1, 4):
        pl.semaphore_signal(barrier, inc=1, device_id=(dp, lax.rem(t + d, 4)), device_id_type=MESH)
    for d in range(1, n_dp):
        pl.semaphore_signal(barrier, inc=1, device_id=(lax.rem(dp + d, n_dp), t), device_id_type=MESH)

    count = {"send": 0, "recv": 0, "local": 0}
    pending = {}

    def alloc(kind, n):
        first = count[kind]
        count[kind] += n
        return first

    def when(pred, fn):
        if pred is None:
            fn()
        else:
            pl.when(pred)(fn)

    def remote(src, dst, recv, dev, pred=None):
        slot = alloc("send", 1) % ssem.shape[0]
        if slot in pending:
            before, copy = pending[slot]
            when(before, copy.wait_send)
        copy = pltpu.make_async_remote_copy(
            src_ref=src, dst_ref=dst, send_sem=ssem.at[slot], recv_sem=rsem.at[recv],
            device_id=dev, device_id_type=MESH,
        )
        when(pred, copy.start)
        pending[slot] = (pred, copy)

    def arrived(dst, recv, pred=None):
        copy = pltpu.make_async_remote_copy(
            src_ref=dst, dst_ref=dst, send_sem=ssem.at[0], recv_sem=rsem.at[recv],
            device_id=(dp, t), device_id_type=MESH,
        )
        when(pred, copy.wait_recv)

    def settle():
        for pred, copy in pending.values():
            when(pred, copy.wait_send)
        pending.clear()

    def local(src, dst):
        copy = pltpu.make_async_copy(src, dst, lsem.at[alloc("local", 1)])
        copy.start()
        return copy

    ld_qkv = [
        local(w, wqkv.at[t, :, :, :, pl.ds(256 * i, 256)]) for i, w in enumerate((wq_in, wk_in, wv_in))
    ]
    ld_x = [local(x_in, xwin.at[2])]
    ld_up = [local(wup_in, wup.at[t])]
    ld_o = [local(wo_in, wo.at[t])]
    ld_dn = [local(wdn_in, wdn.at[t])]
    ld_cot = [local(cot_in, gffn)]

    def done(copies):
        while copies:
            copies.pop().wait()

    class Chunk:
        def __init__(self, ref, first, size, loads, by_y=None):
            self.ref, self.first, self.size, self.loads = ref, first, size, loads
            self.by_y = by_y or size // 2
            self.zr = alloc("recv", 4)
            self.xr, self.yr, self.dr, self.cr = (alloc("recv", 3) - 1 for _ in range(4))

        def region(self, s, place, lo=0, size=None):
            return self.ref.at[s, place, core, pl.ds(self.first + lo, size or self.size), :]

        def send(self):
            done(self.loads)
            own = self.region(t, yx)
            remote(own, own, self.zr + t, (dp, jnp.minimum(t + 1, 3)), t < 3)
            remote(own, own, self.zr + t, (dp, jnp.maximum(t - 1, 0)), t > 0)

        def stage0(self, a):
            s = shard(a)
            own = self.region(s, yx)
            arrived(own, self.zr + s)
            onward = jnp.where(s < t, t + 1, t - 1)
            remote(
                own, own, self.zr + s, (dp, jnp.clip(onward, 0, 3)),
                jnp.logical_and(onward >= 0, onward <= 3),
            )
            remote(own, own, self.xr + a, x_dev)
            remote(own, own, self.yr + a, y_dev)

        def stage1(self, a):
            s = shard(a)
            arrived(self.region(s, yx_x), self.xr + a)
            part = self.region(s, yx_x, 0, self.by_y)
            remote(part, part, self.dr + a, y_dev)
            arrived(self.region(s, yx_y), self.yr + a)
            part = self.region(s, yx_y, self.by_y, self.size - self.by_y)
            remote(part, part, self.dr + a, x_dev)

        def stage2(self, a):
            s = shard(a)
            arrived(self.region(s, yx_d), self.dr + a)
            four = self.ref.at[s, :, core, pl.ds(self.first, self.size), :]
            remote(four, four, self.cr + a, c_dev)

        def stage3(self, a):
            s = shard(a)
            arrived(self.ref.at[s, :, 1 - core, pl.ds(self.first, self.size), :], self.cr + a)

    upward, downward = (dp, jnp.minimum(t + 1, 3)), (dp, jnp.maximum(t - 1, 0))
    after, before = (jnp.minimum(dp + 1, n_dp - 1), t), (jnp.maximum(dp - 1, 0), t)
    not_last, not_first = dp < n_dp - 1, dp > 0

    class Exchange:
        def __init__(self, ref, first, size):
            self.ref, self.low, self.size = ref, first, size
            self.base = alloc("recv", 6)

        def at(self, slot):
            return self.ref.at[slot, pl.ds(self.low, self.size), :]

        def go(self, src, dst, dev, pred):
            remote(self.at(src), self.at(dst), self.base + dst, dev, pred)

        def get(self, slot, pred):
            arrived(self.at(slot), self.base + slot, pred)

        def first(self):
            self.go(2, 1, upward, t < 3)
            self.go(2, 3, downward, t > 0)
            self.go(2, 5, after, jnp.logical_and(t == 3, not_last))
            self.go(2, 5, before, jnp.logical_and(t == 0, not_first))

        def neighbours(self):
            self.get(1, t >= 1)
            self.get(3, t <= 2)
            self.go(1, 0, upward, t == 2)
            self.go(3, 4, downward, t == 1)

        def chain1(self):
            self.get(5, jnp.logical_and(t == 3, not_first))
            self.get(5, jnp.logical_and(t == 0, not_last))
            self.go(5, 5, downward, jnp.logical_and(t == 3, not_first))
            self.go(5, 5, upward, jnp.logical_and(t == 0, not_last))

        def chain2(self):
            self.get(5, jnp.logical_and(t == 2, not_first))
            self.get(5, jnp.logical_and(t == 1, not_last))
            self.go(5, 0, downward, jnp.logical_and(t == 2, not_first))
            self.go(5, 4, upward, jnp.logical_and(t == 1, not_last))
            self.go(1, 0, upward, t == 1)
            self.go(3, 4, downward, t == 2)

        def ends(self):
            self.get(4, t == 0)
            self.get(0, t == 3)
            self.go(4, 0, after, jnp.logical_and(t == 0, not_last))
            self.go(0, 4, before, jnp.logical_and(t == 3, not_first))

        def chain3(self):
            self.get(0, jnp.logical_and(t == 1, not_first))
            self.get(4, jnp.logical_and(t == 2, not_last))
            self.go(0, 1, downward, jnp.logical_and(t == 1, not_first))
            self.go(4, 3, upward, jnp.logical_and(t == 2, not_last))

        def third(self):
            self.get(0, jnp.logical_and(t == 0, not_first))
            self.get(4, jnp.logical_and(t == 3, not_last))

        def last(self):
            self.get(1, jnp.logical_and(t == 0, not_first))
            self.get(3, jnp.logical_and(t == 3, not_last))
            self.get(4, t == 1)
            self.get(0, t == 2)

    lane = lax.broadcasted_iota(jnp.int32, (1, LANES), 1)
    first_half = lane < HD

    def vec(i):
        return vec_in[i : i + 1, :]

    def halves(block):
        zero = jnp.zeros_like(block)
        return jnp.where(first_half, block, zero), jnp.where(first_half, zero, block)

    def clear(ref):
        def fill(pred, slot):
            @pl.when(pred)
            def _():
                ref[slot] = jnp.zeros(ref.shape[1:], ref.dtype)

        fill(jnp.logical_and(dp == 0, t <= 1), 0)
        fill(jnp.logical_and(dp == 0, t == 0), 1)
        fill(jnp.logical_and(dp == n_dp - 1, t >= 2), 4)
        fill(jnp.logical_and(dp == n_dp - 1, t == 3), 3)

    def project(names):
        begin = blocks[names[0]][1] * rows
        place = slice(begin, begin + len(names) * rows)

        def tokens():
            parts = [xwin[blocks[name][0]] for name in names]
            return parts[0] if len(parts) == 1 else jnp.concatenate(parts, axis=0)

        uwin[place] = dot_nt(tokens(), down_in[...]).astype(BF16)

        @pl.loop(0, 4, unroll=2 if len(names) == 1 else 1)
        def _(s):
            y = dot(tokens(), wqkv[s].reshape(width, 3 * 256))
            u = uwin[place, 0:LANES]
            q = y[:, :256] + dot(u, lora_q[s]) + small[s, 16:17, :]
            qwin[place, tile(s)] = (q * (1.0 / math.sqrt(HD))).astype(BF16)
            kwin[place, tile(s)] = y[:, 256:512].astype(BF16)
            v = y[:, 512:] + dot(u, lora_v[s]) + small[s, 17:18, :]
            vwin[place, tile(s)] = v.astype(BF16)

    def loop_pairs(lo, hi, body, unroll=1):
        @pl.loop(lo, hi, unroll=unroll)
        def _(p):
            body(p, pl.ds(pl.multiple_of(p * LANES, LANES), LANES))

    def column(index):
        return jnp.sum(jnp.where(lane == index, stat[...], 0.0), axis=1, keepdims=True)

    def attend(lo, hi):
        begin, end = lo * 256, hi * 256

        def body(p, cols):
            q_heads = halves(qwin[tile(1), cols])
            k = kwin[begin:end, cols]
            v = jnp.concatenate([vwin[begin:end, cols], uwin[begin:end, LANES:]], axis=1)
            before, outs, found, inputs = attf[:, cols], [], stat[...], mixed[...]
            for i in range(2):
                s = dot_nt(q_heads[i], k) + mask[:, begin:end]
                top = jnp.max(s, axis=1, keepdims=True)
                if lo:
                    old = column(2 * p + i)
                    top = jnp.maximum(top, old)
                e = jnp.exp(s - top)
                total = jnp.sum(e, axis=1, keepdims=True)
                o = dot(e.astype(BF16), v)
                o, extra = o[:, :LANES], o[:, LANES:]
                if lo:
                    alpha = jnp.exp(old - top)
                    total = total + column(16 + 2 * p + i) * alpha
                    o = o + before * alpha
                    extra = extra + inputs * alpha
                if hi == 5:
                    o = o * (1.0 / total)
                    extra = extra * (1.0 / total)
                    top = top + jnp.log(total)
                outs.append(o)
                inputs = jnp.where(lane // 8 == 2 * p + i, extra, inputs)
                found = jnp.where(lane == 2 * p + i, top, jnp.where(lane == 16 + 2 * p + i, total, found))
            o = jnp.where(first_half, outs[0], outs[1])
            attf[:, cols] = o
            if hi == 5:
                att[:, cols] = o.astype(BF16)
            stat[...] = found
            mixed[...] = inputs

        return body

    def after_attention():
        @pl.loop(0, 4, unroll=4)
        def _(n):
            acc[:, tile(n)] = dot(att[...], wo[:, :, :, :, tile(n)].reshape(width, 256))

        z = xwin[2].astype(F32) + acc[...] + vec(0)
        centre = z - jnp.mean(z, axis=1, keepdims=True)
        r = lax.rsqrt(jnp.mean(centre * centre, axis=1, keepdims=True) + NORM_EPS)
        n1 = centre * r
        norm1[...] = n1
        stat1[...] = jnp.broadcast_to(r, stat1.shape)
        m = n1 * vec(1) + vec(2)
        midb[...] = m.astype(BF16)
        acc[...] = m + vec(3)

    def up(s):
        @pl.loop(0, 4, unroll=4)
        def _(n):
            b = dot(midb[...], wup[s, :, :, :, tile(n)].reshape(width, 256)) + small[s, pl.ds(18 + n, 1), :]
            cdf = 0.5 + 0.5 * lax.erf(b * (1.0 / math.sqrt(2.0)))
            hid[s, :, tile(n)] = (b * cdf).astype(BF16)
            gelp[s, :, tile(n)] = cdf + b * jnp.exp(-0.5 * b * b) * (1.0 / math.sqrt(2.0 * math.pi))

    def down(s):
        @pl.loop(0, 4, unroll=4)
        def _(n):
            acc[:, tile(n)] += dot(hid[s], wdn[s, :, :, :, tile(n)].reshape(width, 256))

    def second_norm():
        z = acc[...]
        centre = z - jnp.mean(z, axis=1, keepdims=True)
        r = lax.rsqrt(jnp.mean(centre * centre, axis=1, keepdims=True) + NORM_EPS)
        n2 = centre * r
        midb[...] = (n2 * vec(4) + vec(5)).astype(BF16)
        g = gffn[...].astype(F32) * vec(4)
        g = r * (g - jnp.mean(g, axis=1, keepdims=True) - n2 * jnp.mean(g * n2, axis=1, keepdims=True))
        acc[...] = g
        gffn[...] = g.astype(BF16)

    def ffn_back(s):
        @pl.loop(0, 4, unroll=4)
        def _(n):
            toward = dot_nt(gffn[...], wdn[s, n].reshape(256, width))
            gbuf[:, tile(n)] = (toward * gelp[s, :, tile(n)]).astype(BF16)

        @pl.loop(0, 4, unroll=4)
        def _(n):
            acc[:, tile(n)] += dot_nt(gbuf[...], wup[s, n].reshape(256, width))

    def first_norm_back():
        g = acc[...] * vec(1)
        n1 = norm1[...]
        g = g - jnp.mean(g, axis=1, keepdims=True) - n1 * jnp.mean(g * n1, axis=1, keepdims=True)
        g = stat1[:, 0:1] * g
        acc[...] = g
        gffn[...] = g.astype(BF16)

        @pl.loop(0, 4, unroll=4)
        def _(s):
            dowin[2, :, tile(s)] = dot_nt(gffn[...], wo[s].reshape(256, width)).astype(BF16)

    def statistics():
        product = dowin[2].astype(F32) * attf[...]
        high = product.astype(BF16)
        low = (product - high.astype(F32)).astype(BF16)
        at_row = lax.broadcasted_iota(jnp.int32, (width, LANES), 0) // HD + 16
        at_lane = lax.broadcasted_iota(jnp.int32, (width, LANES), 1)
        pick = (at_row == at_lane).astype(F32).astype(BF16)
        delta = dot(high, pick) + dot(low, pick)
        both = jnp.where(lane < 16, stat[...], delta)
        stat[...] = both
        stwin[2] = both.T[0:32]

    def pass_queries(p, cols):
        q_heads, do_heads = halves(qwin[tile(1), cols]), halves(dowin[2, :, cols])
        k, v = kwin[:, cols], vwin[:, cols]
        parts = []
        for i in range(2):
            prob = jnp.exp(dot_nt(q_heads[i], k) + mask[...] - column(2 * p + i))
            ds = prob * (dot_nt(do_heads[i], v) - column(16 + 2 * p + i))
            parts.append(dot(ds.astype(BF16), k))
        dq[:, cols] = (jnp.where(first_half, parts[0], parts[1]) * (1.0 / math.sqrt(HD))).astype(BF16)

    def pass_keys(pieces, at, end, first=False, unroll=1):
        def joined(parts, axis):
            return parts[0] if len(parts) == 1 else jnp.concatenate(parts, axis=axis)

        windows = [slice(blocks[name][1] * rows + lo, blocks[name][1] * rows + hi) for name, lo, hi in pieces]
        few = sum(hi - lo for _, lo, hi in pieces) <= 256

        def line(index):
            return joined([stwin[blocks[name][0], pl.ds(index, 1), :][:, lo:hi] for name, lo, hi in pieces], 1)

        def products(heads, right):
            if few:
                both = dot_nt(jnp.concatenate(heads, axis=0), right)
                return both[:256], both[256:]
            return [dot_nt(head, right) for head in heads]

        def body(p, cols):
            k_heads, v_heads = halves(kwin[tile(1), cols]), halves(vwin[tile(1), cols])
            q = joined([qwin[window, cols] for window in windows], 0)
            do = joined([dowin[blocks[name][0], lo:hi, cols] for name, lo, hi in pieces], 0)
            scores = products(k_heads, q)
            grads = products(v_heads, do)
            apart = joined([mask[:, window] for window in windows], 1)
            probs, ds = [], []
            for i in range(2):
                prob = jnp.exp(scores[i] + apart - line(2 * p + i))
                ds.append((prob * (grads[i] - line(16 + 2 * p + i))).astype(BF16))
                probs.append(prob.astype(BF16))
            for total, lefts, right in ((dk_acc, ds, q), (dv_acc, probs, do)):
                if few:
                    both = dot(jnp.concatenate(lefts, axis=0), right)
                    both = jnp.where(first_half, both[:256], both[256:])
                else:
                    both = jnp.where(first_half, dot(lefts[0], right), dot(lefts[1], right))
                total[:, cols] = both if first else total[:, cols] + both

        loop_pairs(at, end, body, unroll)

    def lora_partial():
        u = uwin[tile(1), 0:LANES].astype(F32).T[0:16].astype(BF16)
        of_queries = dot(u, dq[...])
        each = dot(mixed[...].T.astype(BF16), dowin[2])
        row_head = lax.broadcasted_iota(jnp.int32, each.shape, 0) // 8
        column_head = lax.broadcasted_iota(jnp.int32, each.shape, 1) // HD
        each = jnp.where(row_head == column_head, each, 0.0)
        of_values = each[0:8]
        for h in range(1, 16):
            of_values = of_values + each[8 * h : 8 * h + 8]
        both = jnp.concatenate([of_queries[0:8], of_values], axis=0)
        for s in range(4):
            lsend[s] = both[:, 256 * s : 256 * s + 256]

    def query_gradient():
        gu = jnp.zeros((rows, LANES), F32)
        for s in range(4):
            gu = gu + dot_nt(dq[:, 256 * s : 256 * s + 256], lora_q[s])
        stat1[...] = gu

        @pl.loop(0, 4, unroll=4)
        def _(n):
            total = acc[:, tile(n)]
            for s in range(4):
                weight = wqkv[s, n, :, :, 0:256].reshape(256, 256)
                total = total + dot_nt(dq[:, 256 * s : 256 * s + 256], weight)
            acc[:, tile(n)] = total

    def input_gradient():
        gu = stat1[...]
        for s in range(4):
            gu = gu + dot_nt(dkv[1, :, 256 * s : 256 * s + 256], lora_v[s])
        gu = gu.astype(BF16)
        for n in range(4):
            total = acc[:, tile(n)] + dot(gu, down_in[0:LANES, tile(n)])
            for s in range(4):
                cols = slice(256 * s, 256 * s + 256)
                two = jnp.concatenate([dkv[0, :, cols], dkv[1, :, cols]], axis=1)
                total = total + dot_nt(two, wqkv[s, n, :, :, 256:].reshape(256, 512))
            att[:, tile(n)] = total.astype(BF16)
            final.append(local(att.at[:, tile(n)], dx_ref.at[:, tile(n)]))

    def chunk(*args):
        return Chunk(*args)

    qkv0, qkv1 = chunk(wqkv, 0, 64, ld_qkv), chunk(wqkv, 64, 64, ld_qkv)
    up0, up1 = chunk(wup, 0, 64, ld_up), chunk(wup, 64, 64, ld_up)
    dn0, dn1 = chunk(wdn, 0, 64, ld_dn), chunk(wdn, 64, 64, ld_dn)
    o0 = chunk(wo, 0, 32, ld_o)
    half, quarter = rows // 2, rows // 4
    tok = [Exchange(xwin, i * quarter, quarter) for i in range(4)]
    small_base = alloc("recv", 4)
    wide = [Exchange(dowin, i * quarter, quarter) for i in range(4)]
    narrow = Exchange(stwin, 0, 32)
    lora1 = alloc("recv", 4)
    lora2 = alloc("recv", n_dp)

    def prepare():
        for ref in (xwin, dowin, stwin):
            clear(ref)
        for i in range(8):
            cols = slice(LANES * i, LANES * i + LANES)
            for j, ref in enumerate(vec_refs):
                vec_in[j : j + 1, cols] = ref[i : i + 1, :].astype(F32)
        own_small = [2.0 * qu_in[...].astype(F32), 2.0 * vu_in[...].astype(F32)]
        small[t, 0:8, :] = own_small[0]
        small[t, 8:16, :] = own_small[1]
        for i in range(2):
            cols = slice(LANES * i, LANES * i + LANES)
            small[t, 16:17, cols] = qb_in[i : i + 1, :].astype(F32)
            small[t, 17:18, cols] = vb_in[i : i + 1, :].astype(F32)
            for j in range(4):
                small[t, 18 + j : 19 + j, cols] = ub_in[2 * j + i : 2 * j + i + 1, :].astype(F32)
        small[t, 22:24, :] = jnp.zeros((2, 256), F32)
        value_map = vd_in[...].astype(F32)
        maps = [qd_in[...].astype(F32), value_map, jnp.zeros((LANES - 16, width), F32)] + [value_map] * 16
        down_in[...] = jnp.concatenate(maps, axis=0).astype(BF16)
        for d in range(1, 4):
            remote(small.at[t], small.at[t], small_base + t, (dp, lax.rem(t + d, 4)))

    pl.semaphore_wait(barrier, 3 + n_dp - 1)
    near = jnp.where(t < 3, 3, 1)
    second = jnp.where(lax.rem(t, 2) == 0, 4, 0)
    third = jnp.where(t == 0, 0, jnp.where(t == 3, 4, 1))
    final = jnp.where(t == 0, 1, jnp.where(t == 1, 4, jnp.where(t == 2, 0, 3)))
    blocks = {"n": (near, 0), "2": (2, 1), "s": (second, 2), "t": (third, 3), "l": (final, 4)}
    named = {"q0": qkv0, "q1": qkv1, "u0": up0, "u1": up1, "d0": dn0, "d1": dn1, "o": o0}
    def setup():
        lengths = len_in[...]
        docs = lengths.shape[0] * LANES
        high, low = lengths // 256, lax.rem(lengths, 256)
        upto = (
            lax.broadcasted_iota(jnp.int32, (LANES, LANES), 0)
            <= lax.broadcasted_iota(jnp.int32, (LANES, LANES), 1)
        ).astype(F32).astype(BF16)

        def summed(part):
            return dot(part.astype(F32).astype(BF16), upto)

        ends = 256.0 * summed(high) + summed(low)
        window = mask.shape[1]
        first = (dp * 4 + t) * rows - MAXLEN
        spot = lax.broadcasted_iota(jnp.int32, (1, window), 1)
        place = spot // rows
        where = place
        for slot, nth_place in blocks.values():
            where = jnp.where(place == nth_place, slot, where)
        position = first + where * rows + lax.rem(spot, rows)
        at = position.astype(F32)
        passed = jnp.zeros((1, window), F32)
        before = jnp.zeros((1, 1), F32)
        for r in range(lengths.shape[0]):
            end = ends[r : r + 1, :] + before
            before = end[:, LANES - 1 :]
            column = jnp.broadcast_to(end, (LANES, LANES)).T[:, 0:1]
            passed = passed + jnp.sum((column <= at).astype(F32), axis=0, keepdims=True)
        inside = jnp.logical_and(position >= 0, passed < docs)
        ids = jnp.where(inside, passed, -1.0)
        own = jnp.broadcast_to(ids[:, rows : 2 * rows], (LANES, rows)).T[:, 0:1]
        mask[...] = jnp.where(own == ids, 0.0, MASKED)
        stat[...] = jnp.zeros(stat.shape, F32)

    def small_ready():
        for d in range(1, 4):
            peer = lax.rem(t + d, 4)
            arrived(small.at[peer], small_base + peer)
        none = jnp.zeros((8, 256), F32)
        lora_q[:, 16:, :] = jnp.zeros((4, LANES - 16, 256), BF16)
        lora_v[:, 16:, :] = jnp.zeros((4, LANES - 16, 256), BF16)
        for s in range(4):
            lora_q[s, 0:16, :] = jnp.concatenate([small[s, 0:8, :], none], axis=0).astype(BF16)
            lora_v[s, 0:16, :] = jnp.concatenate([none, small[s, 8:16, :]], axis=0).astype(BF16)


    def part(a):
        return t if a == 0 else shard(a)

    for item in PLAN:
        kind, rest = item[0], item[1:]
        if kind == "+":
            named[rest].send()
        elif kind in "0123":
            getattr(named[rest[:-1]], "stage" + kind)(int(rest[-1]))
        elif kind in STEPS:
            done(ld_x)
            getattr(tok[int(rest)], STEPS[kind])()
        elif kind == "Z":
            prepare()
        elif item == "P0":
            setup()
            small_ready()
        elif kind == "P":
            done(ld_qkv)
            project({"n": "n2", "s": "st", "l": "l"}[rest])
        elif kind == "A":
            at, lo, hi = (int(i) for i in rest)
            loop_pairs(at, at + 4, attend(lo, hi), 2)
        elif kind == "M":
            done(ld_o)
            after_attention()
        elif kind == "U":
            done(ld_up)
            up(part(int(rest)))
        elif kind == "D":
            done(ld_dn)
            down(part(int(rest)))
    for copies in (ld_qkv, ld_o, ld_up, ld_dn):
        done(copies)

    done(ld_cot)
    second_norm()
    final = [local(midb, out_ref)]

    @pl.loop(0, 4)
    def _(s):
        ffn_back(s)

    first_norm_back()

    def swap(step, i):
        for e in [wide[i]] + ([narrow] if i == 0 else []):
            getattr(e, step)()

    for item in PLAN_BACK:
        kind, rest = item[0], item[1:]
        if item == "l3":
            settle()
        if kind in STEPS:
            swap(STEPS[kind], int(rest))
        elif kind == "T":
            statistics()
        elif kind == "Q":
            loop_pairs(int(rest), int(rest) + 2, pass_queries)
        elif kind == "K":
            if rest[0] == "x":
                lo = int(rest[1]) * half
                pass_keys([("s", lo, lo + half), ("t", lo, lo + half)], 0, pairs, unroll=2)
            elif rest[0] == "l":
                pass_keys([("l", 0, rows)], 0, pairs, unroll=2)
            else:
                at = int(rest[2])
                pass_keys([("n", 0, rows), ("2", 0, rows)], at, at + 4, first=True)
        elif kind == "G":
            lora_partial()
            for d in range(1, 4):
                peer = lax.rem(t + d, 4)
                remote(lsend.at[peer], lrecv1.at[t], lora1 + t, (dp, peer))
            lrecv1[t] = lsend[t]
        elif kind == "H":
            for d in range(1, 4):
                peer = lax.rem(t + d, 4)
                arrived(lrecv1.at[peer], lora1 + peer)
            lrecv2[dp] = 2.0 * ((lrecv1[0] + lrecv1[1]) + (lrecv1[2] + lrecv1[3]))
            for d in range(1, n_dp):
                remote(lrecv2.at[dp], lrecv2.at[dp], lora2 + dp, (lax.rem(dp + d, n_dp), t))
        elif kind == "J":
            for d in range(1, n_dp):
                peer = lax.rem(dp + d, n_dp)
                arrived(lrecv2.at[peer], lora2 + peer)
            total = lrecv2[0]
            for i in range(1, n_dp):
                total = total + lrecv2[i]
            lsend[0] = total
            final.append(local(lsend.at[0], lora_ref))
        elif kind == "i":
            query_gradient()
        elif kind == "I":
            dkv[0] = dk_acc[...].astype(BF16)
            dkv[1] = dv_acc[...].astype(BF16)
            input_gradient()
    settle()
    done(final)
    assert count["recv"] <= rsem.shape[0] and count["local"] <= lsem.shape[0]


def hand_over(out, grad, lora, out_to, grad_to, query_to, value_to, out_at, grad_at, lora_at, sems):
    rows = out.shape[0] // 4
    parts = [pl.ds(i * rows, rows) for i in range(4)]
    loads = [(lora, lora_at)]
    stores = [[(lora_at.at[0:8], query_to), (lora_at.at[8:16], value_to)]]
    for source, at, to in ((out, out_at, out_to), (grad, grad_at, grad_to)):
        for part in parts:
            loads.append((source.at[part], at.at[part]))
            stores.append([(at.at[part], to.at[part])])
    copies = [pltpu.make_async_copy(a, b, sems.at[i]) for i, (a, b) in enumerate(loads)]
    for copy in copies:
        copy.start()
    moved = []
    for copy, pairs in zip(copies, stores):
        copy.wait()
        for a, b in pairs:
            moved.append(pltpu.make_async_copy(a, b, sems.at[len(copies) + len(moved)]))
            moved[-1].start()
    for copy in moved:
        copy.wait()


def shards(
    tokens, document_lengths, query_proj_weight, query_proj_bias, key_proj_weight, value_proj_weight,
    value_proj_bias, query_adapter_down, value_adapter_down, query_adapter_up, value_adapter_up,
    attention_out_weight, attention_out_bias, attention_norm_gain, attention_norm_bias, up_proj_weight,
    up_proj_bias, down_proj_weight, down_proj_bias, feedforward_norm_gain, feedforward_norm_bias, cotangent,
):
    rows, width = tokens.shape
    n_dp = lax.axis_size("dp")
    window = rows + 2 * MAXLEN

    def fold(vector):
        return vector.reshape(vector.shape[0] // LANES, LANES)

    def cut(weight):
        return weight.reshape(4, 2, weight.shape[0] // GROUP, weight.shape[1])

    def vmem(shape, dtype):
        return pltpu.VMEM(shape, dtype)

    small_arrays = (
        fold(document_lengths), query_adapter_down.T, value_adapter_down.T, query_adapter_up, value_adapter_up,
        fold(query_proj_bias), fold(value_proj_bias), fold(up_proj_bias), fold(attention_out_bias),
        fold(attention_norm_gain), fold(attention_norm_bias), fold(down_proj_bias), fold(feedforward_norm_gain),
        fold(feedforward_norm_bias),
    )
    any_spec = pl.BlockSpec(memory_space=pl.ANY)
    vmem_spec = pl.BlockSpec(memory_space=pltpu.VMEM)
    full = (rows, width)
    rank = query_adapter_up.shape[0]
    call = pl.pallas_call(
        lambda *refs: layer_kernel(n_dp, *refs),
        out_shape=(
            jax.ShapeDtypeStruct(full, BF16),
            jax.ShapeDtypeStruct(full, BF16),
            jax.ShapeDtypeStruct((16, 256), F32),
        ),
        in_specs=[any_spec] * 8 + [vmem_spec] * 14,
        out_specs=(any_spec,) * 3,
        scratch_shapes=[
            vmem((4, 4, 2, 128, 768), BF16),
            vmem((4, 4, 2, 32, 1024), BF16),
            vmem((4, 4, 2, 128, 1024), BF16),
            vmem((4, 4, 2, 128, 1024), BF16),
            vmem((4, 24, 256), F32),
            vmem((4, 128, 256), BF16),
            vmem((4, 128, 256), BF16),
            vmem((8, width), F32),
            vmem((2 * LANES, width), BF16),
            vmem((6, rows, width), BF16),
            vmem((window, 2 * LANES), BF16),
            vmem((window, width), BF16),
            vmem((window, width), BF16),
            vmem((window, width), BF16),
            vmem((6, rows, width), BF16),
            vmem((6, 32, rows), F32),
            vmem((rows, window), F32),
            vmem((rows, LANES), F32),
            vmem(full, BF16),
            vmem(full, F32),
            vmem((rows, LANES), F32),
            vmem(full, BF16),
            vmem(full, F32),
            vmem((rows, LANES), F32),
            vmem((4, rows, width), BF16),
            vmem((4, rows, width), F32),
            vmem(full, F32),
            vmem(full, BF16),
            vmem(full, BF16),
            vmem(full, BF16),
            vmem(full, F32),
            vmem(full, F32),
            vmem((2, rows, width), BF16),
            vmem((4, 16, 256), F32),
            vmem((4, 16, 256), F32),
            vmem((n_dp, 16, 256), F32),
            pltpu.SemaphoreType.DMA((16,)),
            pltpu.SemaphoreType.DMA((32,)),
            pltpu.SemaphoreType.DMA((174 + n_dp,)),
        ],
        compiler_params=pltpu.CompilerParams(
            collective_id=0, has_side_effects=True, vmem_limit_bytes=63 * 2**20
        ),
        name="layer",
    )
    out, grad, lora = call(
        tokens, cotangent, cut(query_proj_weight), cut(key_proj_weight), cut(value_proj_weight),
        cut(attention_out_weight), cut(up_proj_weight), cut(down_proj_weight), *small_arrays,
    )
    lora_shape = jax.ShapeDtypeStruct((rank, 256), F32)
    return pl.pallas_call(
        hand_over,
        out_shape=(out, grad, lora_shape, lora_shape),
        in_specs=[any_spec] * 3,
        out_specs=(any_spec,) * 4,
        scratch_shapes=[
            vmem(full, BF16), vmem(full, BF16), vmem((2 * rank, 256), F32), pltpu.SemaphoreType.DMA((19,))
        ],
        name="hand_over",
    )(out, grad, lora)


def solution(mesh):
    whole, columns = P(), P(None, "tensor")
    stream = P(("dp", "tensor"), None)
    return jax.shard_map(
        shards,
        mesh=mesh,
        in_specs=(
            stream, whole, columns, P("tensor"), columns, columns, P("tensor"), whole, whole, columns, columns,
            P("tensor", None), whole, whole, whole, columns, P("tensor"), P("tensor", None), whole, whole, whole,
            stream,
        ),
        out_specs=(stream, stream, columns, columns),
        check_vma=False,
    )
```
